32 devices in a mesh: dp: 4 (over y, core), fsdp: 8 (over z, x).
Axes of the slice: x: 2, y: 2, z: 4, core: 2. Of those that a mesh axis runs over, the one named last changes fastest.
Arguments:
- frames: bfloat16 [32, 256, 1024], P(('dp', 'fsdp')), may hold values from -6 to 6
- lengths: int32 [32], P(('dp', 'fsdp')), may hold values from 64 to 256
- cotangent: bfloat16 [32, 256, 1024], P(('dp', 'fsdp')), may hold values from -6 to 6
- panels: bfloat16 [23, 1024, 1024], P(None, 'fsdp')
- vectors: float32 [34, 1024], replicated
- vector_first: float32 [34, 1024], replicated, may hold values from -72.40774 to 72.40774
- vector_second: float32 [34, 1024], replicated, may hold values from 81.92 to 1228.8
- owners: int32 [23], replicated, may hold values from 0 to 7, as said below
- basis_left: float32 [24, 1024, 1024], P('fsdp'), may hold values from -0.1875 to 0.1875
- basis_right: float32 [24, 1024, 1024], P('fsdp'), may hold values from -0.1875 to 0.1875
- panel_first: float32 [1024, 24, 1024], P('dp', 'fsdp'), may hold values from -72.40774 to 72.40774
- panel_second: float32 [1024, 24, 1024], P('dp', 'fsdp'), may hold values from 81.92 to 1228.8
- panel_master: float32 [1024, 24, 1024], P('dp', 'fsdp'), may hold values from -0.1875 to 0.1875
Outputs:
- layer_out: bfloat16 [32, 256, 1024], P(('dp', 'fsdp'))
- frames_grad: bfloat16 [32, 256, 1024], P(('dp', 'fsdp'))
- panel_grads: float32 [23, 1024, 1024], P(None, 'fsdp', 'dp')
- vector_grads: float32 [34, 1024], replicated
- vector_first_new: float32 [34, 1024], replicated
- vector_second_new: float32 [34, 1024], replicated
- vectors_new: float32 [34, 1024], replicated
- panel_first_new: float32 [1024, 24, 1024], P('dp', 'fsdp')
- panel_second_new: float32 [1024, 24, 1024], P('dp', 'fsdp')
- panel_master_new: float32 [1024, 24, 1024], P('dp', 'fsdp')
The draws below stay inside these ranges and needn't reach their ends.
Inputs may be any that keep to these rules, and one draw needn't show every extreme that they name: `owners`: every index along fsdp owns at most 3 panels, and some own exactly 3.
All inputs are finite; a program needn't handle non-finite values.
Results may differ from the reference program's by a relative error of at most 0.023.
Values may be sent and summed in bfloat16 or wider, within the bound.
No kernel may reach another device: no remote copies, remote signals or barrier semaphores. Data moves between devices by JAX's collectives and lax.ppermute only.
A program may use at most 384 MiB of HBM per device.

```python
import math
import jax
import jax.numpy as jnp
from jax import lax

D = 1024
HEADS = 8
KERNEL = 5
PANELS = 23
VROWS = 34
STEPS = 4
BUCKET = 256
SEQS = 32
TOKENS = 8192
SLOTS = 3
SLOTS_ALL = 24
N_FSDP = 8


def draw_lengths(key, part):
    first_key, second_key = jax.random.split(key)
    values = jax.random.randint(first_key, (SEQS,), BUCKET // 4, BUCKET + 1)
    chosen = jax.random.randint(second_key, (), 0, SEQS)
    return jnp.where(jnp.arange(SEQS) == chosen, BUCKET, values).astype(jnp.int32)


def draw_owners(key, part):
    order = jax.random.permutation(key, SLOTS_ALL)
    return (order[:PANELS] // SLOTS).astype(jnp.int32)


def draw_panels(key, part):
    factors = jnp.array([1.0, 1.0, 1.0, 1.0, 1.0, 1.0, 1.0, 1.0, 1.2, 1.2, 1.0, 3.0, 1.0, 1.0, 1.5, 1.0, 1.0, 1.0, 1.0, 1.0, 1.0, 1.0, 1.0], jnp.float32)
    values = jnp.clip(jax.random.normal(key, (PANELS, D, D), jnp.float32), -6.0, 6.0)
    return (values * factors[:, None, None] * D ** (-0.5)).astype(jnp.bfloat16)


def draw_vectors(key, part):
    gain_key, shift_key, tap_key = jax.random.split(key, 3)
    gains = jax.random.uniform(gain_key, (VROWS, D), jnp.float32, 0.7, 1.3)
    shifts = 0.2 * jnp.clip(jax.random.normal(shift_key, (VROWS, D), jnp.float32), -5.0, 5.0)
    taps = 0.45 * jnp.clip(jax.random.normal(tap_key, (VROWS, D), jnp.float32), -5.0, 5.0)
    row_ids = jnp.arange(VROWS)[:, None]
    is_gain = (row_ids < 12) & (row_ids % 2 == 0)
    is_tap = (row_ids >= 28) & (row_ids < 33)
    return jnp.where(is_gain, gains, jnp.where(is_tap, taps, shifts)).astype(jnp.float32)


def steps_of(rng, dims, shards, smallest, top_value):
    loudness, own = 1.0, jax.random.fold_in(rng, 6)
    for dim, blocks in shards:
        draws = jnp.exp(jax.random.uniform(jax.random.fold_in(own, dim), (blocks,), jnp.float32, smallest / len(shards), top_value / len(shards)))
        loudness = loudness * jnp.repeat(draws, dims[dim] // blocks).reshape([-1 if axis == dim else 1 for axis in range(len(dims))])
    return loudness


def gaussian(key, extent, spread, limit, cuts=(), kind=jnp.bfloat16):
    gain = steps_of(key, extent, cuts, -0.22, 0.18) if cuts else 1.0
    values = jax.random.normal(key, extent, jnp.float32) * spread * gain
    return jnp.minimum(jnp.maximum(values, -limit), limit).astype(kind)


def setup_inputs(seed: int = 0) -> dict:
    splits = jax.random.split(jax.random.key(seed), 14)
    frames = gaussian(splits[0], (SEQS, BUCKET, D), 1.0, 6.0, ((0, 32),))
    lengths = draw_lengths(jax.random.fold_in(splits[13], 71), 0)
    cotangent = gaussian(splits[2], (SEQS, BUCKET, D), 1.0, 6.0, ((0, 32),))
    panels = draw_panels(jax.random.fold_in(splits[13], 71), 0)
    vectors = draw_vectors(jax.random.fold_in(splits[13], 71), 0)
    vector_first = gaussian(splits[5], (VROWS, D), (0.2 * TOKENS ** 0.5), 72.40774, (), jnp.float32)
    vector_second = jnp.clip(jnp.exp(jax.random.uniform(splits[6], (VROWS, D), jnp.float32, math.log(81.92), math.log(1228.8))), 81.92, 1228.8)
    owners = draw_owners(jax.random.fold_in(splits[13], 71), 0)
    basis_left = gaussian(splits[8], (SLOTS_ALL, D, D), D ** -0.5, 0.1875, ((0, 8),), jnp.float32)
    basis_right = gaussian(splits[9], (SLOTS_ALL, D, D), D ** -0.5, 0.1875, ((0, 8),), jnp.float32)
    panel_first = gaussian(splits[10], (D, SLOTS_ALL, D), (0.2 * TOKENS ** 0.5), 72.40774, ((0, 4), (1, 8)), jnp.float32)
    panel_second = jnp.clip(jnp.exp(math.log(1228.8) - 2.7080503 * jax.random.uniform(splits[11], (D, SLOTS_ALL, D), jnp.float32) ** steps_of(splits[11], (D, SLOTS_ALL, D), ((0, 4), (1, 8)), -0.2, 0.2)), 81.92, 1228.8)
    panel_master = gaussian(splits[12], (D, SLOTS_ALL, D), D ** -0.5, 0.1875, ((0, 4), (1, 8)), jnp.float32)
    return {"frames": frames, "lengths": lengths, "cotangent": cotangent, "panels": panels, "vectors": vectors, "vector_first": vector_first, "vector_second": vector_second, "owners": owners, "basis_left": basis_left, "basis_right": basis_right, "panel_first": panel_first, "panel_second": panel_second, "panel_master": panel_master}


norm_eps = 1e-05
adam_eps = 1e-08
beta_one = 0.5
beta_two = 0.5
learn_rate = 0.02
vector_rate = 0.25
highest = lax.Precision.HIGHEST

@jax.custom_vjp
def low(v):
    return lax.optimization_barrier(v.astype(jnp.bfloat16)).astype(jnp.float32)

@jax.custom_vjp
def low_back(v):
    return v

def low_keep(v):
    return (low(v), None)

def low_pass(kept, grad):
    return (grad,)

def back_keep(v):
    return (v, None)

def back_low(kept, grad):
    return (low(grad),)
low.defvjp(low_keep, low_pass)
low_back.defvjp(back_keep, back_low)

def layer_norm(values, gain_row, shift_row):
    centred = values - lax.optimization_barrier(jnp.mean(values, axis=-1, keepdims=True))
    inverse = lax.rsqrt(lax.optimization_barrier(jnp.mean(centred * centred, axis=-1, keepdims=True)) + norm_eps)
    return centred * inverse * gain_row + shift_row

def conv_piece(wide, kernel, conv_bias, gain_row, shift_row, frame_mask):
    gated = wide[:, :, 0] * jax.nn.sigmoid(wide[:, :, 1])
    gated = gated * frame_mask[:, :, None]
    seq_len = gated.shape[1]
    margin = KERNEL // 2
    padded = jnp.pad(gated, ((0, 0), (margin, margin), (0, 0)))
    depthwise = conv_bias + kernel[0] * padded[:, 0:seq_len]
    for tap_index in range(1, KERNEL):
        depthwise = depthwise + kernel[tap_index] * padded[:, tap_index:tap_index + seq_len]
    return jax.nn.silu(layer_norm(depthwise, gain_row, shift_row))

def ffn_block(residual, weights, gain_row, shift_row, bias_in, bias_out):
    normed = low(layer_norm(residual, gain_row, shift_row))
    hidden = low_back(jnp.einsum('bld,pdc->blpc', normed, weights[0:4], precision=highest) + bias_in)
    active = low(jax.nn.silu(hidden))
    branch = low_back(jnp.einsum('blpc,pcd->bld', active, weights[4:8], precision=highest) + bias_out)
    return residual + 0.5 * branch

def attention_block(residual, weights, vectors, frame_mask):
    seq_count, seq_len, model_width = residual.shape
    normed = low(layer_norm(residual, vectors[2], vectors[3]))
    biases = jnp.stack([vectors[22], jnp.zeros_like(vectors[22]), vectors[23]])
    projected = low(low_back(jnp.einsum('bld,pdc->blpc', normed, weights[0:3], precision=highest) + biases))
    heads = projected.reshape(seq_count, seq_len, 3, HEADS, model_width // HEADS)
    queries, key_heads, value_heads = (heads[:, :, 0], heads[:, :, 1], heads[:, :, 2])
    score_scale = (model_width // HEADS) ** (-0.5)
    scores = low_back(jnp.einsum('blhe,bmhe->bhlm', queries, key_heads, precision=highest) * score_scale)
    scores = jnp.where(frame_mask[:, None, None, :] > 0, scores, -1000000000.0)
    soft_low = low(jax.nn.softmax(scores, axis=-1))
    mixed = jnp.einsum('bhlm,bmhe->blhe', soft_low, value_heads, precision=highest)
    mixed = low(low_back(mixed.reshape(seq_count, seq_len, model_width)))
    branch = low_back(jnp.einsum('bld,dc->blc', mixed, weights[3], precision=highest) + vectors[24])
    return residual + branch

def conv_block(residual, weights, vectors, frame_mask):
    normed = low(layer_norm(residual, vectors[4], vectors[5]))
    wide = low_back(jnp.einsum('bld,pdc->blpc', normed, weights[0:2], precision=highest) + vectors[25:27])
    active = low(conv_piece(wide, vectors[28:33], vectors[27], vectors[6], vectors[7], frame_mask))
    branch = low_back(jnp.einsum('bld,dc->blc', active, weights[2], precision=highest) + vectors[33])
    return residual + branch

def conformer(frames, frame_mask, weights, vectors):
    residual = ffn_block(frames, weights[0:8], vectors[0], vectors[1], vectors[12:16], vectors[16])
    residual = attention_block(residual, weights[8:12], vectors, frame_mask)
    residual = conv_block(residual, weights[12:15], vectors, frame_mask)
    residual = ffn_block(residual, weights[15:23], vectors[8], vectors[9], vectors[17:21], vectors[21])
    return layer_norm(residual, vectors[10], vectors[11])

def adam_step(first_new, second_new):
    return first_new / (1.0 - beta_one ** STEPS) / (jnp.sqrt(second_new / (1.0 - beta_two ** STEPS)) + adam_eps)

def reference(frames, lengths, cotangent, panels, vectors, vector_first, vector_second, owners, basis_left, basis_right, panel_first, panel_second, panel_master):
    group_size = math.gcd(SEQS, 16)
    group_count = SEQS // group_size
    positions = lax.broadcasted_iota(jnp.int32, (SEQS, BUCKET), 1)
    frame_mask = (positions < lengths[:, None].astype(jnp.int32)).astype(jnp.float32)
    weights = panels.astype(jnp.float32)
    group_data = (frames.reshape(group_count, group_size, BUCKET, D), cotangent.reshape(group_count, group_size, BUCKET, D), frame_mask.reshape(group_count, group_size, BUCKET))

    def run_group(totals, pieces):
        frame_part, cot_part, mask_part = pieces

        def forward(frame_values, weight_values, vector_values):
            return conformer(frame_values, mask_part, weight_values, vector_values)
        output, pull_back = jax.vjp(forward, frame_part.astype(jnp.float32), weights, vectors)
        frame_grad, weight_grad, vector_grad = pull_back(cot_part.astype(jnp.float32) * mask_part[:, :, None])
        return ((totals[0] + weight_grad, totals[1] + vector_grad), (output.astype(jnp.bfloat16), frame_grad.astype(jnp.bfloat16)))
    initial = (jnp.zeros((PANELS, D, D), jnp.float32), jnp.zeros((VROWS, D), jnp.float32))
    (panel_grads, vector_grads), (outputs, frame_grads) = lax.scan(run_group, initial, group_data)
    layer_out = outputs.reshape(SEQS, BUCKET, D)
    frames_grad = frame_grads.reshape(SEQS, BUCKET, D)
    vector_first_new = beta_one * vector_first + (1.0 - beta_one) * vector_grads
    vector_second_new = beta_two * vector_second + (1.0 - beta_two) * vector_grads * vector_grads
    vectors_new = vectors - vector_rate * adam_step(vector_first_new, vector_second_new)
    slots_all = SLOTS * N_FSDP
    panel_index = jnp.arange(PANELS, dtype=jnp.int32)
    owner_ids = owners.astype(jnp.int32)
    same_owner = owner_ids[:, None] == owner_ids[None, :]
    earlier = panel_index[None, :] < panel_index[:, None]
    slot_of = lax.optimization_barrier(jnp.sum((same_owner & earlier).astype(jnp.int32), axis=1)).astype(jnp.int32)
    target = (owner_ids * SLOTS + slot_of).astype(jnp.int32)
    slot_hit = target[:, None] == jnp.arange(slots_all, dtype=jnp.int32)[None, :]
    source = lax.optimization_barrier(jnp.sum(slot_hit.astype(jnp.int32) * panel_index[:, None], axis=0)).astype(jnp.int32)
    filled = jnp.any(slot_hit, axis=0)
    gathered = jnp.where(filled[:, None, None], panel_grads[source], 0.0)
    turned = jnp.einsum('trk,trc->tkc', basis_left, gathered, precision=highest)
    rotated = jnp.einsum('tkc,tcx->tkx', turned, basis_right, precision=highest)
    first_old = jnp.transpose(panel_first, (1, 0, 2))
    second_old = jnp.transpose(panel_second, (1, 0, 2))
    master_old = jnp.transpose(panel_master, (1, 0, 2))
    first_new = beta_one * first_old + (1.0 - beta_one) * rotated
    second_new = beta_two * second_old + (1.0 - beta_two) * rotated * rotated
    step_values = adam_step(first_new, second_new)
    back_turn = jnp.einsum('tkc,txc->tkx', step_values, basis_right, precision=highest)
    update = jnp.einsum('tak,tkx->tax', basis_left, back_turn, precision=highest)
    keep_slot = filled[:, None, None]
    master_new = jnp.where(keep_slot, master_old - learn_rate * update, 0.0)
    first_new = jnp.where(keep_slot, first_new, 0.0)
    second_new = jnp.where(keep_slot, second_new, 0.0)
    return (layer_out, frames_grad, panel_grads, vector_grads, vector_first_new, vector_second_new, vectors_new, jnp.transpose(first_new, (1, 0, 2)), jnp.transpose(second_new, (1, 0, 2)), jnp.transpose(master_new, (1, 0, 2)))
```

```python
import functools

import jax
import jax.numpy as jnp
from jax import lax
from jax.experimental import pallas as pl
from jax.experimental.pallas import tpu as pltpu
from jax.sharding import Mesh
from jax.sharding import PartitionSpec as P

HEADS = 8
KERNEL = 5
STEPS = 4


norm_eps = 1e-05
adam_eps = 1e-08
beta_one = 0.5
beta_two = 0.5
learn_rate = 0.02
vector_rate = 0.25

bf16 = jnp.bfloat16
f32 = jnp.float32
ANY = pl.ANY
VMEM = pltpu.VMEM
SMEM = pltpu.SMEM
SWAP = [(0, 1), (1, 0)]
TILE = 256
tie = lax.optimization_barrier
VMEM_LIMIT = 56 * 1024 * 1024


def layer_norm(values, gain_row, shift_row):
    centred = values - jnp.mean(values, axis=-1, keepdims=True)
    inverse = lax.rsqrt(jnp.mean(centred * centred, axis=-1, keepdims=True) + norm_eps)
    return centred * inverse * gain_row + shift_row


def norm_backward(residual, gain_row, shift_row, normed_grad):
    ignored, pull_back = jax.vjp(layer_norm, residual, gain_row, shift_row)
    return pull_back(normed_grad)


def adam_step(first_new, second_new):
    return (
        first_new
        / (1.0 - beta_one**STEPS)
        / (jnp.sqrt(second_new / (1.0 - beta_two**STEPS)) + adam_eps)
    )


def token_sum(values):
    return jnp.sum(values, axis=0, dtype=f32)


def dot(left, right):
    return lax.dot_general(left, right, (((1,), (0,)), ((), ())), preferred_element_type=f32)


def dot_nt(left, right):
    return lax.dot_general(left, right, (((1,), (1,)), ((), ())), preferred_element_type=f32)


def dot_tn(left, right):
    return lax.dot_general(left, right, (((0,), (0,)), ((), ())), preferred_element_type=f32)


class Cell:
    def __init__(self, value):
        self.value = value


def bind(*cells):
    for cell, value in zip(cells, tie(tuple(cell.value for cell in cells))):
        cell.value = value


class Wires:
    def __init__(self, outer, owners_count):
        self.outer, self.count = outer, owners_count
        walk = list(range(0, owners_count, 2)) + list(range(owners_count - 1, 0, -2))
        onward = [(walk[i], walk[(i + 1) % owners_count]) for i in range(owners_count)]
        self.routes = {
            "onward": ("f", onward),
            "back": ("f", [(b, a) for a, b in onward]),
            "chip": ("o", [(i, i ^ 1) for i in range(outer)]),
            "core": ("c", SWAP),
        }
        for name, count in (("o", outer), ("f", owners_count)):
            step = 1
            while step < count:
                self.routes[f"{name}{step}"] = (name, [(i, i ^ step) for i in range(count)])
                step *= 2
        index = lax.axis_index("f")
        self.place = jnp.where(index % 2 == 0, index // 2, owners_count - 1 - index // 2)
        self.past = []

    def start(self, *groups, after=()):
        sends = [send for group in groups for send in group]
        came = []
        for value, route, take in sends:
            if after:
                value = tie((value, *[cell.value for cell in after]))[0]
            axis, pairs = self.routes[route]
            came.append(Cell(lax.ppermute(value, axis, pairs)))
            take(came[-1])
        return came

    def slot(self, *groups):
        came = self.start(*groups, after=self.past[-2] if len(self.past) >= 2 else ())
        if came:
            self.past.append(came)
        return came

    def index_at(self, steps):
        spot = (self.place + steps + self.count) % self.count
        return jnp.where(spot < self.count // 2, 2 * spot, 2 * (self.count - 1 - spot) + 1)

    def reach(self, turn):
        half = self.count // 2
        return (half, half - 1) if turn == 0 else (half - 1, half)


class Gather:
    def __init__(self, wires, unit, turn):
        self.wires = wires
        self.left = list(wires.reach(turn))
        self.pieces = [Cell(unit)]
        self.origin = [wires.index_at(0)]
        self.moving = [self.pieces[0], self.pieces[0]]
        self.hops = 0

    def hop(self):
        self.hops += 1
        sends = []
        for way, (route, sign) in enumerate((("onward", -1), ("back", 1))):
            if self.left[way]:
                self.left[way] -= 1
                self.origin.append(self.wires.index_at(sign * self.hops))

                def take(cell, way=way):
                    self.moving[way] = cell
                    self.pieces.append(cell)

                sends.append((self.moving[way].value, route, take))
        return sends

    def spots(self):
        return jnp.stack(self.origin).astype(jnp.int32)


class Reduce:
    def __init__(self, wires, part_of, turn):
        self.wires, self.part_of = wires, part_of
        self.left = list(wires.reach(turn))
        self.moving = [None, None]

    def hop(self):
        sends = []
        for way, (route, sign) in enumerate((("onward", 1), ("back", -1))):
            if self.left[way]:
                value = self.part_of(self.wires.index_at(sign * self.left[way]))
                if self.moving[way] is not None:
                    value = value.astype(f32) + self.moving[way].value.astype(f32)

                def take(cell, way=way):
                    self.moving[way] = cell

                sends.append((value.astype(bf16), route, take))
                self.left[way] -= 1
        return sends

    def total(self):
        while any(self.left):
            self.wires.slot(self.hop())
        own = self.part_of(self.wires.index_at(0)).astype(f32)
        return own + self.moving[0].value.astype(f32) + self.moving[1].value.astype(f32)


class AllSum:
    def __init__(self, wires, value):
        self.wires, self.value = wires, Cell(value)
        self.todo = ["core"] + [name for name in wires.routes if name[1:].isdigit()]
        self.came = None

    def hop(self):
        if not self.todo:
            return []
        self.settle()
        return [(self.value.value, self.todo.pop(0), self.take)]

    def take(self, cell):
        self.came = cell

    def settle(self):
        if self.came is not None:
            self.value = Cell(self.value.value + self.came.value)
            self.came = None

    def total(self):
        while self.todo:
            self.wires.slot(self.hop())
        self.settle()
        return self.value.value


class ChipSum:
    def __init__(self, wires, blocks=None, here=None, there=None):
        self.wires, self.blocks = wires, blocks
        if blocks is not None and wires.outer == 2:
            index = lax.axis_index("o")
            here = lax.dynamic_index_in_dim(blocks, index, 0, keepdims=False)
            there = [lax.dynamic_index_in_dim(blocks, 1 - index, 0, keepdims=False)]
        self.here, self.there, self.came = here, list(there or []), []

    def send(self):
        if not self.there:
            return []
        return [(self.there.pop(0).astype(bf16), "chip", self.came.append)]

    def total(self):
        if self.here is None:
            low = self.blocks.astype(bf16)
            low = lax.psum_scatter(low, "o", scatter_dimension=0, tiled=True)
            return low[0].astype(f32)
        while self.there:
            self.wires.slot(self.send())
        came = [cell.value for cell in self.came]
        came = came[0] if len(came) == 1 else jnp.stack(came)
        return self.here.astype(f32) + came.astype(f32)


def swap_cores(values):
    return lax.ppermute(values, "c", SWAP)


def row_parts(depth, *matrices):
    def part_of(index):
        parts = [lax.dynamic_slice_in_dim(m, index * depth, depth, m.ndim - 2) for m in matrices]
        return jnp.concatenate(parts, axis=-3) if len(parts) > 1 else parts[0]

    return part_of


def gather_blocks(values, name, count):
    if count == 2:
        index = lax.axis_index(name)
        other = lax.ppermute(values, name, SWAP)
        first = jnp.where(index == 0, values, other)
        second = jnp.where(index == 0, other, values)
        return jnp.stack([first, second])
    return lax.all_gather(values, name)


def trade_blocks(values, name, count):
    if count == 2:
        index = lax.axis_index(name)
        there = lax.dynamic_index_in_dim(values, 1 - index, 0, keepdims=False)
        here = lax.dynamic_index_in_dim(values, index, 0, keepdims=False)
        came = lax.ppermute(there, name, SWAP)
        return jnp.stack([jnp.where(index == 0, here, came), jnp.where(index == 0, came, here)])
    return lax.all_to_all(values, name, split_axis=0, concat_axis=0, tiled=True)


def pick_kernel(slots, source, grads, out, sems):
    copies = [
        pltpu.make_async_copy(grads.at[source[i]], out.at[i], sems.at[i]) for i in range(slots)
    ]
    for copy in copies:
        copy.start()
    for copy in copies:
        copy.wait()


def pick(grads, source):
    slots = source.shape[0]
    return pl.pallas_call(
        functools.partial(pick_kernel, slots),
        out_shape=jax.ShapeDtypeStruct((slots,) + grads.shape[1:], grads.dtype),
        in_specs=[pl.BlockSpec(memory_space=SMEM), pl.BlockSpec(memory_space=ANY)],
        out_specs=pl.BlockSpec(memory_space=VMEM),
        scratch_shapes=[pltpu.SemaphoreType.DMA((slots,))],
        name="pick",
    )(source, grads)


def load_share(mine, other, spots, depth, first, weights, sems):
    copies = []
    for i in range(len(mine)):
        row = pl.multiple_of(spots[i] * depth, depth)
        for side, pieces in enumerate((mine, other)):
            copies.append(
                pltpu.make_async_copy(
                    pieces[i].at[first],
                    weights.at[2 * first + side, pl.ds(row, depth)],
                    sems.at[first, side, i],
                )
            )
    return copies


def ffn_forward_kernel(count, meta, normed, bias, *refs):
    mine, other = refs[:count], refs[count : 2 * count]
    hidden, active, branch, away, weights, sems = refs[2 * count :]
    depth, width = mine[0].shape[1:]
    tokens = branch.shape[0]
    ins = load_share(mine, other, meta, depth, 0, weights, sems)
    outs = load_share(mine, other, meta, depth, 1, weights, sems)
    start_all(ins + outs)
    wait_all(ins)
    for p in range(2):

        @column_loop(width)
        def columns(cols):
            value = dot(normed[...], weights[p, :, cols]) + bias[p, :, cols]
            hidden[p, :, cols] = value
            active[p, :, cols] = (value * jax.nn.sigmoid(value)).astype(bf16)

    wait_all(outs)

    @column_loop(width)
    def out_columns(cols):
        total = dot(active[0], weights[2, :, cols]) + dot(active[1], weights[3, :, cols])
        branch[:, cols] = total[:tokens]
        away[:, cols] = total[tokens:].astype(bf16)


def ffn_forward_call(normed, bias, mine, other, meta):
    tokens, width = normed.shape
    count = len(mine)
    return pl.pallas_call(
        functools.partial(ffn_forward_kernel, count),
        out_shape=[
            jax.ShapeDtypeStruct((2, tokens, width), f32),
            jax.ShapeDtypeStruct((2, tokens, width), bf16),
            jax.ShapeDtypeStruct((tokens // 2, width), f32),
            jax.ShapeDtypeStruct((tokens // 2, width), bf16),
        ],
        in_specs=[
            pl.BlockSpec(memory_space=SMEM),
            pl.BlockSpec(memory_space=VMEM),
            pl.BlockSpec(memory_space=VMEM),
        ]
        + [pl.BlockSpec(memory_space=ANY)] * (2 * count),
        out_specs=[pl.BlockSpec(memory_space=VMEM)] * 4,
        scratch_shapes=[
            VMEM((4, width, width), bf16),
            pltpu.SemaphoreType.DMA((2, 2, count)),
        ],
        compiler_params=pltpu.CompilerParams(vmem_limit_bytes=VMEM_LIMIT),
        cost_estimate=pl.CostEstimate(
            flops=8 * tokens * width * width,
            bytes_accessed=8 * width * width + tokens * width * 18,
            transcendentals=2 * tokens * width,
        ),
        name="ffn_forward",
    )(meta, normed, bias, *mine, *other)


def ffn_out_backward_kernel(count, bias, blocks, meta, hidden, active, grad, had, *refs):
    mine, other = refs[:count], refs[count : 2 * count]
    low, sums, *matrices, weights, sems = refs[2 * count :]
    depth, width = mine[0].shape[1:]
    outer, ways = blocks
    parity, core = meta[count], meta[count + 1]
    store = share_store(ways, meta[count + 2], matrices)
    sums[...] = had[...]
    copies = load_share(mine, other, meta, depth, 1, weights, sems)
    start_all(copies)
    for p in range(2):
        put_blocks(store, p ^ parity, active.at[p], grad, outer)
    wait_all(copies)
    for p in range(2):
        row = bias + 2 * core + (p ^ parity)

        @column_loop(width)
        def rows(cols):
            value = hidden[p, :, cols]
            share = jax.nn.sigmoid(value)
            slope = share * (1.0 + value * (1.0 - share))
            part = (dot_nt(grad[...], weights[2 + p, cols, :]) * slope).astype(bf16)
            low[p, :, cols] = part
            sums[pl.ds(row, 1), cols] = jnp.sum(part.astype(f32), axis=0, keepdims=True)


def ffn_in_backward_kernel(count, bias, blocks, meta, normed, low, *refs):
    mine, other = refs[:count], refs[count : 2 * count]
    normed_grad, away, *matrices, weights, sems = refs[2 * count :]
    tokens = away.shape[0]
    depth, width = mine[0].shape[1:]
    outer, ways = blocks
    parity = meta[count]
    store = share_store(ways, meta[count + 2], matrices)
    copies = load_share(mine, other, meta, depth, 0, weights, sems)
    start_all(copies)
    for p in range(2):
        put_blocks(store, p ^ parity, normed, low.at[p], outer)
    wait_all(copies)

    @column_loop(width)
    def back(cols):
        total = dot_nt(low[0], weights[0, cols, :]) + dot_nt(low[1], weights[1, cols, :])
        normed_grad[:, cols] = total[:tokens]
        away[:, cols] = total[tokens:].astype(bf16)


def share_store(ways, chip, matrices):
    if ways:
        return store_by_chip(chip, matrices[0], matrices[1:])
    return store_all(matrices[0])


def ffn_backward_call(kernel, name, bias, outer, ways, meta, arrays, mine, other, outs):
    width = mine[0].shape[-1]
    tokens = arrays[0].shape[-2]
    count = len(mine)
    quarter = width // (2 * outer)
    if ways:
        part = jax.ShapeDtypeStruct((2, width, quarter), bf16)
        blocks = [jax.ShapeDtypeStruct((2, 2, width, quarter), bf16), part, part]
    else:
        blocks = [jax.ShapeDtypeStruct((outer, 2, 2, width, quarter), bf16)]
    return pl.pallas_call(
        functools.partial(kernel, count, bias, (outer, ways)),
        out_shape=[*outs, *blocks],
        in_specs=[pl.BlockSpec(memory_space=SMEM)]
        + [pl.BlockSpec(memory_space=VMEM)] * len(arrays)
        + [pl.BlockSpec(memory_space=ANY)] * (2 * count),
        out_specs=[pl.BlockSpec(memory_space=VMEM)] * (len(outs) + len(blocks)),
        scratch_shapes=[
            VMEM((4, width, width), bf16),
            pltpu.SemaphoreType.DMA((2, 2, count)),
        ],
        compiler_params=pltpu.CompilerParams(vmem_limit_bytes=VMEM_LIMIT),
        cost_estimate=pl.CostEstimate(
            flops=8 * tokens * width * width,
            bytes_accessed=8 * width * width + tokens * width * 16,
            transcendentals=tokens * width,
        ),
        name=name,
    )(meta, *arrays, *mine, *other)


def norm_parts(values):
    centred = values - jnp.mean(values, axis=-1, keepdims=True)
    inverse = lax.rsqrt(jnp.mean(centred * centred, axis=-1, keepdims=True) + norm_eps)
    return centred * inverse, inverse


def norm_pull(normed, inverse, gain_row, grad):
    scaled = grad * gain_row
    along = jnp.mean(scaled * normed, axis=-1, keepdims=True)
    return inverse * (scaled - jnp.mean(scaled, axis=-1, keepdims=True) - normed * along)


def column_sum(values):
    return jnp.sum(values, axis=0, keepdims=True)


def halves_to_panels(first, last, own, other, spots, core, weights, sems):
    depth, half = own[0].shape[1:]
    copies = []
    for i in range(len(own)):
        row = pl.multiple_of(spots[i] * depth, depth)
        for side, pieces in ((core, own), (1 - core, other)):
            col = pl.multiple_of(side * half, half)
            copies.append(
                pltpu.make_async_copy(
                    pieces[i].at[pl.ds(first, last - first)],
                    weights.at[pl.ds(0, last - first), pl.ds(row, depth), pl.ds(col, half)],
                    sems.at[len(copies)],
                )
            )
    return copies


def start_all(copies):
    for copy in copies:
        copy.start()


def wait_all(copies):
    for copy in copies:
        copy.wait()


def column_loop(width):
    def run(body):
        @pl.loop(0, width // TILE)
        def step(j):
            body(pl.ds(pl.multiple_of(j * TILE, TILE), TILE))

    return run


def put_blocks(store, panel, left, right, outer):
    quarter = right.shape[-1] // (2 * outer)

    @column_loop(left.shape[1])
    def rows(part):
        value = dot_tn(left[:, part], right[...]).astype(bf16)
        for o in range(outer):
            for c in range(2):
                at = (2 * o + c) * quarter
                store(o, c, panel, part, value[:, at : at + quarter])


def store_all(blocks):
    def store(o, c, panel, part, value):
        blocks[o, c, panel, part, :] = value

    return store


def store_by_core(core, here, there):
    def store(o, c, panel, part, value):
        @pl.when(c == core)
        def kept():
            here[o, panel, part, :] = value

        @pl.when(c != core)
        def sent():
            there[o, panel, part, :] = value

    return store


def store_by_chip(chip, here, there):
    def store(o, c, panel, part, value):
        @pl.when(o == chip)
        def kept():
            here[c, panel, part, :] = value

        @pl.when(o != chip)
        def sent():
            there[c][panel, part, :] = value

    return store


def attend(queries, keys, head, size, length, score_scale):
    cols = slice(head * size, (head + 1) * size)
    scores = dot_nt(queries[:, cols], keys[:, cols]) * score_scale
    spot = lax.broadcasted_iota(jnp.int32, scores.shape, 1)
    scores = jnp.where(spot < length, scores, -1000000000.0)
    peak = jnp.max(scores, axis=-1, keepdims=True)
    raised = jnp.exp(scores - peak)
    return raised * (1.0 / jnp.sum(raised, axis=-1, keepdims=True)), cols


def attention_forward_kernel(count, meta, stream, rows, *refs):
    own, other = refs[:count], refs[count : 2 * count]
    out, normed, queries, keys, values, mixed, weights, sems = refs[2 * count :]
    core, length = meta[count], meta[count + 1]
    width = stream.shape[1]
    size = width // HEADS
    copies = halves_to_panels(0, 4, own, other, meta, core, weights, sems)
    start_all(copies)
    inside, ignored = norm_parts(stream[...])
    normed[...] = (inside * rows[2:3] + rows[3:4]).astype(bf16)
    wait_all(copies)

    @column_loop(width)
    def project(cols):
        low = normed[...]
        queries[:, cols] = (dot(low, weights[0, :, cols]) + rows[22:23, cols]).astype(bf16)
        keys[:, cols] = dot(low, weights[1, :, cols]).astype(bf16)
        values[:, cols] = (dot(low, weights[2, :, cols]) + rows[23:24, cols]).astype(bf16)

    for head in range(HEADS):
        soft, cols = attend(queries, keys, head, size, length, size ** (-0.5))
        mixed[:, cols] = dot(soft.astype(bf16), values[:, cols]).astype(bf16)

    @column_loop(width)
    def branch(cols):
        out[:, cols] = (
            stream[:, cols] + dot(mixed[...], weights[3, :, cols]) + rows[24:25, cols]
        )


def attention_heads_backward_kernel(
    count, meta, grad, queries, keys, values, mixed, had, *refs
):
    own, other = refs[:count], refs[count : 2 * count]
    lows, here, there, sums, weights, branch_grad, low_mixed, sems = refs[2 * count :]
    store = store_by_core(meta[count], here, there)
    sums[...] = had[...]
    core, length = meta[count], meta[count + 1]
    width = grad.shape[1]
    size = width // HEADS
    score_scale = size ** (-0.5)
    copies = halves_to_panels(3, 4, own, other, meta, core, weights, sems)
    start_all(copies)
    branch_grad[...] = grad[...].astype(bf16)
    sums[24:25] = column_sum(branch_grad[...].astype(f32))
    put_blocks(store, 0, mixed, branch_grad, here.shape[0])
    wait_all(copies)

    @column_loop(width)
    def through(cols):
        low_mixed[:, cols] = dot_nt(branch_grad[...], weights[0, cols, :]).astype(bf16)

    for head in range(HEADS):
        soft, cols = attend(queries, keys, head, size, length, score_scale)
        low = low_mixed[:, cols]
        soft_grad = dot_nt(low, values[:, cols])
        lows[2, :, cols] = dot_tn(soft.astype(bf16), low).astype(bf16)
        along = jnp.sum(soft_grad * soft, axis=-1, keepdims=True)
        score_grad = (soft * (soft_grad - along)).astype(bf16)
        lows[0, :, cols] = (dot(score_grad, keys[:, cols]) * score_scale).astype(bf16)
        lows[1, :, cols] = (dot_tn(score_grad, queries[:, cols]) * score_scale).astype(bf16)

    sums[22:23] = column_sum(lows[0].astype(f32))
    sums[23:24] = column_sum(lows[2].astype(f32))


def attention_in_backward_kernel(count, meta, grad, stream, normed, lows, rows, had, *refs):
    own, other = refs[:count], refs[count : 2 * count]
    out, here, there, sums, half_low, weights, normed_grad, sems = refs[2 * count :]
    core = meta[count]
    store = store_by_core(core, here, there)
    sums[...] = had[...]
    width = stream.shape[1]
    copies = halves_to_panels(0, 3, own, other, meta, core, weights, sems)
    start_all(copies)
    for i in range(3):
        put_blocks(store, i, normed, lows.at[i], here.shape[0])
    wait_all(copies)

    @column_loop(width)
    def back(cols):
        total = dot_nt(lows[0], weights[0, cols, :])
        total = total + dot_nt(lows[1], weights[1, cols, :])
        normed_grad[:, cols] = total + dot_nt(lows[2], weights[2, cols, :])

    inside, inverse = norm_parts(stream[...])
    pulled = normed_grad[...]
    sums[2:3] = column_sum(pulled * inside)
    sums[3:4] = column_sum(pulled)
    flow = grad[...] + norm_pull(inside, inverse, rows[2:3], pulled)
    out[...] = flow
    half_low[...] = (0.5 * flow).astype(bf16)
    sums[16:17] = column_sum(half_low[...].astype(f32))


def moved(values, steps):
    if steps == 0:
        return values
    tall = values.shape[0]
    spot = lax.broadcasted_iota(jnp.int32, values.shape, 0) + steps
    return jnp.where((spot >= 0) & (spot < tall), pltpu.roll(values, (-steps) % tall, 0), 0.0)


def gated_depth(wide, rows, length):
    value, gate = wide[0], wide[1]
    open_gate = jax.nn.sigmoid(gate)
    inside = lax.broadcasted_iota(jnp.int32, value.shape, 0) < length
    gated = jnp.where(inside, value * open_gate, 0.0)
    depth = rows[27:28] + rows[28:29] * moved(gated, -(KERNEL // 2))
    for tap in range(1, KERNEL):
        depth = depth + rows[28 + tap : 29 + tap] * moved(gated, tap - KERNEL // 2)
    return value, open_gate, inside, gated, depth


def conv_forward_kernel(count, meta, stream, rows, *refs):
    own, other = refs[:count], refs[count : 2 * count]
    out, normed, wide, active, weights, sems = refs[2 * count :]
    core, length = meta[count], meta[count + 1]
    width = stream.shape[1]
    copies = halves_to_panels(4, 7, own, other, meta, core, weights, sems)
    start_all(copies)
    inside, ignored = norm_parts(stream[...])
    normed[...] = (inside * rows[4:5] + rows[5:6]).astype(bf16)
    wait_all(copies)

    @column_loop(width)
    def project(cols):
        for i in range(2):
            wide[i, :, cols] = dot(normed[...], weights[i, :, cols]) + rows[25 + i : 26 + i, cols]

    depth = gated_depth(wide, rows, length)[-1]
    inside, ignored = norm_parts(depth)
    shifted = inside * rows[6:7] + rows[7:8]
    active[...] = (shifted * jax.nn.sigmoid(shifted)).astype(bf16)

    @column_loop(width)
    def branch(cols):
        out[:, cols] = (
            stream[:, cols] + dot(active[...], weights[2, :, cols]) + rows[33:34, cols]
        )


def conv_out_backward_kernel(count, meta, grad, wide, active, rows, had, *refs):
    own, other = refs[:count], refs[count : 2 * count]
    lows, here, there, sums, weights, full, sems = refs[2 * count :]
    core, length = meta[count], meta[count + 1]
    store = store_by_core(core, here, there)
    sums[...] = had[...]
    width = grad.shape[1]
    copies = halves_to_panels(6, 7, own, other, meta, core, weights, sems)
    start_all(copies)
    branch_grad = grad[...].astype(bf16)
    lows[0] = branch_grad
    sums[33:34] = column_sum(branch_grad.astype(f32))
    put_blocks(store, 0, active, lows.at[0], here.shape[0])
    wait_all(copies)

    @column_loop(width)
    def through(cols):
        full[:, cols] = dot_nt(lows[0], weights[0, cols, :])

    value, open_gate, valid, gated, depth = gated_depth(wide, rows, length)
    inside, inverse = norm_parts(depth)
    shifted = inside * rows[6:7] + rows[7:8]
    share = jax.nn.sigmoid(shifted)
    outer_grad = full[...] * share * (1.0 + shifted * (1.0 - share))
    sums[6:7] = column_sum(outer_grad * inside)
    sums[7:8] = column_sum(outer_grad)
    depth_grad = norm_pull(inside, inverse, rows[6:7], outer_grad)
    sums[27:28] = column_sum(depth_grad)
    gated_grad = jnp.zeros_like(depth_grad)
    for tap in range(KERNEL):
        off = tap - KERNEL // 2
        sums[28 + tap : 29 + tap] = column_sum(depth_grad * moved(gated, off))
        gated_grad = gated_grad + rows[28 + tap : 29 + tap] * moved(depth_grad, -off)
    gated_grad = jnp.where(valid, gated_grad, 0.0)
    lows[0] = (gated_grad * open_gate).astype(bf16)
    lows[1] = (gated_grad * value * open_gate * (1.0 - open_gate)).astype(bf16)
    for i in range(2):
        sums[25 + i : 26 + i] = column_sum(lows[i].astype(f32))


def conv_in_backward_kernel(count, meta, grad, stream, normed, lows, rows, had, *refs):
    own, other = refs[:count], refs[count : 2 * count]
    out, here, there, sums, weights, full, sems = refs[2 * count :]
    core = meta[count]
    store = store_by_core(core, here, there)
    sums[...] = had[...]
    width = stream.shape[1]
    copies = halves_to_panels(4, 6, own, other, meta, core, weights, sems)
    start_all(copies)
    for i in range(2):
        put_blocks(store, i, normed, lows.at[i], here.shape[0])
    wait_all(copies)

    @column_loop(width)
    def back(cols):
        full[:, cols] = dot_nt(lows[0], weights[0, cols, :]) + dot_nt(lows[1], weights[1, cols, :])

    inside, inverse = norm_parts(stream[...])
    pulled = full[...]
    sums[4:5] = column_sum(pulled * inside)
    sums[5:6] = column_sum(pulled)
    out[...] = grad[...] + norm_pull(inside, inverse, rows[4:5], pulled)


def pull_kernel(gain, grad, stream, mine, came, rows, had, out, sums):
    sums[...] = had[...]
    inside, inverse = norm_parts(stream[...])
    pulled = mine[...] + came[...].astype(f32)
    sums[gain : gain + 1] = column_sum(pulled * inside)
    sums[gain + 1 : gain + 2] = column_sum(pulled)
    flow = grad[...] + norm_pull(inside, inverse, rows[gain : gain + 1], pulled)
    out[...] = flow.astype(out.dtype)


def pull_call(gain, grad, stream, mine, came, rows, had, dtype):
    return pl.pallas_call(
        functools.partial(pull_kernel, gain),
        out_shape=[
            jax.ShapeDtypeStruct(grad.shape, dtype),
            jax.ShapeDtypeStruct(had.shape, f32),
        ],
        cost_estimate=pl.CostEstimate(
            flops=20 * grad.size, bytes_accessed=16 * grad.size, transcendentals=0
        ),
        compiler_params=pltpu.CompilerParams(vmem_limit_bytes=VMEM_LIMIT),
        name="norm_pull",
    )(grad, stream, mine, came, rows, had)


def turn_kernel(meta, stream, mine, came, cotangent, rows, layer_out, out, half_low, sums):
    last = stream[...] + 0.5 * (mine[...] + came[...].astype(f32) + rows[21:22])
    inside, inverse = norm_parts(last)
    layer_out[...] = (inside * rows[10:11] + rows[11:12]).astype(bf16)
    spot = lax.broadcasted_iota(jnp.int32, last.shape, 0)
    grad = jnp.where(spot < meta[0], cotangent[...].astype(f32), 0.0)
    sums[...] = jnp.zeros_like(sums)
    sums[10:11] = column_sum(grad * inside)
    sums[11:12] = column_sum(grad)
    flow = norm_pull(inside, inverse, rows[10:11], grad)
    out[...] = flow
    half_low[...] = (0.5 * flow).astype(bf16)
    sums[21:22] = column_sum(half_low[...].astype(f32))


def turn_call(length, stream, mine, came, cotangent, rows):
    return pl.pallas_call(
        turn_kernel,
        in_specs=[pl.BlockSpec(memory_space=SMEM)] + [pl.BlockSpec(memory_space=VMEM)] * 5,
        out_shape=[
            jax.ShapeDtypeStruct(stream.shape, bf16),
            jax.ShapeDtypeStruct(stream.shape, f32),
            jax.ShapeDtypeStruct(stream.shape, bf16),
            jax.ShapeDtypeStruct(rows.shape, f32),
        ],
        cost_estimate=pl.CostEstimate(
            flops=30 * stream.size, bytes_accessed=20 * stream.size, transcendentals=0
        ),
        compiler_params=pltpu.CompilerParams(vmem_limit_bytes=VMEM_LIMIT),
        name="turn",
    )(length, stream, mine, came, cotangent, rows)


def panel_call(kernel, name, panels, meta, blocks, own, other, outs, scratch, flops):
    count = len(own)
    width = blocks[0].shape[1]
    return pl.pallas_call(
        functools.partial(kernel, count),
        out_shape=outs,
        in_specs=[pl.BlockSpec(memory_space=SMEM)]
        + [pl.BlockSpec(memory_space=VMEM)] * len(blocks)
        + [pl.BlockSpec(memory_space=ANY)] * (2 * count),
        out_specs=[pl.BlockSpec(memory_space=VMEM)] * len(outs),
        scratch_shapes=[VMEM((panels, width, width), bf16)]
        + scratch
        + [pltpu.SemaphoreType.DMA((2 * count,))],
        compiler_params=pltpu.CompilerParams(vmem_limit_bytes=VMEM_LIMIT),
        cost_estimate=pl.CostEstimate(
            flops=flops,
            bytes_accessed=panels * width * width * 2 + 8 * blocks[0].size * 4,
            transcendentals=2 * blocks[0].size,
        ),
        name=name,
    )(meta, *blocks, *own, *other)


def both_cores(values):
    return jnp.concatenate([values, swap_cores(values)], axis=0)


def on_device(
    outer,
    owners_count,
    frames,
    lengths,
    cotangent,
    panels,
    vectors,
    vector_first,
    vector_second,
    owners,
    basis_left,
    basis_right,
    panel_first,
    panel_second,
    panel_master,
):
    seq_count, seq_len, width = frames.shape
    tokens = seq_count * seq_len
    depth = panels.shape[1]
    half = width // 2
    quarter = width // (2 * outer)
    core = lax.axis_index("c")
    parity = lax.axis_index("o") % 2
    wires = Wires(outer, owners_count)
    shape = jax.ShapeDtypeStruct

    def chip_share(first, side):
        panel = 2 * core + side
        ins = lax.dynamic_slice_in_dim(panels, first + panel, 1, 0)
        outs = lax.dynamic_slice_in_dim(panels, first + 4 + panel, 1, 0)
        return jnp.concatenate([ins, outs], axis=0)

    first = Gather(wires, chip_share(0, parity), 0)
    middle = Gather(wires, lax.dynamic_slice_in_dim(panels[8:15], core * half, half, 2), 1)
    second = Gather(wires, chip_share(15, parity), 0)
    first_other = [Cell(chip_share(0, 1 - parity))]
    second_other = [Cell(chip_share(15, 1 - parity))]
    middle_other = []

    class Passing:
        def __init__(self, gather, route, store, start):
            self.gather, self.route, self.store, self.next = gather, route, store, start

        def more(self, most=1):
            sends = []
            while most and self.next < len(self.gather.pieces):
                sends.append((self.gather.pieces[self.next].value, self.route, self.store.append))
                self.next += 1
                most -= 1
            return sends

    to_chip = Passing(first, "chip", first_other, 1)
    to_chip_too = Passing(second, "chip", second_other, 1)
    to_core = Passing(middle, "core", middle_other, 0)
    slot = wires.slot

    def values(cells):
        return [cell.value for cell in cells]

    def core_rows(first):
        rows = lax.dynamic_slice_in_dim(vectors, first + 2 * core, 2, 0)
        rows = jnp.where(parity == 0, rows, rows[::-1])
        return rows[:, None, :]

    def meta_of(gather, *more):
        return jnp.concatenate([gather.spots(), jnp.stack(more).astype(jnp.int32)])

    low_stream = shape((tokens, width), bf16)
    stream = shape((tokens, width), f32)

    left = Cell(basis_left.astype(bf16))
    right = Cell(basis_right.astype(bf16))
    start = Cell(frames.reshape(tokens, width).astype(f32))
    normed = Cell(
        both_cores(layer_norm(start.value, vectors[0], vectors[1]).astype(bf16))
    )
    bias_first, bias_second = Cell(core_rows(12)), Cell(core_rows(17))
    ready = [start, normed, bias_first, bias_second, *first_other, *second_other]
    came = slot(first.hop(), to_core.more())
    bind(*ready, *came)
    slot(first.hop(), to_chip.more())
    slot(middle.hop(), to_chip.more(2))
    slot(first.hop(), to_chip.more(), to_core.more(2))
    slot(second.hop(), to_chip.more())
    slot(first.hop(), to_chip.more())
    came = slot(middle.hop(), to_chip.more(), to_chip_too.more())
    bind(left, right, *wires.past[-2])
    while any(first.left):
        came = slot(first.hop())
    while to_chip.next < len(first.pieces):
        came = slot(to_chip.more(2))
    came = slot(second.hop(), to_chip_too.more(), to_core.more(2))
    bind(normed, *wires.past[-2])
    slot(middle.hop(), to_chip_too.more(2))
    hidden, active, mine, away = ffn_forward_call(
        normed.value, bias_first.value, values(first.pieces), values(first_other),
        meta_of(first, parity),
    )
    after_first = Cell(
        start.value + 0.5 * (mine + swap_cores(away).astype(f32) + vectors[16])
    )
    kept_first = (normed.value, hidden, active)
    bind(after_first, *wires.past[-1], *wires.past[-2])
    slot(second.hop(), to_core.more(2))
    slot(middle.hop(), second.hop(), to_chip_too.more(2))
    while any(middle.left) or any(second.left):
        slot(middle.hop(), second.hop(), to_chip_too.more(2), to_core.more(2))
    came = wires.start(to_core.more(2), to_chip_too.more(), after=wires.past[-1])
    while to_core.next < len(middle.pieces):
        came += slot(to_core.more(2))
    middle_meta = meta_of(middle, core, lengths[0])
    bind(after_first, *wires.past[-1])
    after_attn, attn_normed, queries, keys, values_, mixed = panel_call(
        attention_forward_kernel,
        "attention_forward",
        4,
        middle_meta,
        [after_first.value, vectors],
        values(middle.pieces),
        values(middle_other),
        [stream] + [low_stream] * 5,
        [],
        8 * tokens * width * width,
    )
    after_attn = Cell(after_attn)
    bind(after_attn, *came)
    came = []
    while to_chip_too.next < len(second.pieces):
        came += wires.start(to_chip_too.more(2), after=[after_attn])
    after_conv, conv_normed, wide, conv_active = panel_call(
        conv_forward_kernel,
        "conv_forward",
        3,
        middle_meta,
        [after_attn.value, vectors],
        values(middle.pieces),
        values(middle_other),
        [stream, low_stream, shape((2, tokens, width), f32), low_stream],
        [],
        6 * tokens * width * width,
    )
    normed = both_cores(layer_norm(after_conv, vectors[8], vectors[9]).astype(bf16))
    hidden, active, mine, away = ffn_forward_call(
        normed, bias_second.value, values(second.pieces), values(second_other),
        meta_of(second, parity),
    )
    kept_second = (normed, hidden, active)
    layer_out, grad_flow, half_low, sums = turn_call(
        lengths, after_conv, mine, swap_cores(away), cotangent.reshape(tokens, width), vectors
    )

    def ring_of(turn, *matrices):
        return Reduce(wires, row_parts(depth, *matrices), turn)

    class Share:
        def __init__(self, here, there):
            self.here, self.there = here, there

        def hop(self):
            return [(self.there, "core", self.take)]

        def take(self, cell):
            self.came = cell

        def total(self):
            return (self.here.astype(f32) + self.came.value.astype(f32)).astype(bf16)

    def trade_cores(block):
        there = lax.dynamic_index_in_dim(block, 1 - core, 0, keepdims=False)
        here = lax.dynamic_index_in_dim(block, core, 0, keepdims=False)
        came = swap_cores(there.astype(bf16)).astype(f32)
        return jnp.where(
            core == 0, jnp.concatenate([here, came]), jnp.concatenate([came, here])
        )

    chip = lax.axis_index("o")
    pairs = outer == 2

    def ffn_backward_out(half_low, gather, other, kept, bias, sums, ways):
        normed, hidden, active = kept
        return ffn_backward_call(
            ffn_out_backward_kernel,
            "ffn_out_backward",
            bias,
            outer,
            ways,
            meta_of(gather, parity, core, chip),
            [hidden, active, both_cores(half_low), sums],
            values(gather.pieces),
            values(other),
            [shape((2, 2 * tokens, width), bf16), shape(vectors.shape, f32)],
        )

    def ffn_backward_in(low, gather, other, kept, ways):
        return ffn_backward_call(
            ffn_in_backward_kernel,
            "ffn_in_backward",
            0,
            outer,
            ways,
            meta_of(gather, parity, core, chip),
            [kept[0], low],
            values(gather.pieces),
            values(other),
            [shape((tokens, width), f32), shape((tokens, width), bf16)],
        )

    def middle_call(kernel, name, used, arrays, outs, scratch, flops):
        block_shape = shape((outer, used, width, quarter), bf16)
        return panel_call(
            kernel,
            name,
            used,
            middle_meta,
            arrays,
            values(middle.pieces),
            values(middle_other),
            [outs[0], block_shape, block_shape, shape(vectors.shape, f32), *outs[1:]],
            scratch,
            flops * tokens * width * width,
        )

    class Part:
        def __init__(self, matrices, turn):
            self.turn = turn
            self.ring = None
            if len(matrices) == 3:
                self.chips = ChipSum(wires, here=matrices[0], there=matrices[1:])
            else:
                self.chips = None
                self.ring = ring_of(turn, *matrices)

        def send(self):
            return self.chips.send()

        def hop(self):
            if self.ring is None:
                self.ring = ring_of(self.turn, self.chips.total().astype(bf16))
            return self.ring.hop()

        def finish(self):
            if self.chips is not None:
                return []
            self.chips = ChipSum(wires, blocks=self.ring.total())
            self.late = True
            return self.chips.send()

        def total(self):
            if self.chips is None:
                slot(self.finish())
            return self.chips.total() if hasattr(self, "late") else self.ring.total()

    begin = wires.start
    low, sums, *matrices = ffn_backward_out(
        half_low, second, second_other, kept_second, 17, sums, False
    )
    second_out = Part(matrices, 0)
    low = Cell(low)
    came = begin(second_out.hop(), after=[low])
    mine, away, *matrices = ffn_backward_in(
        low.value, second, second_other, kept_second, pairs
    )
    mine = Cell(mine)
    bind(mine, *came)
    second_in = Part(matrices, 1)
    came = begin(second_out.hop(), second_in.send() if pairs else [], after=[mine])
    grad_flow, sums = pull_call(
        8, grad_flow, after_conv, mine.value, swap_cores(away), vectors, sums, f32
    )
    lows, here, there, sums = middle_call(
        conv_out_backward_kernel,
        "conv_out_backward",
        1,
        [grad_flow, wide, conv_active, vectors, sums],
        [shape((2, tokens, width), bf16)],
        [VMEM((tokens, width), f32)],
        4,
    )
    lows = Cell(lows)
    bind(lows, *came)
    conv_out = Share(here, there)
    came = begin(
        second_out.hop(), second_in.send() if pairs else [], conv_out.hop(), after=[lows]
    )
    flow, here, there, sums = middle_call(
        conv_in_backward_kernel,
        "conv_in_backward",
        2,
        [grad_flow, after_attn.value, conv_normed, lows.value, vectors, sums],
        [stream],
        [VMEM((tokens, width), f32)],
        8,
    )
    flow = Cell(flow)
    conv_in = Share(here, there)
    lows, here, there, sums = middle_call(
        attention_heads_backward_kernel,
        "attention_heads_backward",
        1,
        [flow.value, queries, keys, values_, mixed, sums],
        [shape((3, tokens, width), bf16)],
        [VMEM((tokens, width), bf16), VMEM((tokens, width), bf16)],
        6,
    )
    lows = Cell(lows)
    bind(lows, *came)
    attn_out = Share(here, there)
    came = begin(
        second_out.hop(), second_in.hop(), conv_in.hop(), attn_out.hop(), after=[lows]
    )
    flow.value, here, there, sums, half_low = middle_call(
        attention_in_backward_kernel,
        "attention_in_backward",
        3,
        [flow.value, after_first.value, attn_normed, lows.value, vectors, sums],
        [stream, low_stream],
        [VMEM((tokens, width), f32)],
        12,
    )
    half_low = Cell(half_low)
    bind(half_low, *came)
    attn_in = Share(here, there)
    conv_part = ring_of(0, conv_in.total(), conv_out.total())
    came = begin(
        conv_part.hop(), second_in.hop(), attn_in.hop(), second_out.finish(), after=[half_low]
    )
    low, sums, *matrices = ffn_backward_out(
        half_low.value, first, first_other, kept_first, 12, sums, pairs
    )
    first_out = Part(matrices, 1)
    low = Cell(low)
    bind(low, *came)
    attn_in_total, attn_out_total = attn_in.total(), attn_out.total()
    if pairs:
        attn_chips = ChipSum(
            wires, blocks=jnp.concatenate([attn_in_total, attn_out_total], axis=1)
        )
        attn_sends = attn_chips.send()
    else:
        attn_part, attn_sends = ring_of(1, attn_in_total, attn_out_total), []
    came = begin(conv_part.hop(), second_in.hop(), attn_sends, after=[low])
    mine, away, *matrices = ffn_backward_in(low.value, first, first_other, kept_first, False)
    first_in = Part(matrices, 0)
    mine = Cell(mine)
    bind(mine, *came)
    wires.past = [came]
    slot(first_in.hop(), conv_part.hop(), first_out.send() if pairs else [])
    frames_grad, sums = pull_call(
        0, flow.value, start.value, mine.value, swap_cores(away), vectors, sums, bf16
    )
    frames_grad, sums = Cell(frames_grad), Cell(sums)
    bind(sums, frames_grad, *came)
    vector_sum = AllSum(wires, sums.value)
    if pairs:
        attn_part = ring_of(1, attn_chips.total().astype(bf16))
    slot(first_in.hop(), attn_part.hop(), first_out.send() if pairs else [], vector_sum.hop())
    slot(first_in.hop(), conv_part.hop(), second_in.hop(), vector_sum.hop())
    slot(first_in.hop(), attn_part.hop(), vector_sum.hop())
    conv_chips = ChipSum(wires, blocks=conv_part.total())
    slot(attn_part.hop(), first_out.hop(), conv_chips.send(), vector_sum.hop())
    slot(attn_part.hop(), first_out.hop(), first_in.finish(), vector_sum.hop())
    early = [trade_cores(second_in.total()), trade_cores(second_out.total()), conv_chips.total()]
    early = [Cell(part) for part in early]
    slot(first_out.hop())
    slot(first_out.hop())
    late = [trade_cores(first_in.total()), attn_part.total()]
    if not pairs:
        late[1] = ChipSum(wires, blocks=late[1]).total()
    late = [Cell(part) for part in late]
    vector_grads = Cell(vector_sum.total())
    bind(vector_grads, *early, *late, *wires.past[-2])
    vector_grads = vector_grads.value
    panel_grads = jnp.concatenate(
        [
            late[0].value,
            trade_cores(first_out.total()),
            late[1].value,
            early[2].value,
            early[0].value,
            early[1].value,
        ],
        axis=0,
    )
    vector_first_new = beta_one * vector_first + (1.0 - beta_one) * vector_grads
    vector_second_new = beta_two * vector_second + (1.0 - beta_two) * vector_grads * vector_grads
    vectors_new = vectors - vector_rate * adam_step(vector_first_new, vector_second_new)
    panel_grads = Cell(panel_grads)
    updated = [Cell(vector_first_new), Cell(vector_second_new), Cell(vectors_new)]
    bind(panel_grads, frames_grad, *updated)
    panel_grads = panel_grads.value

    slot_count = panel_first.shape[1]
    panel_count = owners.shape[0]
    panel_index = jnp.arange(panel_count, dtype=jnp.int32)
    same_owner = owners[:, None] == owners[None, :]
    earlier = panel_index[None, :] < panel_index[:, None]
    slot_of = jnp.sum((same_owner & earlier).astype(jnp.int32), axis=1)
    target = owners * slot_count + slot_of
    slot_hit = target[:, None] == jnp.arange(owners_count * slot_count, dtype=jnp.int32)[None, :]
    source = jnp.sum(slot_hit.astype(jnp.int32) * panel_index[:, None], axis=0)
    filled = jnp.any(slot_hit, axis=0)
    mine = lax.dynamic_slice_in_dim(filled, lax.axis_index("f") * slot_count, slot_count)

    outgoing = pick(panel_grads.astype(bf16), source)
    outgoing = outgoing.reshape(owners_count, slot_count, depth, quarter)
    incoming = lax.all_to_all(outgoing, "f", split_axis=0, concat_axis=0, tiled=True)
    block = lax.axis_index("o") * 2 + core
    left_rows = lax.dynamic_slice_in_dim(left.value, block * quarter, quarter, 1)
    results = []
    for s in range(slot_count):
        turned = dot_tn(left.value[s], incoming[:, s].reshape(width, quarter)).astype(bf16)
        turned = trade_blocks(turned.reshape(outer, 2 * quarter, quarter), "o", outer)
        turned = turned.reshape(outer, 2, quarter, quarter).transpose(1, 0, 2, 3)
        turned = trade_blocks(turned, "c", 2)
        turned = turned.transpose(2, 1, 0, 3).reshape(quarter, width)
        rotated = dot(turned, right.value[s])
        first_new = beta_one * panel_first[:, s] + (1.0 - beta_one) * rotated
        second_new = beta_two * panel_second[:, s] + (1.0 - beta_two) * rotated * rotated
        step_values = adam_step(first_new, second_new).astype(bf16)
        back_turn = dot_nt(step_values, right.value[s]).astype(bf16)
        back_turn = gather_blocks(back_turn, "o", outer)
        back_turn = gather_blocks(back_turn, "c", 2)
        back_turn = back_turn.transpose(1, 0, 2, 3).reshape(width, width)
        update = dot(left_rows[s], back_turn)
        results.append(
            (
                jnp.where(mine[s], first_new, 0.0),
                jnp.where(mine[s], second_new, 0.0),
                jnp.where(mine[s], panel_master[:, s] - learn_rate * update, 0.0),
            )
        )
    first_new, second_new, master_new = [jnp.stack(part, axis=1) for part in zip(*results)]
    return (
        layer_out.reshape(frames.shape),
        frames_grad.value.reshape(frames.shape),
        panel_grads,
        vector_grads,
        *values(updated),
        first_new,
        second_new,
        master_new,
    )


def solution(mesh):
    outer = mesh.shape["dp"] // 2
    owners_count = mesh.shape["fsdp"]
    split = Mesh(mesh.devices.reshape(outer, 2, owners_count), ("o", "c", "f"))
    every = P(("o", "c", "f"), None, None)
    state = P(("o", "c"), "f", None)
    return jax.shard_map(
        functools.partial(on_device, outer, owners_count),
        mesh=split,
        in_specs=(
            every,
            P(("o", "c", "f")),
            every,
            P(None, "f", None),
            P(),
            P(),
            P(),
            P(),
            P("f", None, None),
            P("f", None, None),
            state,
            state,
            state,
        ),
        out_specs=(
            every,
            every,
            P(None, "f", ("o", "c")),
            P(),
            P(),
            P(),
            P(),
            state,
            state,
            state,
        ),
        check_vma=False,
    )
```

```python
import functools

import jax
import jax.numpy as jnp
from jax import lax
from jax.experimental import pallas as pl
from jax.experimental.pallas import tpu as pltpu
from jax.sharding import Mesh
from jax.sharding import PartitionSpec as P

HEADS = 8
KERNEL = 5
STEPS = 4


norm_eps = 1e-05
adam_eps = 1e-08
beta_one = 0.5
beta_two = 0.5
learn_rate = 0.02
vector_rate = 0.25

bf16 = jnp.bfloat16
f32 = jnp.float32
ANY = pl.ANY
VMEM = pltpu.VMEM
SMEM = pltpu.SMEM
SWAP = [(0, 1), (1, 0)]
TILE = 1024
tie = lax.optimization_barrier
VMEM_LIMIT = 56 * 1024 * 1024


def layer_norm(values, gain_row, shift_row):
    centred = values - jnp.mean(values, axis=-1, keepdims=True)
    inverse = lax.rsqrt(jnp.mean(centred * centred, axis=-1, keepdims=True) + norm_eps)
    return centred * inverse * gain_row + shift_row


def norm_backward(residual, gain_row, shift_row, normed_grad):
    ignored, pull_back = jax.vjp(layer_norm, residual, gain_row, shift_row)
    return pull_back(normed_grad)


def adam_step(first_new, second_new):
    return (
        first_new
        / (1.0 - beta_one**STEPS)
        / (jnp.sqrt(second_new / (1.0 - beta_two**STEPS)) + adam_eps)
    )


def token_sum(values):
    return jnp.sum(values, axis=0, dtype=f32)


def dot(left, right):
    return lax.dot_general(left, right, (((1,), (0,)), ((), ())), preferred_element_type=f32)


def dot_nt(left, right):
    return lax.dot_general(left, right, (((1,), (1,)), ((), ())), preferred_element_type=f32)


def dot_tn(left, right):
    return lax.dot_general(left, right, (((0,), (0,)), ((), ())), preferred_element_type=f32)


class Cell:
    def __init__(self, value):
        self.value = value


def bind(*cells):
    for cell, value in zip(cells, tie(tuple(cell.value for cell in cells))):
        cell.value = value


class Wires:
    def __init__(self, outer, owners_count):
        self.outer, self.count = outer, owners_count
        walk = list(range(0, owners_count, 2)) + list(range(owners_count - 1, 0, -2))
        onward = [(walk[i], walk[(i + 1) % owners_count]) for i in range(owners_count)]
        self.routes = {
            "onward": ("f", onward),
            "back": ("f", [(b, a) for a, b in onward]),
            "chip": ("o", [(i, i ^ 1) for i in range(outer)]),
            "core": ("c", SWAP),
        }
        for name, count in (("o", outer), ("f", owners_count)):
            step = 1
            while step < count:
                self.routes[f"{name}{step}"] = (name, [(i, i ^ step) for i in range(count)])
                step *= 2
        index = lax.axis_index("f")
        self.place = jnp.where(index % 2 == 0, index // 2, owners_count - 1 - index // 2)
        self.past = []

    def start(self, *groups, after=(), beside=()):
        sends = [send for group in groups for send in group]
        if sends and not after:
            cells = [Cell(value) for value, route, take in sends]
            bind(*cells, *beside)
            sends = [(cell.value, *send[1:]) for cell, send in zip(cells, sends)]
        came = []
        for value, route, take in sends:
            if after:
                value = tie((value, *[cell.value for cell in after]))[0]
            axis, pairs = self.routes[route]
            came.append(Cell(lax.ppermute(value, axis, pairs)))
            take(came[-1])
        return came

    def slot(self, *groups):
        came = self.start(*groups, after=self.past[-2] if len(self.past) >= 2 else ())
        if came:
            self.past.append(came)
        return came

    def index_at(self, steps):
        spot = (self.place + steps + self.count) % self.count
        return jnp.where(spot < self.count // 2, 2 * spot, 2 * (self.count - 1 - spot) + 1)

    def reach(self, turn):
        half = self.count // 2
        return (half, half - 1) if turn == 0 else (half - 1, half)


class Gather:
    def __init__(self, wires, unit, turn):
        self.wires = wires
        self.left = list(wires.reach(turn))
        self.pieces = [Cell(unit)]
        self.origin = [wires.index_at(0)]
        self.moving = [self.pieces[0], self.pieces[0]]
        self.hops = 0

    def hop(self):
        self.hops += 1
        sends = []
        for way, (route, sign) in enumerate((("onward", -1), ("back", 1))):
            if self.left[way]:
                self.left[way] -= 1
                self.origin.append(self.wires.index_at(sign * self.hops))

                def take(cell, way=way):
                    self.moving[way] = cell
                    self.pieces.append(cell)

                sends.append((self.moving[way].value, route, take))
        return sends

    def spots(self):
        return jnp.stack(self.origin).astype(jnp.int32)


class Reduce:
    def __init__(self, wires, matrices, depth, turn):
        self.wires, self.depth = wires, depth
        self.lead = matrices.shape[:-2]
        self.flat = matrices.reshape((-1,) + matrices.shape[-2:])
        self.left = list(wires.reach(turn))
        self.moving = [None, None]

    def hop(self):
        return hop_together(self)

    def arrived(self, way):
        cell, first = self.moving[way]
        return cell.value[first : first + self.flat.shape[0]]

    def total(self):
        while any(self.left):
            self.wires.slot(self.hop())
        start = self.wires.index_at(0) * self.depth
        own = lax.dynamic_slice_in_dim(self.flat, start, self.depth, 1).astype(f32)
        total = own + self.arrived(0).astype(f32) + self.arrived(1).astype(f32)
        return total.reshape(self.lead + total.shape[1:])


def hop_kernel(plan, counts, starts, *refs):
    n_in = counts[0]
    outs = refs[n_in : n_in + counts[1]]
    came, sems = refs[n_in + counts[1] : -1], refs[-1]
    depth = outs[0].shape[1]
    copies = []
    for i, (way, place, panels, matrix, had, spot) in enumerate(plan):
        row = pl.multiple_of(starts[i] * depth, depth)
        out = outs[way].at[pl.ds(place, panels)]
        copies.append(
            pltpu.make_async_copy(refs[matrix].at[:, pl.ds(row, depth)], out, sems.at[2 * i])
        )
        if had is not None:
            copies.append(
                pltpu.make_async_copy(
                    refs[had].at[pl.ds(spot, panels)],
                    came[way].at[pl.ds(place, panels)],
                    sems.at[2 * i + 1],
                )
            )
    start_all(copies)
    wait_all(copies)
    for way, place, panels, matrix, had, spot in plan:
        if had is not None:
            for p in range(place, place + panels):
                total = outs[way][p].astype(f32) + came[way][p].astype(f32)
                outs[way][p] = total.astype(bf16)


def hop_together(*sums):
    wires, depth = sums[0].wires, sums[0].depth
    columns = sums[0].flat.shape[-1]
    arrays = [part.flat for part in sums]
    cells, plan, starts, sends, sizes = [], [], [], [], []
    for way, (route, sign) in enumerate((("onward", 1), ("back", -1))):
        going = [i for i, part in enumerate(sums) if part.left[way]]
        if not going:
            continue
        place = 0
        places = []
        for i in going:
            part = sums[i]
            had, spot = None, 0
            if part.moving[way] is not None:
                cell, spot = part.moving[way]
                if all(cell is not c for c in cells):
                    cells.append(cell)
                had = len(arrays) + [cell is c for c in cells].index(True)
            panels = part.flat.shape[0]
            plan.append((len(sends), place, panels, i, had, spot))
            starts.append(wires.index_at(sign * part.left[way]))
            part.left[way] -= 1
            places.append((part, place))
            place += panels

        def take(cell, way=way, places=places):
            for part, first in places:
                part.moving[way] = (cell, first)

        sends.append((route, take))
        sizes.append(place)
    if not sends:
        return []
    inputs = arrays + [cell.value for cell in cells]
    messages = pl.pallas_call(
        functools.partial(hop_kernel, tuple(plan), (len(inputs), len(sizes))),
        out_shape=[jax.ShapeDtypeStruct((n, depth, columns), bf16) for n in sizes],
        in_specs=[pl.BlockSpec(memory_space=SMEM)] + [pl.BlockSpec(memory_space=ANY)] * len(inputs),
        out_specs=[pl.BlockSpec(memory_space=VMEM)] * len(sizes),
        scratch_shapes=[VMEM((n, depth, columns), bf16) for n in sizes]
        + [pltpu.SemaphoreType.DMA((2 * len(plan),))],
        compiler_params=pltpu.CompilerParams(vmem_limit_bytes=VMEM_LIMIT),
        cost_estimate=pl.CostEstimate(
            flops=sum(sizes) * depth * columns,
            bytes_accessed=6 * sum(sizes) * depth * columns,
            transcendentals=0,
        ),
        name="hop",
    )(jnp.stack(starts).astype(jnp.int32), *inputs)
    return [(message, *send) for message, send in zip(messages, sends)]


class AllSum:
    def __init__(self, wires, value):
        self.wires, self.value = wires, Cell(value)
        self.todo = ["core"] + [name for name in wires.routes if name[1:].isdigit()]
        self.came = None

    def hop(self):
        if not self.todo:
            return []
        self.settle()
        return [(self.value.value, self.todo.pop(0), self.take)]

    def take(self, cell):
        self.came = cell

    def settle(self):
        if self.came is not None:
            self.value = Cell(self.value.value + self.came.value)
            self.came = None

    def total(self):
        while self.todo:
            self.wires.slot(self.hop())
        self.settle()
        return self.value.value


class ChipSum:
    def __init__(self, wires, blocks=None, here=None, there=None, cuts=None):
        self.wires, self.blocks, self.cuts = wires, blocks, cuts
        if blocks is not None and wires.outer == 2:
            index = lax.axis_index("o")
            here = lax.dynamic_index_in_dim(blocks, index, 0, keepdims=False)
            there = lax.dynamic_index_in_dim(blocks, 1 - index, 0, keepdims=False)
            there = [there] if cuts is None else [there[a:b] for a, b in cuts]
        self.here, self.there, self.came = here, list(there or []), []

    def send(self):
        if not self.there:
            return []
        return [(self.there.pop(0).astype(bf16), "chip", self.came.append)]

    def total(self):
        if self.here is None:
            low = self.blocks.astype(bf16)
            low = lax.psum_scatter(low, "o", scatter_dimension=0, tiled=True)
            return low[0].astype(f32)
        while self.there:
            self.wires.slot(self.send())
        came = [cell.value for cell in self.came]
        if len(came) > 1:
            came = jnp.stack(came) if self.cuts is None else jnp.concatenate(came)
        else:
            came = came[0]
        return self.here.astype(f32) + came.astype(f32)


def swap_cores(values):
    return lax.ppermute(values, "c", SWAP)


def gather_blocks(values, name, count):
    if count == 2:
        index = lax.axis_index(name)
        other = lax.ppermute(values, name, SWAP)
        first = jnp.where(index == 0, values, other)
        second = jnp.where(index == 0, other, values)
        return jnp.stack([first, second])
    return lax.all_gather(values, name)


def trade_blocks(values, name, count):
    if count == 2:
        index = lax.axis_index(name)
        there = lax.dynamic_index_in_dim(values, 1 - index, 0, keepdims=False)
        here = lax.dynamic_index_in_dim(values, index, 0, keepdims=False)
        came = lax.ppermute(there, name, SWAP)
        return jnp.stack([jnp.where(index == 0, here, came), jnp.where(index == 0, came, here)])
    return lax.all_to_all(values, name, split_axis=0, concat_axis=0, tiled=True)


def pick_kernel(slots, source, grads, out, sems):
    copies = [
        pltpu.make_async_copy(grads.at[source[i]], out.at[i], sems.at[i]) for i in range(slots)
    ]
    for copy in copies:
        copy.start()
    for copy in copies:
        copy.wait()


def pick(grads, source):
    slots = source.shape[0]
    return pl.pallas_call(
        functools.partial(pick_kernel, slots),
        out_shape=jax.ShapeDtypeStruct((slots,) + grads.shape[1:], grads.dtype),
        in_specs=[pl.BlockSpec(memory_space=SMEM), pl.BlockSpec(memory_space=ANY)],
        out_specs=pl.BlockSpec(memory_space=VMEM),
        scratch_shapes=[pltpu.SemaphoreType.DMA((slots,))],
        name="pick",
    )(source, grads)


def load_share(sides, spots, first, weights, sems):
    depth = sides[0][0].shape[1]
    copies = []
    for side, pieces in enumerate(sides):
        for i, piece in enumerate(pieces):
            row = pl.multiple_of(spots[i] * depth, depth)
            copies.append(
                pltpu.make_async_copy(
                    piece.at[first],
                    weights.at[len(sides) * first + side, pl.ds(row, depth)],
                    sems.at[first, side, i],
                )
            )
    return copies


def cut_sides(refs, count, halves):
    return [refs[i * count : (i + 1) * count] for i in range(halves)], refs[halves * count :]


def ffn_forward_kernel(count, halves, meta, normed, bias, *refs):
    sides, refs = cut_sides(refs, count, halves)
    hidden, active, branch, away, weights, sems = refs
    tokens, width = branch.shape
    ins = load_share(sides, meta, 0, weights, sems)
    outs = load_share(sides, meta, 1, weights, sems)
    start_all(ins + outs)
    wait_all(ins)
    for p in range(halves):

        @column_loop(width)
        def columns(cols):
            value = dot(normed[...], weights[p, :, cols]) + bias[p, :, cols]
            hidden[p, :, cols] = value
            active[p, :, cols] = (value * jax.nn.sigmoid(value)).astype(bf16)

    wait_all(outs)

    @column_loop(width)
    def out_columns(cols):
        total = dot(active[0], weights[halves, :, cols])
        for p in range(1, halves):
            total = total + dot(active[p], weights[halves + p, :, cols])
        branch[:, cols] = total[:tokens]
        away[:, cols] = total[tokens:].astype(bf16)


def ffn_forward_call(normed, bias, sides, meta):
    tokens, width = normed.shape
    count, halves = len(sides[0]), len(sides)
    return pl.pallas_call(
        functools.partial(ffn_forward_kernel, count, halves),
        out_shape=[
            jax.ShapeDtypeStruct((halves, tokens, width), f32),
            jax.ShapeDtypeStruct((halves, tokens, width), bf16),
            jax.ShapeDtypeStruct((tokens // 2, width), f32),
            jax.ShapeDtypeStruct((tokens // 2, width), bf16),
        ],
        in_specs=[
            pl.BlockSpec(memory_space=SMEM),
            pl.BlockSpec(memory_space=VMEM),
            pl.BlockSpec(memory_space=VMEM),
        ]
        + [pl.BlockSpec(memory_space=ANY)] * (halves * count),
        out_specs=[pl.BlockSpec(memory_space=VMEM)] * 4,
        scratch_shapes=[
            VMEM((2 * halves, width, width), bf16),
            pltpu.SemaphoreType.DMA((2, halves, count)),
        ],
        compiler_params=pltpu.CompilerParams(vmem_limit_bytes=VMEM_LIMIT),
        cost_estimate=pl.CostEstimate(
            flops=4 * halves * tokens * width * width,
            bytes_accessed=8 * width * width + tokens * width * 18,
            transcendentals=halves * tokens * width,
        ),
        name="ffn_forward",
    )(meta, normed, bias, *[piece for pieces in sides for piece in pieces])


def ffn_out_backward_kernel(count, halves, bias, blocks, meta, hidden, active, grad, had, *refs):
    sides, refs = cut_sides(refs, count, halves)
    low, sums, *matrices, weights, sems = refs
    outer, ways = blocks
    width = low.shape[-1]
    parity, core = meta[count], meta[count + 1]
    store = share_store(ways, meta[count + 2], matrices)
    sums[...] = had[...]
    copies = load_share(sides, meta, 1, weights, sems)
    start_all(copies)
    for p in range(halves):
        put_blocks(store, p ^ parity if halves == 2 else p, active.at[p], grad, outer)
    wait_all(copies)
    for p in range(halves):
        row = bias + 2 * core + (p ^ parity)

        @column_loop(width)
        def rows(cols):
            value = hidden[p, :, cols]
            share = jax.nn.sigmoid(value)
            slope = share * (1.0 + value * (1.0 - share))
            part = (dot_nt(grad[...], weights[halves + p, cols, :]) * slope).astype(bf16)
            low[p, :, cols] = part
            sums[pl.ds(row, 1), cols] = jnp.sum(part.astype(f32), axis=0, keepdims=True)


def ffn_in_backward_kernel(count, halves, bias, blocks, meta, normed, low, *refs):
    sides, refs = cut_sides(refs, count, halves)
    normed_grad, away, *matrices, weights, sems = refs
    tokens, width = away.shape
    outer, ways = blocks
    parity = meta[count]
    store = share_store(ways, meta[count + 2], matrices)
    copies = load_share(sides, meta, 0, weights, sems)
    start_all(copies)
    for p in range(halves):
        put_blocks(store, p ^ parity if halves == 2 else p, normed, low.at[p], outer)
    wait_all(copies)

    @column_loop(width)
    def back(cols):
        total = dot_nt(low[0], weights[0, cols, :])
        for p in range(1, halves):
            total = total + dot_nt(low[p], weights[p, cols, :])
        normed_grad[:, cols] = total[:tokens]
        away[:, cols] = total[tokens:].astype(bf16)


def share_store(ways, chip, matrices):
    if ways:
        return store_by_chip(chip, matrices[0], matrices[1:])
    return store_all(matrices[0])


def ffn_backward_call(kernel, name, bias, outer, ways, meta, arrays, sides, outs):
    width = sides[0][0].shape[-1]
    tokens = arrays[0].shape[-2]
    count, halves = len(sides[0]), len(sides)
    quarter = width // (2 * outer)
    if ways:
        part = jax.ShapeDtypeStruct((2, width, quarter), bf16)
        blocks = [jax.ShapeDtypeStruct((2, 2, width, quarter), bf16), part, part]
    else:
        blocks = [jax.ShapeDtypeStruct((outer, 2, halves, width, quarter), bf16)]
    return pl.pallas_call(
        functools.partial(kernel, count, halves, bias, (outer, ways)),
        out_shape=[*outs, *blocks],
        in_specs=[pl.BlockSpec(memory_space=SMEM)]
        + [pl.BlockSpec(memory_space=VMEM)] * len(arrays)
        + [pl.BlockSpec(memory_space=ANY)] * (halves * count),
        out_specs=[pl.BlockSpec(memory_space=VMEM)] * (len(outs) + len(blocks)),
        scratch_shapes=[
            VMEM((2 * halves, width, width), bf16),
            pltpu.SemaphoreType.DMA((2, halves, count)),
        ],
        compiler_params=pltpu.CompilerParams(vmem_limit_bytes=VMEM_LIMIT),
        cost_estimate=pl.CostEstimate(
            flops=4 * halves * tokens * width * width,
            bytes_accessed=8 * width * width + tokens * width * 16,
            transcendentals=tokens * width,
        ),
        name=name,
    )(meta, *arrays, *[piece for pieces in sides for piece in pieces])


def norm_parts(values):
    centred = values - jnp.mean(values, axis=-1, keepdims=True)
    inverse = lax.rsqrt(jnp.mean(centred * centred, axis=-1, keepdims=True) + norm_eps)
    return centred * inverse, inverse


def norm_pull(normed, inverse, gain_row, grad):
    scaled = grad * gain_row
    along = jnp.mean(scaled * normed, axis=-1, keepdims=True)
    return inverse * (scaled - jnp.mean(scaled, axis=-1, keepdims=True) - normed * along)


def column_sum(values):
    return jnp.sum(values, axis=0, keepdims=True)


def halves_to_panels(first, last, own, other, spots, core, weights, sems):
    depth, half = own[0].shape[1:]
    copies = []
    for i in range(len(own)):
        row = pl.multiple_of(spots[i] * depth, depth)
        for side, pieces in ((core, own), (1 - core, other)):
            col = pl.multiple_of(side * half, half)
            copies.append(
                pltpu.make_async_copy(
                    pieces[i].at[pl.ds(first, last - first)],
                    weights.at[pl.ds(0, last - first), pl.ds(row, depth), pl.ds(col, half)],
                    sems.at[len(copies)],
                )
            )
    return copies


def start_all(copies):
    for copy in copies:
        copy.start()


def wait_all(copies):
    for copy in copies:
        copy.wait()


def column_loop(width):
    def run(body):
        for start in range(0, width, TILE):
            body(slice(start, start + TILE))

    return run


def put_blocks(store, panel, left, right, outer):
    quarter = right.shape[-1] // (2 * outer)

    @column_loop(left.shape[1])
    def rows(part):
        value = dot_tn(left[:, part], right[...]).astype(bf16)
        for o in range(outer):
            for c in range(2):
                at = (2 * o + c) * quarter
                store(o, c, panel, part, value[:, at : at + quarter])


def store_all(blocks):
    def store(o, c, panel, part, value):
        blocks[o, c, panel, part, :] = value

    return store


def store_by_core(core, here, there):
    def store(o, c, panel, part, value):
        @pl.when(c == core)
        def kept():
            here[o, panel, part, :] = value

        @pl.when(c != core)
        def sent():
            there[o, panel, part, :] = value

    return store


def store_by_chip(chip, here, there):
    def store(o, c, panel, part, value):
        @pl.when(o == chip)
        def kept():
            here[c, panel, part, :] = value

        @pl.when(o != chip)
        def sent():
            there[c][panel, part, :] = value

    return store


def attend(queries, keys, head, size, length, score_scale):
    cols = slice(head * size, (head + 1) * size)
    scores = dot_nt(queries[:, cols], keys[:, cols]) * score_scale
    spot = lax.broadcasted_iota(jnp.int32, scores.shape, 1)
    scores = jnp.where(spot < length, scores, -1000000000.0)
    peak = jnp.max(scores, axis=-1, keepdims=True)
    raised = jnp.exp(scores - peak)
    return raised * (1.0 / jnp.sum(raised, axis=-1, keepdims=True)), cols


def attention_forward_kernel(count, meta, stream, rows, *refs):
    own, other = refs[:count], refs[count : 2 * count]
    out, normed, queries, keys, values, mixed, weights, sems = refs[2 * count :]
    core, length = meta[count], meta[count + 1]
    width = stream.shape[1]
    size = width // HEADS
    copies = halves_to_panels(0, 4, own, other, meta, core, weights, sems)
    start_all(copies)
    inside, ignored = norm_parts(stream[...])
    normed[...] = (inside * rows[2:3] + rows[3:4]).astype(bf16)
    wait_all(copies)

    @column_loop(width)
    def project(cols):
        low = normed[...]
        queries[:, cols] = (dot(low, weights[0, :, cols]) + rows[22:23, cols]).astype(bf16)
        keys[:, cols] = dot(low, weights[1, :, cols]).astype(bf16)
        values[:, cols] = (dot(low, weights[2, :, cols]) + rows[23:24, cols]).astype(bf16)

    for head in range(HEADS):
        soft, cols = attend(queries, keys, head, size, length, size ** (-0.5))
        mixed[:, cols] = dot(soft.astype(bf16), values[:, cols]).astype(bf16)

    @column_loop(width)
    def branch(cols):
        out[:, cols] = (
            stream[:, cols] + dot(mixed[...], weights[3, :, cols]) + rows[24:25, cols]
        )


def attention_heads_backward_kernel(
    count, meta, grad, queries, keys, values, mixed, had, *refs
):
    own, other = refs[:count], refs[count : 2 * count]
    lows, here, there, sums, weights, branch_grad, low_mixed, sems = refs[2 * count :]
    store = store_by_core(meta[count], here, there)
    sums[...] = had[...]
    core, length = meta[count], meta[count + 1]
    width = grad.shape[1]
    size = width // HEADS
    score_scale = size ** (-0.5)
    copies = halves_to_panels(3, 4, own, other, meta, core, weights, sems)
    start_all(copies)
    branch_grad[...] = grad[...].astype(bf16)
    sums[24:25] = column_sum(branch_grad[...].astype(f32))
    put_blocks(store, 0, mixed, branch_grad, here.shape[0])
    wait_all(copies)

    @column_loop(width)
    def through(cols):
        low_mixed[:, cols] = dot_nt(branch_grad[...], weights[0, cols, :]).astype(bf16)

    for head in range(HEADS):
        soft, cols = attend(queries, keys, head, size, length, score_scale)
        low = low_mixed[:, cols]
        soft_grad = dot_nt(low, values[:, cols])
        lows[2, :, cols] = dot_tn(soft.astype(bf16), low).astype(bf16)
        along = jnp.sum(soft_grad * soft, axis=-1, keepdims=True)
        score_grad = (soft * (soft_grad - along)).astype(bf16)
        lows[0, :, cols] = (dot(score_grad, keys[:, cols]) * score_scale).astype(bf16)
        lows[1, :, cols] = (dot_tn(score_grad, queries[:, cols]) * score_scale).astype(bf16)

    sums[22:23] = column_sum(lows[0].astype(f32))
    sums[23:24] = column_sum(lows[2].astype(f32))


def attention_in_backward_kernel(count, meta, grad, stream, normed, lows, rows, had, *refs):
    own, other = refs[:count], refs[count : 2 * count]
    out, here, there, sums, half_low, weights, normed_grad, sems = refs[2 * count :]
    core = meta[count]
    store = store_by_core(core, here, there)
    sums[...] = had[...]
    width = stream.shape[1]
    copies = halves_to_panels(0, 3, own, other, meta, core, weights, sems)
    start_all(copies)
    for i in range(3):
        put_blocks(store, i, normed, lows.at[i], here.shape[0])
    wait_all(copies)

    @column_loop(width)
    def back(cols):
        total = dot_nt(lows[0], weights[0, cols, :])
        total = total + dot_nt(lows[1], weights[1, cols, :])
        normed_grad[:, cols] = total + dot_nt(lows[2], weights[2, cols, :])

    inside, inverse = norm_parts(stream[...])
    pulled = normed_grad[...]
    sums[2:3] = column_sum(pulled * inside)
    sums[3:4] = column_sum(pulled)
    flow = grad[...] + norm_pull(inside, inverse, rows[2:3], pulled)
    out[...] = flow
    half_low[...] = (0.5 * flow).astype(bf16)
    sums[16:17] = column_sum(half_low[...].astype(f32))


def moved(values, steps):
    if steps == 0:
        return values
    tall = values.shape[0]
    spot = lax.broadcasted_iota(jnp.int32, values.shape, 0) + steps
    return jnp.where((spot >= 0) & (spot < tall), pltpu.roll(values, (-steps) % tall, 0), 0.0)


def gated_depth(wide, rows, length):
    value, gate = wide[0], wide[1]
    open_gate = jax.nn.sigmoid(gate)
    inside = lax.broadcasted_iota(jnp.int32, value.shape, 0) < length
    gated = jnp.where(inside, value * open_gate, 0.0)
    depth = rows[27:28] + rows[28:29] * moved(gated, -(KERNEL // 2))
    for tap in range(1, KERNEL):
        depth = depth + rows[28 + tap : 29 + tap] * moved(gated, tap - KERNEL // 2)
    return value, open_gate, inside, gated, depth


def conv_forward_kernel(count, meta, stream, rows, *refs):
    own, other = refs[:count], refs[count : 2 * count]
    out, normed, wide, active, weights, sems = refs[2 * count :]
    core, length = meta[count], meta[count + 1]
    width = stream.shape[1]
    copies = halves_to_panels(4, 7, own, other, meta, core, weights, sems)
    start_all(copies)
    inside, ignored = norm_parts(stream[...])
    normed[...] = (inside * rows[4:5] + rows[5:6]).astype(bf16)
    wait_all(copies)

    @column_loop(width)
    def project(cols):
        for i in range(2):
            wide[i, :, cols] = dot(normed[...], weights[i, :, cols]) + rows[25 + i : 26 + i, cols]

    depth = gated_depth(wide, rows, length)[-1]
    inside, ignored = norm_parts(depth)
    shifted = inside * rows[6:7] + rows[7:8]
    active[...] = (shifted * jax.nn.sigmoid(shifted)).astype(bf16)

    @column_loop(width)
    def branch(cols):
        out[:, cols] = (
            stream[:, cols] + dot(active[...], weights[2, :, cols]) + rows[33:34, cols]
        )


def conv_out_backward_kernel(count, meta, grad, wide, active, rows, had, *refs):
    own, other = refs[:count], refs[count : 2 * count]
    lows, here, there, sums, weights, full, sems = refs[2 * count :]
    core, length = meta[count], meta[count + 1]
    store = store_by_core(core, here, there)
    sums[...] = had[...]
    width = grad.shape[1]
    copies = halves_to_panels(6, 7, own, other, meta, core, weights, sems)
    start_all(copies)
    branch_grad = grad[...].astype(bf16)
    lows[0] = branch_grad
    sums[33:34] = column_sum(branch_grad.astype(f32))
    put_blocks(store, 0, active, lows.at[0], here.shape[0])
    wait_all(copies)

    @column_loop(width)
    def through(cols):
        full[:, cols] = dot_nt(lows[0], weights[0, cols, :])

    value, open_gate, valid, gated, depth = gated_depth(wide, rows, length)
    inside, inverse = norm_parts(depth)
    shifted = inside * rows[6:7] + rows[7:8]
    share = jax.nn.sigmoid(shifted)
    outer_grad = full[...] * share * (1.0 + shifted * (1.0 - share))
    sums[6:7] = column_sum(outer_grad * inside)
    sums[7:8] = column_sum(outer_grad)
    depth_grad = norm_pull(inside, inverse, rows[6:7], outer_grad)
    sums[27:28] = column_sum(depth_grad)
    gated_grad = jnp.zeros_like(depth_grad)
    for tap in range(KERNEL):
        off = tap - KERNEL // 2
        sums[28 + tap : 29 + tap] = column_sum(depth_grad * moved(gated, off))
        gated_grad = gated_grad + rows[28 + tap : 29 + tap] * moved(depth_grad, -off)
    gated_grad = jnp.where(valid, gated_grad, 0.0)
    lows[0] = (gated_grad * open_gate).astype(bf16)
    lows[1] = (gated_grad * value * open_gate * (1.0 - open_gate)).astype(bf16)
    for i in range(2):
        sums[25 + i : 26 + i] = column_sum(lows[i].astype(f32))


def conv_in_backward_kernel(count, meta, grad, stream, normed, lows, rows, had, *refs):
    own, other = refs[:count], refs[count : 2 * count]
    out, here, there, sums, weights, full, sems = refs[2 * count :]
    core = meta[count]
    store = store_by_core(core, here, there)
    sums[...] = had[...]
    width = stream.shape[1]
    copies = halves_to_panels(4, 6, own, other, meta, core, weights, sems)
    start_all(copies)
    for i in range(2):
        put_blocks(store, i, normed, lows.at[i], here.shape[0])
    wait_all(copies)

    @column_loop(width)
    def back(cols):
        full[:, cols] = dot_nt(lows[0], weights[0, cols, :]) + dot_nt(lows[1], weights[1, cols, :])

    inside, inverse = norm_parts(stream[...])
    pulled = full[...]
    sums[4:5] = column_sum(pulled * inside)
    sums[5:6] = column_sum(pulled)
    out[...] = grad[...] + norm_pull(inside, inverse, rows[4:5], pulled)


def pull_kernel(gain, grad, stream, mine, came, rows, had, out, sums):
    sums[...] = had[...]
    inside, inverse = norm_parts(stream[...])
    pulled = mine[...] + came[...].astype(f32)
    sums[gain : gain + 1] = column_sum(pulled * inside)
    sums[gain + 1 : gain + 2] = column_sum(pulled)
    flow = grad[...] + norm_pull(inside, inverse, rows[gain : gain + 1], pulled)
    out[...] = flow.astype(out.dtype)


def pull_call(gain, grad, stream, mine, came, rows, had, dtype):
    return pl.pallas_call(
        functools.partial(pull_kernel, gain),
        out_shape=[
            jax.ShapeDtypeStruct(grad.shape, dtype),
            jax.ShapeDtypeStruct(had.shape, f32),
        ],
        cost_estimate=pl.CostEstimate(
            flops=20 * grad.size, bytes_accessed=16 * grad.size, transcendentals=0
        ),
        compiler_params=pltpu.CompilerParams(vmem_limit_bytes=VMEM_LIMIT),
        name="norm_pull",
    )(grad, stream, mine, came, rows, had)


def turn_kernel(meta, stream, mine, came, cotangent, rows, layer_out, out, half_low, sums):
    last = stream[...] + 0.5 * (mine[...] + came[...].astype(f32) + rows[21:22])
    inside, inverse = norm_parts(last)
    layer_out[...] = (inside * rows[10:11] + rows[11:12]).astype(bf16)
    spot = lax.broadcasted_iota(jnp.int32, last.shape, 0)
    grad = jnp.where(spot < meta[0], cotangent[...].astype(f32), 0.0)
    sums[...] = jnp.zeros_like(sums)
    sums[10:11] = column_sum(grad * inside)
    sums[11:12] = column_sum(grad)
    flow = norm_pull(inside, inverse, rows[10:11], grad)
    out[...] = flow
    half_low[...] = (0.5 * flow).astype(bf16)
    sums[21:22] = column_sum(half_low[...].astype(f32))


def turn_call(length, stream, mine, came, cotangent, rows):
    return pl.pallas_call(
        turn_kernel,
        in_specs=[pl.BlockSpec(memory_space=SMEM)] + [pl.BlockSpec(memory_space=VMEM)] * 5,
        out_shape=[
            jax.ShapeDtypeStruct(stream.shape, bf16),
            jax.ShapeDtypeStruct(stream.shape, f32),
            jax.ShapeDtypeStruct(stream.shape, bf16),
            jax.ShapeDtypeStruct(rows.shape, f32),
        ],
        cost_estimate=pl.CostEstimate(
            flops=30 * stream.size, bytes_accessed=20 * stream.size, transcendentals=0
        ),
        compiler_params=pltpu.CompilerParams(vmem_limit_bytes=VMEM_LIMIT),
        name="turn",
    )(length, stream, mine, came, cotangent, rows)


def panel_call(kernel, name, panels, meta, blocks, own, other, outs, scratch, flops):
    count = len(own)
    width = blocks[0].shape[1]
    return pl.pallas_call(
        functools.partial(kernel, count),
        out_shape=outs,
        in_specs=[pl.BlockSpec(memory_space=SMEM)]
        + [pl.BlockSpec(memory_space=VMEM)] * len(blocks)
        + [pl.BlockSpec(memory_space=ANY)] * (2 * count),
        out_specs=[pl.BlockSpec(memory_space=VMEM)] * len(outs),
        scratch_shapes=[VMEM((panels, width, width), bf16)]
        + scratch
        + [pltpu.SemaphoreType.DMA((2 * count,))],
        compiler_params=pltpu.CompilerParams(vmem_limit_bytes=VMEM_LIMIT),
        cost_estimate=pl.CostEstimate(
            flops=flops,
            bytes_accessed=panels * width * width * 2 + 8 * blocks[0].size * 4,
            transcendentals=2 * blocks[0].size,
        ),
        name=name,
    )(meta, *blocks, *own, *other)


def both_cores(values):
    return jnp.concatenate([values, swap_cores(values)], axis=0)


def on_device(
    outer,
    owners_count,
    frames,
    lengths,
    cotangent,
    panels,
    vectors,
    vector_first,
    vector_second,
    owners,
    basis_left,
    basis_right,
    panel_first,
    panel_second,
    panel_master,
):
    seq_count, seq_len, width = frames.shape
    tokens = seq_count * seq_len
    depth = panels.shape[1]
    half = width // 2
    quarter = width // (2 * outer)
    core = lax.axis_index("c")
    parity = lax.axis_index("o") % 2
    wires = Wires(outer, owners_count)
    shape = jax.ShapeDtypeStruct

    def chip_share(first, side):
        panel = first + 2 * core + side
        ins = lax.dynamic_slice_in_dim(panels, panel, 1, 0)
        outs = lax.dynamic_slice_in_dim(panels, panel + 4, 1, 0)
        return jnp.concatenate([ins, outs], axis=0)

    first = Gather(wires, chip_share(0, parity), 0)
    middle = Gather(wires, lax.dynamic_slice(panels, (8, 0, core * half), (7, depth, half)), 1)
    second = Gather(wires, chip_share(15, parity), 0)
    second_other = [Cell(chip_share(15, 1 - parity))]
    middle_other = []

    class Passing:
        def __init__(self, gather, route, store, start):
            self.gather, self.route, self.store, self.next = gather, route, store, start

        def more(self, most=1):
            sends = []
            while most and self.next < len(self.gather.pieces):
                sends.append((self.gather.pieces[self.next].value, self.route, self.store.append))
                self.next += 1
                most -= 1
            return sends

    to_chip = Passing(second, "chip", second_other, 1)
    to_core = Passing(middle, "core", middle_other, 0)
    slot = wires.slot

    def values(cells):
        return [cell.value for cell in cells]

    def core_rows(first):
        rows = lax.dynamic_slice_in_dim(vectors, first + 2 * core, 2, 0)
        rows = jnp.where(parity == 0, rows, rows[::-1])
        return rows[:, None, :]

    def meta_of(gather, *more):
        return jnp.concatenate([gather.spots(), jnp.stack(more).astype(jnp.int32)])

    low_stream = shape((tokens, width), bf16)
    stream = shape((tokens, width), f32)

    left = Cell(basis_left.astype(bf16))
    right = Cell(basis_right.astype(bf16))
    def exchange(values):
        return lax.ppermute(values, "o", wires.routes["chip"][1])

    def all_four(own, came):
        mine = jnp.concatenate([own, came])
        return jnp.concatenate([mine, swap_cores(mine)])

    def sum_four(mine, away):
        total = mine + swap_cores(away).astype(f32)
        return total[:tokens], total[tokens:].astype(bf16)

    start = Cell(frames.reshape(tokens, width).astype(f32))
    own_first = layer_norm(start.value, vectors[0], vectors[1]).astype(bf16)
    bias_first, bias_second = Cell(core_rows(12)[:1]), Cell(core_rows(17))
    ready = [start, bias_first, bias_second, *second_other]
    far_first = []
    came = slot(first.hop(), [(own_first, "chip", far_first.append)])
    bind(*ready, *came)
    slot(middle.hop(), to_core.more())
    normed = Cell(all_four(own_first, far_first[0].value))
    slot(first.hop())
    bind(normed, *wires.past[-2])
    slot(second.hop(), to_core.more(2))
    slot(first.hop(), to_chip.more())
    came = slot(middle.hop(), to_chip.more())
    bind(left, right, *wires.past[-2])
    came = slot(first.hop())
    while any(first.left):
        came = slot(first.hop())
    slot(second.hop(), to_core.more(2))
    bind(normed, *came)
    slot(middle.hop(), to_chip.more())
    hidden, active, mine, away = ffn_forward_call(
        normed.value, bias_first.value, [values(first.pieces)], meta_of(first, parity)
    )
    own, far = sum_four(mine, away)
    own, far = Cell(own), Cell(far)
    kept_first = (normed.value, hidden, active)
    bind(own, far, *wires.past[-1], *wires.past[-2])
    far_came = []
    slot(second.hop(), to_chip.more(), [(far.value, "chip", far_came.append)])
    slot(middle.hop(), to_chip.more(), to_core.more(2))
    slot(second.hop(), to_chip.more())
    while any(middle.left) or any(second.left):
        slot(middle.hop(), second.hop(), to_chip.more(2), to_core.more(2))
    after_first = Cell(
        start.value + 0.5 * (own.value + far_came[0].value.astype(f32) + vectors[16])
    )
    came = wires.start(to_core.more(2), to_chip.more(), after=wires.past[-1])
    while to_core.next < len(middle.pieces):
        came += slot(to_core.more(2))
    middle_meta = meta_of(middle, core, lengths[0])

    def sides_of(gather, other):
        return [values(gather.pieces)] + ([values(other)] if other else [])

    bind(after_first, *[cell for past in wires.past[-4:] for cell in past])
    after_attn, attn_normed, queries, keys, values_, mixed = panel_call(
        attention_forward_kernel,
        "attention_forward",
        4,
        middle_meta,
        [after_first.value, vectors],
        values(middle.pieces),
        values(middle_other),
        [stream] + [low_stream] * 5,
        [],
        8 * tokens * width * width,
    )
    after_attn = Cell(after_attn)
    bind(after_attn, *came)
    came = []
    while to_chip.next < len(second.pieces):
        came += wires.start(to_chip.more(2), after=[after_attn])
    after_conv, conv_normed, wide, conv_active = panel_call(
        conv_forward_kernel,
        "conv_forward",
        3,
        middle_meta,
        [after_attn.value, vectors],
        values(middle.pieces),
        values(middle_other),
        [stream, low_stream, shape((2, tokens, width), f32), low_stream],
        [],
        6 * tokens * width * width,
    )
    normed = both_cores(layer_norm(after_conv, vectors[8], vectors[9]).astype(bf16))
    hidden, active, mine, away = ffn_forward_call(
        normed, bias_second.value, sides_of(second, second_other), meta_of(second, parity)
    )
    kept_second = (normed, hidden, active)
    layer_out, grad_flow, half_low, sums = turn_call(
        lengths, after_conv, mine, swap_cores(away), cotangent.reshape(tokens, width), vectors
    )

    def ring_of(turn, matrices):
        return Reduce(wires, matrices, depth, turn)

    class Share:
        def __init__(self, here, there):
            self.here, self.there = here, there

        def hop(self):
            return [(self.there, "core", self.take)]

        def take(self, cell):
            self.came = cell

        def total(self):
            return (self.here.astype(f32) + self.came.value.astype(f32)).astype(bf16)

    def trade_cores(block):
        there = lax.dynamic_index_in_dim(block, 1 - core, 0, keepdims=False)
        here = lax.dynamic_index_in_dim(block, core, 0, keepdims=False)
        came = swap_cores(there.astype(bf16)).astype(f32)
        return jnp.where(
            core == 0, jnp.concatenate([here, came]), jnp.concatenate([came, here])
        )

    chip = lax.axis_index("o")
    pairs = outer == 2

    def ffn_backward_out(both_low, gather, other, kept, bias, sums, ways):
        normed, hidden, active = kept
        return ffn_backward_call(
            ffn_out_backward_kernel,
            "ffn_out_backward",
            bias,
            outer,
            ways,
            meta_of(gather, parity, core, chip),
            [hidden, active, both_low, sums],
            sides_of(gather, other),
            [shape(active.shape, bf16), shape(vectors.shape, f32)],
        )

    def ffn_backward_in(low, gather, other, kept, ways):
        return ffn_backward_call(
            ffn_in_backward_kernel,
            "ffn_in_backward",
            0,
            outer,
            ways,
            meta_of(gather, parity, core, chip),
            [kept[0], low],
            sides_of(gather, other),
            [
                shape((kept[0].shape[0] // 2, width), f32),
                shape((kept[0].shape[0] // 2, width), bf16),
            ],
        )

    def middle_call(kernel, name, used, arrays, outs, scratch, flops):
        block_shape = shape((outer, used, width, quarter), bf16)
        return panel_call(
            kernel,
            name,
            used,
            middle_meta,
            arrays,
            values(middle.pieces),
            values(middle_other),
            [outs[0], block_shape, block_shape, shape(vectors.shape, f32), *outs[1:]],
            scratch,
            flops * tokens * width * width,
        )

    class Part:
        def __init__(self, matrices, turn):
            self.turn = turn
            self.ring = None
            if len(matrices) == 3:
                self.chips = ChipSum(wires, here=matrices[0], there=matrices[1:])
            else:
                self.chips = None
                self.ring = ring_of(turn, matrices[0])

        def send(self):
            return self.chips.send() if self.chips is not None and not hasattr(self, "late") else []

        def ready(self):
            if self.ring is None:
                self.ring = ring_of(self.turn, self.chips.total().astype(bf16))

        def hop(self):
            self.ready()
            return self.ring.hop()

        def finish(self):
            if self.chips is not None:
                return []
            self.chips = ChipSum(wires, blocks=self.ring.total())
            self.late = True
            return self.chips.send()

        def total(self):
            if self.chips is None:
                slot(self.finish())
            return self.chips.total() if hasattr(self, "late") else self.ring.total()

    begin = wires.start
    low, sums, *matrices = ffn_backward_out(
        both_cores(half_low), second, second_other, kept_second, 17, sums, False
    )
    second_out = Part(matrices, 0)
    low = Cell(low)
    came = begin(second_out.hop(), beside=[low])
    mine, away, *matrices = ffn_backward_in(low.value, second, second_other, kept_second, pairs)
    mine, away = Cell(mine), Cell(away)
    bind(mine, away, *came)
    second_in = Part(matrices, 1)
    came = begin(second_out.hop(), second_in.send(), beside=[mine, away])
    grad_flow, sums = pull_call(
        8, grad_flow, after_conv, mine.value, swap_cores(away.value), vectors, sums, f32
    )
    lows, here, there, sums = middle_call(
        conv_out_backward_kernel,
        "conv_out_backward",
        1,
        [grad_flow, wide, conv_active, vectors, sums],
        [shape((2, tokens, width), bf16)],
        [VMEM((tokens, width), f32)],
        4,
    )
    lows = Cell(lows)
    conv_out = Share(here, there)
    bind(lows, *came)
    came = begin(second_out.hop(), second_in.send(), conv_out.hop(), beside=[lows])
    flow, here, there, sums = middle_call(
        conv_in_backward_kernel,
        "conv_in_backward",
        2,
        [grad_flow, after_attn.value, conv_normed, lows.value, vectors, sums],
        [stream],
        [VMEM((tokens, width), f32)],
        8,
    )
    flow = Cell(flow)
    conv_in = Share(here, there)
    lows, here, there, sums = middle_call(
        attention_heads_backward_kernel,
        "attention_heads_backward",
        1,
        [flow.value, queries, keys, values_, mixed, sums],
        [shape((3, tokens, width), bf16)],
        [VMEM((tokens, width), bf16), VMEM((tokens, width), bf16)],
        6,
    )
    lows = Cell(lows)
    attn_out = Share(here, there)
    bind(lows, *came)
    second_in.ready()
    came = begin(
        hop_together(second_out.ring, second_in.ring),
        conv_in.hop(),
        attn_out.hop(),
        beside=[lows],
    )
    flow.value, here, there, sums, half_low = middle_call(
        attention_in_backward_kernel,
        "attention_in_backward",
        3,
        [flow.value, after_first.value, attn_normed, lows.value, vectors, sums],
        [stream, low_stream],
        [VMEM((tokens, width), f32)],
        12,
    )
    attn_in = Share(here, there)
    half_low = Cell(half_low)
    bind(half_low, *came)
    conv_total = jnp.concatenate([conv_in.total(), conv_out.total()], axis=1)
    if pairs:
        conv_chips = ChipSum(wires, blocks=conv_total, cuts=[(0, 2), (2, 3)])
    else:
        conv_part = ring_of(0, conv_total)
    far_low = []
    came = begin(
        second_in.hop(),
        attn_in.hop(),
        [(half_low.value, "chip", far_low.append)],
        beside=[half_low],
    )
    both_low = Cell(all_four(half_low.value, far_low[0].value))
    low, sums, *matrices = ffn_backward_out(
        both_low.value, first, [], kept_first, 12, sums, False
    )
    first_out = ring_of(0, matrices[0])
    low = Cell(low)
    bind(low, *came)
    attn_part = ring_of(1, jnp.concatenate([attn_in.total(), attn_out.total()], axis=1))
    conv_sends = conv_chips.send() if pairs else []
    came = begin(hop_together(second_in.ring, attn_part, first_out), conv_sends, beside=[low])
    mine, away, *matrices = ffn_backward_in(low.value, first, [], kept_first, False)
    first_in = ring_of(0, matrices[0])
    own, far = sum_four(mine, away)
    own, far = Cell(own), Cell(far)
    bind(own, far, *came)
    conv_sends = conv_chips.send() if pairs else []
    far_came = []
    came = begin(
        hop_together(second_in.ring, attn_part, first_out, first_in),
        conv_sends,
        [(far.value, "chip", far_came.append)],
        beside=[own],
    )
    bind(*came)
    if pairs:
        conv_part = ring_of(1, conv_chips.total().astype(bf16))
    came = begin(hop_together(attn_part, first_out, first_in, conv_part), second_out.finish())
    frames_grad, sums = pull_call(
        0, flow.value, start.value, own.value, far_came[0].value, vectors, sums, bf16
    )
    frames_grad, sums = Cell(frames_grad), Cell(sums)
    vector_sum = AllSum(wires, sums.value)
    bind(vector_sum.value, frames_grad, *came)
    came = begin(hop_together(attn_part, first_out, first_in, conv_part))
    bind(*came)
    attn_chips = ChipSum(wires, blocks=attn_part.total())
    came = begin(hop_together(first_out, first_in, conv_part), attn_chips.send())
    bind(*came)
    came = begin(hop_together(first_in, conv_part))
    bind(*came)
    conv_total = conv_part.total()
    if not pairs:
        conv_total = ChipSum(wires, blocks=conv_total).total()

    def spread(mine):
        if not pairs:
            big = jnp.zeros((outer, 2, 2, 2) + mine.shape[2:], f32)
            at = (lax.broadcasted_iota(jnp.int32, (1, 1, 2, 2, 1, 1, 1), 2) == core) & (
                lax.broadcasted_iota(jnp.int32, (1, 1, 2, 2, 1, 1, 1), 3) == parity
            )
            big = jnp.where(at, mine[:, :, None, None], big).astype(bf16)
            big = big.reshape((outer * 2,) + big.shape[2:])
            return lax.psum_scatter(big, ("o", "c"), scatter_dimension=0, tiled=True)[0].astype(f32)
        low = trade_blocks(mine.astype(bf16), "o", outer)
        low = trade_blocks(low.transpose(1, 0, 2, 3, 4), "c", 2)
        return low.astype(f32)

    first_sum = spread(jnp.concatenate([first_in.total(), first_out.total()], axis=2))
    first_sum = [first_sum[:, :, kind].reshape(4, depth, quarter) for kind in range(2)]
    early = [trade_cores(second_in.total()), trade_cores(second_out.total()), conv_total]
    early = [Cell(part) for part in early]
    late = [Cell(first_sum[0]), Cell(attn_chips.total()), Cell(first_sum[1])]
    bind(*early, *late)
    panel_grads = jnp.concatenate(
        [
            late[0].value,
            late[2].value,
            late[1].value,
            early[2].value,
            early[0].value,
            early[1].value,
        ],
        axis=0,
    )
    panel_grads = Cell(panel_grads)
    bind(panel_grads, vector_sum.value, frames_grad)
    panel_grads = panel_grads.value

    slot_count = panel_first.shape[1]
    panel_count = owners.shape[0]
    panel_index = jnp.arange(panel_count, dtype=jnp.int32)
    same_owner = owners[:, None] == owners[None, :]
    earlier = panel_index[None, :] < panel_index[:, None]
    slot_of = jnp.sum((same_owner & earlier).astype(jnp.int32), axis=1)
    target = owners * slot_count + slot_of
    slot_hit = target[:, None] == jnp.arange(owners_count * slot_count, dtype=jnp.int32)[None, :]
    source = jnp.sum(slot_hit.astype(jnp.int32) * panel_index[:, None], axis=0)
    filled = jnp.any(slot_hit, axis=0)
    mine = lax.dynamic_slice_in_dim(filled, lax.axis_index("f") * slot_count, slot_count)

    outgoing = pick(panel_grads.astype(bf16), source)
    outgoing = outgoing.reshape(owners_count, slot_count, depth, quarter)
    incoming = lax.all_to_all(outgoing, "f", split_axis=0, concat_axis=0, tiled=True)
    block = lax.axis_index("o") * 2 + core
    left_rows = lax.dynamic_slice_in_dim(left.value, block * quarter, quarter, 1)
    incoming = Cell(incoming)
    last = None
    while vector_sum.todo:
        last = begin(vector_sum.hop())
        if len(vector_sum.todo) == 2:
            bind(incoming, *last)
    vector_grads = vector_sum.total()
    vector_first_new = beta_one * vector_first + (1.0 - beta_one) * vector_grads
    vector_second_new = beta_two * vector_second + (1.0 - beta_two) * vector_grads * vector_grads
    vectors_new = vectors - vector_rate * adam_step(vector_first_new, vector_second_new)
    updated = [Cell(vector_first_new), Cell(vector_second_new), Cell(vectors_new)]

    traded = []
    for s in range(slot_count):
        turned = dot_tn(left.value[s], incoming.value[:, s].reshape(width, quarter)).astype(bf16)
        turned = turned.reshape(outer, 2 * quarter, quarter)
        traded.append(Cell(trade_blocks(turned, "o", outer)))
    backs, firsts, seconds = [], [], []
    for s in range(slot_count):
        if s:
            bind(traded[s], backs[-1])
        turned = traded[s].value.reshape(outer, 2, quarter, quarter).transpose(1, 0, 2, 3)
        turned = trade_blocks(turned, "c", 2)
        turned = turned.transpose(2, 1, 0, 3).reshape(quarter, width)
        rotated = dot(turned, right.value[s])
        first_new = beta_one * panel_first[:, s] + (1.0 - beta_one) * rotated
        second_new = beta_two * panel_second[:, s] + (1.0 - beta_two) * rotated * rotated
        step_values = adam_step(first_new, second_new).astype(bf16)
        back_turn = Cell(dot_nt(step_values, right.value[s]).astype(bf16))
        firsts.append(jnp.where(mine[s], first_new, 0.0))
        seconds.append(jnp.where(mine[s], second_new, 0.0))
        backs.append(back_turn)
    masters = []
    for s in range(slot_count):
        back_turn = gather_blocks(backs[s].value, "o", outer)
        back_turn = gather_blocks(back_turn, "c", 2)
        back_turn = back_turn.transpose(1, 0, 2, 3).reshape(width, width)
        update = dot(left_rows[s], back_turn)
        masters.append(jnp.where(mine[s], panel_master[:, s] - learn_rate * update, 0.0))
    results = list(zip(firsts, seconds, masters))
    first_new, second_new, master_new = [jnp.stack(part, axis=1) for part in zip(*results)]
    return (
        layer_out.reshape(frames.shape),
        frames_grad.value.reshape(frames.shape),
        panel_grads,
        vector_grads,
        *values(updated),
        first_new,
        second_new,
        master_new,
    )


def solution(mesh):
    outer = mesh.shape["dp"] // 2
    owners_count = mesh.shape["fsdp"]
    split = Mesh(mesh.devices.reshape(outer, 2, owners_count), ("o", "c", "f"))
    every = P(("o", "c", "f"), None, None)
    state = P(("o", "c"), "f", None)
    return jax.shard_map(
        functools.partial(on_device, outer, owners_count),
        mesh=split,
        in_specs=(
            every,
            P(("o", "c", "f")),
            every,
            P(None, "f", None),
            P(),
            P(),
            P(),
            P(),
            P("f", None, None),
            P("f", None, None),
            state,
            state,
            state,
        ),
        out_specs=(
            every,
            every,
            P(None, "f", ("o", "c")),
            P(),
            P(),
            P(),
            P(),
            state,
            state,
            state,
        ),
        check_vma=False,
    )
```

```python
import functools

import jax
import jax.numpy as jnp
from jax import lax
from jax.experimental import pallas as pl
from jax.experimental.pallas import tpu as pltpu
from jax.sharding import Mesh
from jax.sharding import PartitionSpec as P

HEADS = 8
KERNEL = 5
STEPS = 4


norm_eps = 1e-05
adam_eps = 1e-08
beta_one = 0.5
beta_two = 0.5
learn_rate = 0.02
vector_rate = 0.25

bf16 = jnp.bfloat16
f32 = jnp.float32
ANY = pl.ANY
VMEM = pltpu.VMEM
SMEM = pltpu.SMEM
SWAP = [(0, 1), (1, 0)]
TILE = 1024
tie = lax.optimization_barrier
VMEM_LIMIT = 56 * 1024 * 1024


def layer_norm(values, gain_row, shift_row):
    centred = values - jnp.mean(values, axis=-1, keepdims=True)
    inverse = lax.rsqrt(jnp.mean(centred * centred, axis=-1, keepdims=True) + norm_eps)
    return centred * inverse * gain_row + shift_row


def norm_backward(residual, gain_row, shift_row, normed_grad):
    ignored, pull_back = jax.vjp(layer_norm, residual, gain_row, shift_row)
    return pull_back(normed_grad)


def adam_step(first_new, second_new):
    return (
        first_new
        / (1.0 - beta_one**STEPS)
        / (jnp.sqrt(second_new / (1.0 - beta_two**STEPS)) + adam_eps)
    )


def token_sum(values):
    return jnp.sum(values, axis=0, dtype=f32)


def dot(left, right):
    return lax.dot_general(left, right, (((1,), (0,)), ((), ())), preferred_element_type=f32)


def dot_nt(left, right):
    return lax.dot_general(left, right, (((1,), (1,)), ((), ())), preferred_element_type=f32)


def dot_tn(left, right):
    return lax.dot_general(left, right, (((0,), (0,)), ((), ())), preferred_element_type=f32)


class Cell:
    def __init__(self, value):
        self.value = value


def bind(*cells):
    for cell, value in zip(cells, tie(tuple(cell.value for cell in cells))):
        cell.value = value


class Wires:
    def __init__(self, outer, owners_count):
        self.outer, self.count = outer, owners_count
        walk = list(range(0, owners_count, 2)) + list(range(owners_count - 1, 0, -2))
        onward = [(walk[i], walk[(i + 1) % owners_count]) for i in range(owners_count)]
        self.routes = {
            "onward": ("f", onward),
            "back": ("f", [(b, a) for a, b in onward]),
            "chip": ("o", [(i, i ^ 1) for i in range(outer)]),
            "core": ("c", SWAP),
        }
        for name, count in (("o", outer), ("f", owners_count)):
            step = 1
            while step < count:
                self.routes[f"{name}{step}"] = (name, [(i, i ^ step) for i in range(count)])
                step *= 2
        index = lax.axis_index("f")
        self.place = jnp.where(index % 2 == 0, index // 2, owners_count - 1 - index // 2)
        self.past = []

    def start(self, *groups, after=(), beside=()):
        sends = [send for group in groups for send in group]
        if sends and not after:
            cells = [Cell(value) for value, route, take in sends]
            bind(*cells, *beside)
            sends = [(cell.value, *send[1:]) for cell, send in zip(cells, sends)]
        came = []
        for value, route, take in sends:
            if after:
                value = tie((value, *[cell.value for cell in after]))[0]
            axis, pairs = self.routes[route]
            came.append(Cell(lax.ppermute(value, axis, pairs)))
            take(came[-1])
        return came

    def slot(self, *groups):
        came = self.start(*groups, after=self.past[-2] if len(self.past) >= 2 else ())
        if came:
            self.past.append(came)
        return came

    def index_at(self, steps):
        spot = (self.place + steps + self.count) % self.count
        return jnp.where(spot < self.count // 2, 2 * spot, 2 * (self.count - 1 - spot) + 1)

    def reach(self, turn):
        half = self.count // 2
        return (half, half - 1) if turn == 0 else (half - 1, half)


class Gather:
    def __init__(self, wires, unit, turn):
        self.wires = wires
        self.left = list(wires.reach(turn))
        self.pieces = [Cell(unit)]
        self.origin = [wires.index_at(0)]
        self.moving = [self.pieces[0], self.pieces[0]]
        self.hops = 0

    def hop(self):
        self.hops += 1
        sends = []
        for way, (route, sign) in enumerate((("onward", -1), ("back", 1))):
            if self.left[way]:
                self.left[way] -= 1
                self.origin.append(self.wires.index_at(sign * self.hops))

                def take(cell, way=way):
                    self.moving[way] = cell
                    self.pieces.append(cell)

                sends.append((self.moving[way].value, route, take))
        return sends

    def spots(self):
        return jnp.stack(self.origin).astype(jnp.int32)


class Reduce:
    def __init__(self, wires, matrices, depth, turn):
        self.wires, self.depth = wires, depth
        self.lead = matrices.shape[:-2]
        self.flat = matrices.reshape((-1,) + matrices.shape[-2:])
        self.left = list(wires.reach(turn))
        self.moving = [None, None]

    def hop(self):
        return hop_together(self)

    def arrived(self, way):
        cell, first = self.moving[way]
        return cell.value[first : first + self.flat.shape[0]]

    def total(self):
        while any(self.left):
            self.wires.slot(self.hop())
        start = self.wires.index_at(0) * self.depth
        own = lax.dynamic_slice_in_dim(self.flat, start, self.depth, 1).astype(f32)
        total = own + self.arrived(0).astype(f32) + self.arrived(1).astype(f32)
        return total.reshape(self.lead + total.shape[1:])


def hop_kernel(plan, counts, starts, *refs):
    n_in = counts[0]
    outs = refs[n_in : n_in + counts[1]]
    came, sems = refs[n_in + counts[1] : -1], refs[-1]
    depth = outs[0].shape[1]
    copies = []
    for i, (way, place, panels, matrix, had, spot) in enumerate(plan):
        row = pl.multiple_of(starts[i] * depth, depth)
        out = outs[way].at[pl.ds(place, panels)]
        copies.append(
            pltpu.make_async_copy(refs[matrix].at[:, pl.ds(row, depth)], out, sems.at[2 * i])
        )
        if had is not None:
            copies.append(
                pltpu.make_async_copy(
                    refs[had].at[pl.ds(spot, panels)],
                    came[way].at[pl.ds(place, panels)],
                    sems.at[2 * i + 1],
                )
            )
    start_all(copies)
    wait_all(copies)
    for way, place, panels, matrix, had, spot in plan:
        if had is not None:
            for p in range(place, place + panels):
                total = outs[way][p].astype(f32) + came[way][p].astype(f32)
                outs[way][p] = total.astype(bf16)


def hop_together(*sums):
    wires, depth = sums[0].wires, sums[0].depth
    columns = sums[0].flat.shape[-1]
    arrays = [part.flat for part in sums]
    cells, plan, starts, sends, sizes = [], [], [], [], []
    for way, (route, sign) in enumerate((("onward", 1), ("back", -1))):
        going = [i for i, part in enumerate(sums) if part.left[way]]
        if not going:
            continue
        place = 0
        places = []
        for i in going:
            part = sums[i]
            had, spot = None, 0
            if part.moving[way] is not None:
                cell, spot = part.moving[way]
                if all(cell is not c for c in cells):
                    cells.append(cell)
                had = len(arrays) + [cell is c for c in cells].index(True)
            panels = part.flat.shape[0]
            plan.append((len(sends), place, panels, i, had, spot))
            starts.append(wires.index_at(sign * part.left[way]))
            part.left[way] -= 1
            places.append((part, place))
            place += panels

        def take(cell, way=way, places=places):
            for part, first in places:
                part.moving[way] = (cell, first)

        sends.append((route, take))
        sizes.append(place)
    if not sends:
        return []
    inputs = arrays + [cell.value for cell in cells]
    messages = pl.pallas_call(
        functools.partial(hop_kernel, tuple(plan), (len(inputs), len(sizes))),
        out_shape=[jax.ShapeDtypeStruct((n, depth, columns), bf16) for n in sizes],
        in_specs=[pl.BlockSpec(memory_space=SMEM)] + [pl.BlockSpec(memory_space=ANY)] * len(inputs),
        out_specs=[pl.BlockSpec(memory_space=VMEM)] * len(sizes),
        scratch_shapes=[VMEM((n, depth, columns), bf16) for n in sizes]
        + [pltpu.SemaphoreType.DMA((2 * len(plan),))],
        compiler_params=pltpu.CompilerParams(vmem_limit_bytes=VMEM_LIMIT),
        cost_estimate=pl.CostEstimate(
            flops=sum(sizes) * depth * columns,
            bytes_accessed=6 * sum(sizes) * depth * columns,
            transcendentals=0,
        ),
        name="hop",
    )(jnp.stack(starts).astype(jnp.int32), *inputs)
    return [(message, *send) for message, send in zip(messages, sends)]


class AllSum:
    def __init__(self, wires, value):
        self.wires, self.value = wires, Cell(value)
        self.todo = ["core"] + [name for name in wires.routes if name[1:].isdigit()]
        self.came = None

    def hop(self):
        if not self.todo:
            return []
        self.settle()
        return [(self.value.value, self.todo.pop(0), self.take)]

    def take(self, cell):
        self.came = cell

    def settle(self):
        if self.came is not None:
            self.value = Cell(self.value.value + self.came.value)
            self.came = None

    def total(self):
        while self.todo:
            self.wires.slot(self.hop())
        self.settle()
        return self.value.value


class ChipSum:
    def __init__(self, wires, blocks=None, here=None, there=None, cuts=None):
        self.wires, self.blocks, self.cuts = wires, blocks, cuts
        if blocks is not None and wires.outer == 2:
            index = lax.axis_index("o")
            here = lax.dynamic_index_in_dim(blocks, index, 0, keepdims=False)
            there = lax.dynamic_index_in_dim(blocks, 1 - index, 0, keepdims=False)
            there = [there] if cuts is None else [there[a:b] for a, b in cuts]
        self.here, self.there, self.came = here, list(there or []), []

    def send(self):
        if not self.there:
            return []
        return [(self.there.pop(0).astype(bf16), "chip", self.came.append)]

    def total(self):
        if self.here is None:
            low = self.blocks.astype(bf16)
            low = lax.psum_scatter(low, "o", scatter_dimension=0, tiled=True)
            return low[0].astype(f32)
        while self.there:
            self.wires.slot(self.send())
        came = [cell.value for cell in self.came]
        if len(came) > 1:
            came = jnp.stack(came) if self.cuts is None else jnp.concatenate(came)
        else:
            came = came[0]
        return self.here.astype(f32) + came.astype(f32)


def swap_cores(values):
    return lax.ppermute(values, "c", SWAP)


def gather_blocks(values, name, count):
    if count == 2:
        index = lax.axis_index(name)
        other = lax.ppermute(values, name, SWAP)
        first = jnp.where(index == 0, values, other)
        second = jnp.where(index == 0, other, values)
        return jnp.stack([first, second])
    return lax.all_gather(values, name)


def trade_blocks(values, name, count):
    if count == 2:
        index = lax.axis_index(name)
        there = lax.dynamic_index_in_dim(values, 1 - index, 0, keepdims=False)
        here = lax.dynamic_index_in_dim(values, index, 0, keepdims=False)
        came = lax.ppermute(there, name, SWAP)
        return jnp.stack([jnp.where(index == 0, here, came), jnp.where(index == 0, came, here)])
    return lax.all_to_all(values, name, split_axis=0, concat_axis=0, tiled=True)


def pick_kernel(slots, source, grads, out, sems):
    copies = [
        pltpu.make_async_copy(grads.at[source[i]], out.at[i], sems.at[i]) for i in range(slots)
    ]
    for copy in copies:
        copy.start()
    for copy in copies:
        copy.wait()


def pick(grads, source):
    slots = source.shape[0]
    return pl.pallas_call(
        functools.partial(pick_kernel, slots),
        out_shape=jax.ShapeDtypeStruct((slots,) + grads.shape[1:], grads.dtype),
        in_specs=[pl.BlockSpec(memory_space=SMEM), pl.BlockSpec(memory_space=ANY)],
        out_specs=pl.BlockSpec(memory_space=VMEM),
        scratch_shapes=[pltpu.SemaphoreType.DMA((slots,))],
        name="pick",
    )(source, grads)


def load_share(sides, spots, first, weights, sems):
    depth = sides[0][0].shape[1]
    copies = []
    for side, pieces in enumerate(sides):
        for i, piece in enumerate(pieces):
            row = pl.multiple_of(spots[i] * depth, depth)
            copies.append(
                pltpu.make_async_copy(
                    piece.at[first],
                    weights.at[len(sides) * first + side, pl.ds(row, depth)],
                    sems.at[first, side, i],
                )
            )
    return copies


def cut_sides(refs, count, halves):
    return [refs[i * count : (i + 1) * count] for i in range(halves)], refs[halves * count :]


def ffn_forward_kernel(count, halves, meta, normed, bias, *refs):
    sides, refs = cut_sides(refs, count, halves)
    hidden, active, branch, away, weights, sems = refs
    tokens, width = branch.shape
    ins = load_share(sides, meta, 0, weights, sems)
    outs = load_share(sides, meta, 1, weights, sems)
    start_all(ins + outs)
    wait_all(ins)
    for p in range(halves):

        @column_loop(width)
        def columns(cols):
            value = dot(normed[...], weights[p, :, cols]) + bias[p, :, cols]
            hidden[p, :, cols] = value
            active[p, :, cols] = (value * jax.nn.sigmoid(value)).astype(bf16)

    wait_all(outs)

    @column_loop(width)
    def out_columns(cols):
        total = dot(active[0], weights[halves, :, cols])
        for p in range(1, halves):
            total = total + dot(active[p], weights[halves + p, :, cols])
        branch[:, cols] = total[:tokens]
        away[:, cols] = total[tokens:].astype(bf16)


def ffn_forward_call(normed, bias, sides, meta):
    tokens, width = normed.shape
    count, halves = len(sides[0]), len(sides)
    return pl.pallas_call(
        functools.partial(ffn_forward_kernel, count, halves),
        out_shape=[
            jax.ShapeDtypeStruct((halves, tokens, width), f32),
            jax.ShapeDtypeStruct((halves, tokens, width), bf16),
            jax.ShapeDtypeStruct((tokens // 2, width), f32),
            jax.ShapeDtypeStruct((tokens // 2, width), bf16),
        ],
        in_specs=[
            pl.BlockSpec(memory_space=SMEM),
            pl.BlockSpec(memory_space=VMEM),
            pl.BlockSpec(memory_space=VMEM),
        ]
        + [pl.BlockSpec(memory_space=ANY)] * (halves * count),
        out_specs=[pl.BlockSpec(memory_space=VMEM)] * 4,
        scratch_shapes=[
            VMEM((2 * halves, width, width), bf16),
            pltpu.SemaphoreType.DMA((2, halves, count)),
        ],
        compiler_params=pltpu.CompilerParams(vmem_limit_bytes=VMEM_LIMIT),
        cost_estimate=pl.CostEstimate(
            flops=4 * halves * tokens * width * width,
            bytes_accessed=8 * width * width + tokens * width * 18,
            transcendentals=halves * tokens * width,
        ),
        name="ffn_forward",
    )(meta, normed, bias, *[piece for pieces in sides for piece in pieces])


def ffn_out_backward_kernel(count, halves, bias, blocks, meta, hidden, active, grad, had, *refs):
    sides, refs = cut_sides(refs, count, halves)
    low, sums, *matrices, weights, sems = refs
    outer, ways = blocks
    width = low.shape[-1]
    parity, core = meta[count], meta[count + 1]
    store = share_store(ways, meta[count + 2], matrices)
    sums[...] = had[...]
    copies = load_share(sides, meta, 1, weights, sems)
    start_all(copies)
    for p in range(halves):
        put_blocks(store, p ^ parity if halves == 2 else p, active.at[p], grad, outer)
    wait_all(copies)
    for p in range(halves):
        row = bias + 2 * core + (p ^ parity)

        @column_loop(width)
        def rows(cols):
            value = hidden[p, :, cols]
            share = jax.nn.sigmoid(value)
            slope = share * (1.0 + value * (1.0 - share))
            part = (dot_nt(grad[...], weights[halves + p, cols, :]) * slope).astype(bf16)
            low[p, :, cols] = part
            sums[pl.ds(row, 1), cols] = jnp.sum(part.astype(f32), axis=0, keepdims=True)


def ffn_in_backward_kernel(count, halves, bias, blocks, meta, normed, low, *refs):
    sides, refs = cut_sides(refs, count, halves)
    normed_grad, away, *matrices, weights, sems = refs
    tokens, width = away.shape
    outer, ways = blocks
    parity = meta[count]
    store = share_store(ways, meta[count + 2], matrices)
    copies = load_share(sides, meta, 0, weights, sems)
    start_all(copies)
    for p in range(halves):
        put_blocks(store, p ^ parity if halves == 2 else p, normed, low.at[p], outer)
    wait_all(copies)

    @column_loop(width)
    def back(cols):
        total = dot_nt(low[0], weights[0, cols, :])
        for p in range(1, halves):
            total = total + dot_nt(low[p], weights[p, cols, :])
        normed_grad[:, cols] = total[:tokens]
        away[:, cols] = total[tokens:].astype(bf16)


def share_store(ways, chip, matrices):
    if ways:
        return store_by_chip(chip, matrices[0], matrices[1:])
    return store_all(matrices[0])


def ffn_backward_call(kernel, name, bias, outer, ways, meta, arrays, sides, outs):
    width = sides[0][0].shape[-1]
    tokens = arrays[0].shape[-2]
    count, halves = len(sides[0]), len(sides)
    quarter = width // (2 * outer)
    if ways:
        part = jax.ShapeDtypeStruct((2, width, quarter), bf16)
        blocks = [jax.ShapeDtypeStruct((2, 2, width, quarter), bf16), part, part]
    else:
        blocks = [jax.ShapeDtypeStruct((outer, 2, halves, width, quarter), bf16)]
    return pl.pallas_call(
        functools.partial(kernel, count, halves, bias, (outer, ways)),
        out_shape=[*outs, *blocks],
        in_specs=[pl.BlockSpec(memory_space=SMEM)]
        + [pl.BlockSpec(memory_space=VMEM)] * len(arrays)
        + [pl.BlockSpec(memory_space=ANY)] * (halves * count),
        out_specs=[pl.BlockSpec(memory_space=VMEM)] * (len(outs) + len(blocks)),
        scratch_shapes=[
            VMEM((2 * halves, width, width), bf16),
            pltpu.SemaphoreType.DMA((2, halves, count)),
        ],
        compiler_params=pltpu.CompilerParams(vmem_limit_bytes=VMEM_LIMIT),
        cost_estimate=pl.CostEstimate(
            flops=4 * halves * tokens * width * width,
            bytes_accessed=8 * width * width + tokens * width * 16,
            transcendentals=tokens * width,
        ),
        name=name,
    )(meta, *arrays, *[piece for pieces in sides for piece in pieces])


def norm_parts(values):
    centred = values - jnp.mean(values, axis=-1, keepdims=True)
    inverse = lax.rsqrt(jnp.mean(centred * centred, axis=-1, keepdims=True) + norm_eps)
    return centred * inverse, inverse


def norm_pull(normed, inverse, gain_row, grad):
    scaled = grad * gain_row
    along = jnp.mean(scaled * normed, axis=-1, keepdims=True)
    return inverse * (scaled - jnp.mean(scaled, axis=-1, keepdims=True) - normed * along)


def column_sum(values):
    return jnp.sum(values, axis=0, keepdims=True)


def halves_to_panels(first, last, own, other, spots, core, weights, sems):
    depth, half = own[0].shape[1:]
    copies = []
    for i in range(len(own)):
        row = pl.multiple_of(spots[i] * depth, depth)
        for side, pieces in ((core, own), (1 - core, other)):
            col = pl.multiple_of(side * half, half)
            copies.append(
                pltpu.make_async_copy(
                    pieces[i].at[pl.ds(first, last - first)],
                    weights.at[pl.ds(0, last - first), pl.ds(row, depth), pl.ds(col, half)],
                    sems.at[len(copies)],
                )
            )
    return copies


def start_all(copies):
    for copy in copies:
        copy.start()


def wait_all(copies):
    for copy in copies:
        copy.wait()


def column_loop(width):
    def run(body):
        for start in range(0, width, TILE):
            body(slice(start, start + TILE))

    return run


def put_blocks(store, panel, left, right, outer):
    quarter = right.shape[-1] // (2 * outer)

    @column_loop(left.shape[1])
    def rows(part):
        value = dot_tn(left[:, part], right[...]).astype(bf16)
        for o in range(outer):
            for c in range(2):
                at = (2 * o + c) * quarter
                store(o, c, panel, part, value[:, at : at + quarter])


def store_all(blocks):
    def store(o, c, panel, part, value):
        blocks[o, c, panel, part, :] = value

    return store


def store_by_core(core, here, there):
    def store(o, c, panel, part, value):
        @pl.when(c == core)
        def kept():
            here[o, panel, part, :] = value

        @pl.when(c != core)
        def sent():
            there[o, panel, part, :] = value

    return store


def store_by_chip(chip, here, there):
    def store(o, c, panel, part, value):
        @pl.when(o == chip)
        def kept():
            here[c, panel, part, :] = value

        @pl.when(o != chip)
        def sent():
            there[c][panel, part, :] = value

    return store


def attend(queries, keys, head, size, length, score_scale):
    cols = slice(head * size, (head + 1) * size)
    scores = dot_nt(queries[:, cols], keys[:, cols]) * score_scale
    spot = lax.broadcasted_iota(jnp.int32, scores.shape, 1)
    scores = jnp.where(spot < length, scores, -1000000000.0)
    peak = jnp.max(scores, axis=-1, keepdims=True)
    raised = jnp.exp(scores - peak)
    return raised * (1.0 / jnp.sum(raised, axis=-1, keepdims=True)), cols


def attention_forward_kernel(count, meta, stream, rows, *refs):
    own, other = refs[:count], refs[count : 2 * count]
    out, normed, queries, keys, values, mixed, weights, sems = refs[2 * count :]
    core, length = meta[count], meta[count + 1]
    width = stream.shape[1]
    size = width // HEADS
    copies = halves_to_panels(0, 4, own, other, meta, core, weights, sems)
    start_all(copies)
    inside, ignored = norm_parts(stream[...])
    normed[...] = (inside * rows[2:3] + rows[3:4]).astype(bf16)
    wait_all(copies)

    @column_loop(width)
    def project(cols):
        low = normed[...]
        queries[:, cols] = (dot(low, weights[0, :, cols]) + rows[22:23, cols]).astype(bf16)
        keys[:, cols] = dot(low, weights[1, :, cols]).astype(bf16)
        values[:, cols] = (dot(low, weights[2, :, cols]) + rows[23:24, cols]).astype(bf16)

    for head in range(HEADS):
        soft, cols = attend(queries, keys, head, size, length, size ** (-0.5))
        mixed[:, cols] = dot(soft.astype(bf16), values[:, cols]).astype(bf16)

    @column_loop(width)
    def branch(cols):
        out[:, cols] = (
            stream[:, cols] + dot(mixed[...], weights[3, :, cols]) + rows[24:25, cols]
        )


def attention_heads_backward_kernel(
    count, meta, grad, queries, keys, values, mixed, had, *refs
):
    own, other = refs[:count], refs[count : 2 * count]
    lows, here, there, sums, weights, branch_grad, low_mixed, sems = refs[2 * count :]
    store = store_by_core(meta[count], here, there)
    sums[...] = had[...]
    core, length = meta[count], meta[count + 1]
    width = grad.shape[1]
    size = width // HEADS
    score_scale = size ** (-0.5)
    copies = halves_to_panels(3, 4, own, other, meta, core, weights, sems)
    start_all(copies)
    branch_grad[...] = grad[...].astype(bf16)
    sums[24:25] = column_sum(branch_grad[...].astype(f32))
    put_blocks(store, 0, mixed, branch_grad, here.shape[0])
    wait_all(copies)

    @column_loop(width)
    def through(cols):
        low_mixed[:, cols] = dot_nt(branch_grad[...], weights[0, cols, :]).astype(bf16)

    for head in range(HEADS):
        soft, cols = attend(queries, keys, head, size, length, score_scale)
        low = low_mixed[:, cols]
        soft_grad = dot_nt(low, values[:, cols])
        lows[2, :, cols] = dot_tn(soft.astype(bf16), low).astype(bf16)
        along = jnp.sum(soft_grad * soft, axis=-1, keepdims=True)
        score_grad = (soft * (soft_grad - along)).astype(bf16)
        lows[0, :, cols] = (dot(score_grad, keys[:, cols]) * score_scale).astype(bf16)
        lows[1, :, cols] = (dot_tn(score_grad, queries[:, cols]) * score_scale).astype(bf16)

    sums[22:23] = column_sum(lows[0].astype(f32))
    sums[23:24] = column_sum(lows[2].astype(f32))


def attention_in_backward_kernel(count, meta, grad, stream, normed, lows, rows, had, *refs):
    own, other = refs[:count], refs[count : 2 * count]
    out, here, there, sums, half_low, weights, normed_grad, sems = refs[2 * count :]
    core = meta[count]
    store = store_by_core(core, here, there)
    sums[...] = had[...]
    width = stream.shape[1]
    copies = halves_to_panels(0, 3, own, other, meta, core, weights, sems)
    start_all(copies)
    for i in range(3):
        put_blocks(store, i, normed, lows.at[i], here.shape[0])
    wait_all(copies)

    @column_loop(width)
    def back(cols):
        total = dot_nt(lows[0], weights[0, cols, :])
        total = total + dot_nt(lows[1], weights[1, cols, :])
        normed_grad[:, cols] = total + dot_nt(lows[2], weights[2, cols, :])

    inside, inverse = norm_parts(stream[...])
    pulled = normed_grad[...]
    sums[2:3] = column_sum(pulled * inside)
    sums[3:4] = column_sum(pulled)
    flow = grad[...] + norm_pull(inside, inverse, rows[2:3], pulled)
    out[...] = flow
    half_low[...] = (0.5 * flow).astype(bf16)
    sums[16:17] = column_sum(half_low[...].astype(f32))


def moved(values, steps):
    if steps == 0:
        return values
    tall = values.shape[0]
    spot = lax.broadcasted_iota(jnp.int32, values.shape, 0) + steps
    return jnp.where((spot >= 0) & (spot < tall), pltpu.roll(values, (-steps) % tall, 0), 0.0)


def gated_depth(wide, rows, length):
    value, gate = wide[0], wide[1]
    open_gate = jax.nn.sigmoid(gate)
    inside = lax.broadcasted_iota(jnp.int32, value.shape, 0) < length
    gated = jnp.where(inside, value * open_gate, 0.0)
    depth = rows[27:28] + rows[28:29] * moved(gated, -(KERNEL // 2))
    for tap in range(1, KERNEL):
        depth = depth + rows[28 + tap : 29 + tap] * moved(gated, tap - KERNEL // 2)
    return value, open_gate, inside, gated, depth


def conv_forward_kernel(count, meta, stream, rows, *refs):
    own, other = refs[:count], refs[count : 2 * count]
    out, normed, wide, active, next_low, weights, sems = refs[2 * count :]
    core, length = meta[count], meta[count + 1]
    width = stream.shape[1]
    copies = halves_to_panels(4, 7, own, other, meta, core, weights, sems)
    start_all(copies)
    inside, ignored = norm_parts(stream[...])
    normed[...] = (inside * rows[4:5] + rows[5:6]).astype(bf16)
    wait_all(copies)

    @column_loop(width)
    def project(cols):
        for i in range(2):
            wide[i, :, cols] = dot(normed[...], weights[i, :, cols]) + rows[25 + i : 26 + i, cols]

    depth = gated_depth(wide, rows, length)[-1]
    inside, ignored = norm_parts(depth)
    shifted = inside * rows[6:7] + rows[7:8]
    active[...] = (shifted * jax.nn.sigmoid(shifted)).astype(bf16)

    @column_loop(width)
    def branch(cols):
        out[:, cols] = (
            stream[:, cols] + dot(active[...], weights[2, :, cols]) + rows[33:34, cols]
        )

    inside, ignored = norm_parts(out[...])
    next_low[...] = (inside * rows[8:9] + rows[9:10]).astype(bf16)


def conv_out_backward_kernel(count, meta, grad, wide, active, rows, had, *refs):
    own, other = refs[:count], refs[count : 2 * count]
    lows, here, there, sums, weights, full, sems = refs[2 * count :]
    core, length = meta[count], meta[count + 1]
    store = store_by_core(core, here, there)
    sums[...] = had[...]
    width = grad.shape[1]
    copies = halves_to_panels(6, 7, own, other, meta, core, weights, sems)
    start_all(copies)
    branch_grad = grad[...].astype(bf16)
    lows[0] = branch_grad
    sums[33:34] = column_sum(branch_grad.astype(f32))
    put_blocks(store, 0, active, lows.at[0], here.shape[0])
    wait_all(copies)

    @column_loop(width)
    def through(cols):
        full[:, cols] = dot_nt(lows[0], weights[0, cols, :])

    value, open_gate, valid, gated, depth = gated_depth(wide, rows, length)
    inside, inverse = norm_parts(depth)
    shifted = inside * rows[6:7] + rows[7:8]
    share = jax.nn.sigmoid(shifted)
    outer_grad = full[...] * share * (1.0 + shifted * (1.0 - share))
    sums[6:7] = column_sum(outer_grad * inside)
    sums[7:8] = column_sum(outer_grad)
    depth_grad = norm_pull(inside, inverse, rows[6:7], outer_grad)
    sums[27:28] = column_sum(depth_grad)
    gated_grad = jnp.zeros_like(depth_grad)
    for tap in range(KERNEL):
        off = tap - KERNEL // 2
        sums[28 + tap : 29 + tap] = column_sum(depth_grad * moved(gated, off))
        gated_grad = gated_grad + rows[28 + tap : 29 + tap] * moved(depth_grad, -off)
    gated_grad = jnp.where(valid, gated_grad, 0.0)
    lows[0] = (gated_grad * open_gate).astype(bf16)
    lows[1] = (gated_grad * value * open_gate * (1.0 - open_gate)).astype(bf16)
    for i in range(2):
        sums[25 + i : 26 + i] = column_sum(lows[i].astype(f32))


def conv_in_backward_kernel(count, meta, grad, stream, normed, lows, rows, had, *refs):
    own, other = refs[:count], refs[count : 2 * count]
    out, here, there, sums, weights, full, sems = refs[2 * count :]
    core = meta[count]
    store = store_by_core(core, here, there)
    sums[...] = had[...]
    width = stream.shape[1]
    copies = halves_to_panels(4, 6, own, other, meta, core, weights, sems)
    start_all(copies)
    for i in range(2):
        put_blocks(store, i, normed, lows.at[i], here.shape[0])
    wait_all(copies)

    @column_loop(width)
    def back(cols):
        full[:, cols] = dot_nt(lows[0], weights[0, cols, :]) + dot_nt(lows[1], weights[1, cols, :])

    inside, inverse = norm_parts(stream[...])
    pulled = full[...]
    sums[4:5] = column_sum(pulled * inside)
    sums[5:6] = column_sum(pulled)
    out[...] = grad[...] + norm_pull(inside, inverse, rows[4:5], pulled)


def pull_kernel(gain, grad, stream, mine, came, rows, had, out, sums):
    sums[...] = had[...]
    inside, inverse = norm_parts(stream[...])
    pulled = mine[...] + came[...].astype(f32)
    sums[gain : gain + 1] = column_sum(pulled * inside)
    sums[gain + 1 : gain + 2] = column_sum(pulled)
    flow = grad[...] + norm_pull(inside, inverse, rows[gain : gain + 1], pulled)
    out[...] = flow.astype(out.dtype)


def pull_call(gain, grad, stream, mine, came, rows, had, dtype):
    return pl.pallas_call(
        functools.partial(pull_kernel, gain),
        out_shape=[
            jax.ShapeDtypeStruct(grad.shape, dtype),
            jax.ShapeDtypeStruct(had.shape, f32),
        ],
        cost_estimate=pl.CostEstimate(
            flops=20 * grad.size, bytes_accessed=16 * grad.size, transcendentals=0
        ),
        compiler_params=pltpu.CompilerParams(vmem_limit_bytes=VMEM_LIMIT),
        name="norm_pull",
    )(grad, stream, mine, came, rows, had)


def turn_kernel(meta, stream, mine, came, cotangent, rows, layer_out, out, half_low, sums):
    last = stream[...] + 0.5 * (mine[...] + came[...].astype(f32) + rows[21:22])
    inside, inverse = norm_parts(last)
    layer_out[...] = (inside * rows[10:11] + rows[11:12]).astype(bf16)
    spot = lax.broadcasted_iota(jnp.int32, last.shape, 0)
    grad = jnp.where(spot < meta[0], cotangent[...].astype(f32), 0.0)
    sums[...] = jnp.zeros_like(sums)
    sums[10:11] = column_sum(grad * inside)
    sums[11:12] = column_sum(grad)
    flow = norm_pull(inside, inverse, rows[10:11], grad)
    out[...] = flow
    half_low[...] = (0.5 * flow).astype(bf16)
    sums[21:22] = column_sum(half_low[...].astype(f32))


def turn_call(length, stream, mine, came, cotangent, rows):
    return pl.pallas_call(
        turn_kernel,
        in_specs=[pl.BlockSpec(memory_space=SMEM)] + [pl.BlockSpec(memory_space=VMEM)] * 5,
        out_shape=[
            jax.ShapeDtypeStruct(stream.shape, bf16),
            jax.ShapeDtypeStruct(stream.shape, f32),
            jax.ShapeDtypeStruct(stream.shape, bf16),
            jax.ShapeDtypeStruct(rows.shape, f32),
        ],
        cost_estimate=pl.CostEstimate(
            flops=30 * stream.size, bytes_accessed=20 * stream.size, transcendentals=0
        ),
        compiler_params=pltpu.CompilerParams(vmem_limit_bytes=VMEM_LIMIT),
        name="turn",
    )(length, stream, mine, came, cotangent, rows)


def panel_call(kernel, name, panels, meta, blocks, own, other, outs, scratch, flops):
    count = len(own)
    width = blocks[0].shape[1]
    return pl.pallas_call(
        functools.partial(kernel, count),
        out_shape=outs,
        in_specs=[pl.BlockSpec(memory_space=SMEM)]
        + [pl.BlockSpec(memory_space=VMEM)] * len(blocks)
        + [pl.BlockSpec(memory_space=ANY)] * (2 * count),
        out_specs=[pl.BlockSpec(memory_space=VMEM)] * len(outs),
        scratch_shapes=[VMEM((panels, width, width), bf16)]
        + scratch
        + [pltpu.SemaphoreType.DMA((2 * count,))],
        compiler_params=pltpu.CompilerParams(vmem_limit_bytes=VMEM_LIMIT),
        cost_estimate=pl.CostEstimate(
            flops=flops,
            bytes_accessed=panels * width * width * 2 + 8 * blocks[0].size * 4,
            transcendentals=2 * blocks[0].size,
        ),
        name=name,
    )(meta, *blocks, *own, *other)


def both_cores(values):
    return jnp.concatenate([values, swap_cores(values)], axis=0)


def on_device(
    outer,
    owners_count,
    frames,
    lengths,
    cotangent,
    panels,
    vectors,
    vector_first,
    vector_second,
    owners,
    basis_left,
    basis_right,
    panel_first,
    panel_second,
    panel_master,
):
    seq_count, seq_len, width = frames.shape
    tokens = seq_count * seq_len
    depth = panels.shape[1]
    half = width // 2
    quarter = width // (2 * outer)
    core = lax.axis_index("c")
    parity = lax.axis_index("o") % 2
    wires = Wires(outer, owners_count)
    shape = jax.ShapeDtypeStruct

    def chip_share(first, side):
        panel = first + 2 * core + side
        ins = lax.dynamic_slice_in_dim(panels, panel, 1, 0)
        outs = lax.dynamic_slice_in_dim(panels, panel + 4, 1, 0)
        return jnp.concatenate([ins, outs], axis=0)

    first = Gather(wires, chip_share(0, parity), 0)
    middle = Gather(wires, lax.dynamic_slice(panels, (8, 0, core * half), (7, depth, half)), 1)
    second = Gather(wires, chip_share(15, parity), 0)
    second_other = [Cell(chip_share(15, 1 - parity))]
    middle_other = []

    class Passing:
        def __init__(self, gather, route, store, start):
            self.gather, self.route, self.store, self.next = gather, route, store, start

        def more(self, most=1):
            sends = []
            while most and self.next < len(self.gather.pieces):
                sends.append((self.gather.pieces[self.next].value, self.route, self.store.append))
                self.next += 1
                most -= 1
            return sends

    to_chip = Passing(second, "chip", second_other, 1)
    to_core = Passing(middle, "core", middle_other, 0)
    slot = wires.slot

    def values(cells):
        return [cell.value for cell in cells]

    def core_rows(first):
        rows = lax.dynamic_slice_in_dim(vectors, first + 2 * core, 2, 0)
        rows = jnp.where(parity == 0, rows, rows[::-1])
        return rows[:, None, :]

    def meta_of(gather, *more):
        return jnp.concatenate([gather.spots(), jnp.stack(more).astype(jnp.int32)])

    low_stream = shape((tokens, width), bf16)
    stream = shape((tokens, width), f32)

    left = Cell(basis_left.astype(bf16))
    right = Cell(basis_right.astype(bf16))
    def exchange(values):
        return lax.ppermute(values, "o", wires.routes["chip"][1])

    def all_four(own, came):
        mine = jnp.concatenate([own, came])
        return jnp.concatenate([mine, swap_cores(mine)])

    def sum_four(mine, away):
        total = mine + swap_cores(away).astype(f32)
        return total[:tokens], total[tokens:].astype(bf16)

    start = Cell(frames.reshape(tokens, width).astype(f32))
    own_first = layer_norm(start.value, vectors[0], vectors[1]).astype(bf16)
    bias_first, bias_second = Cell(core_rows(12)[:1]), Cell(core_rows(17))
    ready = [start, bias_first, bias_second, *second_other]
    far_first = []
    came = slot(first.hop(), [(own_first, "chip", far_first.append)])
    bind(*ready, *came)
    slot(middle.hop(), to_core.more())
    normed = Cell(all_four(own_first, far_first[0].value))
    slot(first.hop())
    bind(normed, left, right, *wires.past[-2])
    slot(second.hop(), to_core.more(2))
    slot(first.hop(), to_chip.more())
    slot(middle.hop(), to_chip.more())
    came = slot(first.hop())
    while any(first.left):
        came = slot(first.hop())
    slot(second.hop(), to_core.more(2))
    bind(normed, *came)
    slot(middle.hop(), to_chip.more())
    hidden, active, mine, away = ffn_forward_call(
        normed.value, bias_first.value, [values(first.pieces)], meta_of(first, parity)
    )
    own, far = sum_four(mine, away)
    own, far = Cell(own), Cell(far)
    kept_first = (normed.value, hidden, active)
    bind(own, far, *wires.past[-1], *wires.past[-2])
    far_came = []
    slot(second.hop(), to_chip.more(), [(far.value, "chip", far_came.append)])
    slot(middle.hop(), to_chip.more(), to_core.more(2))
    slot(second.hop(), to_chip.more())
    while any(middle.left) or any(second.left):
        slot(middle.hop(), second.hop(), to_chip.more(2), to_core.more(2))
    after_first = Cell(
        start.value + 0.5 * (own.value + far_came[0].value.astype(f32) + vectors[16])
    )
    came = wires.start(to_core.more(2), to_chip.more(), after=wires.past[-1])
    while to_core.next < len(middle.pieces):
        came += slot(to_core.more(2))
    middle_meta = meta_of(middle, core, lengths[0])

    def sides_of(gather, other):
        return [values(gather.pieces)] + ([values(other)] if other else [])

    bind(after_first, *[cell for past in wires.past[-4:] for cell in past])
    after_attn, attn_normed, queries, keys, values_, mixed = panel_call(
        attention_forward_kernel,
        "attention_forward",
        4,
        middle_meta,
        [after_first.value, vectors],
        values(middle.pieces),
        values(middle_other),
        [stream] + [low_stream] * 5,
        [],
        8 * tokens * width * width,
    )
    after_attn = Cell(after_attn)
    bind(after_attn, *came)
    came = []
    while to_chip.next < len(second.pieces):
        came += wires.start(to_chip.more(2), after=[after_attn])
    after_conv, conv_normed, wide, conv_active, second_low = panel_call(
        conv_forward_kernel,
        "conv_forward",
        3,
        middle_meta,
        [after_attn.value, vectors],
        values(middle.pieces),
        values(middle_other),
        [stream, low_stream, shape((2, tokens, width), f32), low_stream, low_stream],
        [],
        6 * tokens * width * width,
    )
    normed = both_cores(second_low)
    hidden, active, mine, away = ffn_forward_call(
        normed, bias_second.value, sides_of(second, second_other), meta_of(second, parity)
    )
    kept_second = (normed, hidden, active)
    layer_out, grad_flow, half_low, sums = turn_call(
        lengths, after_conv, mine, swap_cores(away), cotangent.reshape(tokens, width), vectors
    )

    def ring_of(turn, matrices):
        return Reduce(wires, matrices, depth, turn)

    class Share:
        def __init__(self, here, there):
            self.here, self.there = here, there

        def hop(self):
            return [(self.there, "core", self.take)]

        def take(self, cell):
            self.came = cell

        def total(self):
            return (self.here.astype(f32) + self.came.value.astype(f32)).astype(bf16)

    def trade_cores(block):
        there = lax.dynamic_index_in_dim(block, 1 - core, 0, keepdims=False)
        here = lax.dynamic_index_in_dim(block, core, 0, keepdims=False)
        came = swap_cores(there.astype(bf16)).astype(f32)
        return jnp.where(
            core == 0, jnp.concatenate([here, came]), jnp.concatenate([came, here])
        )

    chip = lax.axis_index("o")
    pairs = outer == 2

    def ffn_backward_out(both_low, gather, other, kept, bias, sums, ways):
        normed, hidden, active = kept
        return ffn_backward_call(
            ffn_out_backward_kernel,
            "ffn_out_backward",
            bias,
            outer,
            ways,
            meta_of(gather, parity, core, chip),
            [hidden, active, both_low, sums],
            sides_of(gather, other),
            [shape(active.shape, bf16), shape(vectors.shape, f32)],
        )

    def ffn_backward_in(low, gather, other, kept, ways):
        return ffn_backward_call(
            ffn_in_backward_kernel,
            "ffn_in_backward",
            0,
            outer,
            ways,
            meta_of(gather, parity, core, chip),
            [kept[0], low],
            sides_of(gather, other),
            [
                shape((kept[0].shape[0] // 2, width), f32),
                shape((kept[0].shape[0] // 2, width), bf16),
            ],
        )

    def middle_call(kernel, name, used, arrays, outs, scratch, flops):
        block_shape = shape((outer, used, width, quarter), bf16)
        return panel_call(
            kernel,
            name,
            used,
            middle_meta,
            arrays,
            values(middle.pieces),
            values(middle_other),
            [outs[0], block_shape, block_shape, shape(vectors.shape, f32), *outs[1:]],
            scratch,
            flops * tokens * width * width,
        )

    class Part:
        def __init__(self, matrices, turn):
            self.turn = turn
            self.ring = None
            if len(matrices) == 3:
                self.chips = ChipSum(wires, here=matrices[0], there=matrices[1:])
            else:
                self.chips = None
                self.ring = ring_of(turn, matrices[0])

        def send(self):
            return self.chips.send() if self.chips is not None and not hasattr(self, "late") else []

        def ready(self):
            if self.ring is None:
                self.ring = ring_of(self.turn, self.chips.total().astype(bf16))

        def hop(self):
            self.ready()
            return self.ring.hop()

        def finish(self):
            if self.chips is not None:
                return []
            self.chips = ChipSum(wires, blocks=self.ring.total())
            self.late = True
            return self.chips.send()

        def total(self):
            if self.chips is None:
                slot(self.finish())
            return self.chips.total() if hasattr(self, "late") else self.ring.total()

    begin = wires.start
    low, sums, *matrices = ffn_backward_out(
        both_cores(half_low), second, second_other, kept_second, 17, sums, False
    )
    second_out = Part(matrices, 0)
    low = Cell(low)
    came = begin(second_out.hop(), beside=[low])
    mine, away, *matrices = ffn_backward_in(low.value, second, second_other, kept_second, pairs)
    mine, away = Cell(mine), Cell(away)
    bind(mine, away, *came)
    second_in = Part(matrices, 1)
    came = begin(second_out.hop(), second_in.send(), beside=[mine, away])
    grad_flow, sums = pull_call(
        8, grad_flow, after_conv, mine.value, swap_cores(away.value), vectors, sums, f32
    )
    lows, here, there, sums = middle_call(
        conv_out_backward_kernel,
        "conv_out_backward",
        1,
        [grad_flow, wide, conv_active, vectors, sums],
        [shape((2, tokens, width), bf16)],
        [VMEM((tokens, width), f32)],
        4,
    )
    lows = Cell(lows)
    conv_out = Share(here, there)
    bind(lows, *came)
    came = begin(second_out.hop(), second_in.send(), conv_out.hop(), beside=[lows])
    flow, here, there, sums = middle_call(
        conv_in_backward_kernel,
        "conv_in_backward",
        2,
        [grad_flow, after_attn.value, conv_normed, lows.value, vectors, sums],
        [stream],
        [VMEM((tokens, width), f32)],
        8,
    )
    flow = Cell(flow)
    conv_in = Share(here, there)
    lows, here, there, sums = middle_call(
        attention_heads_backward_kernel,
        "attention_heads_backward",
        1,
        [flow.value, queries, keys, values_, mixed, sums],
        [shape((3, tokens, width), bf16)],
        [VMEM((tokens, width), bf16), VMEM((tokens, width), bf16)],
        6,
    )
    lows = Cell(lows)
    attn_out = Share(here, there)
    bind(lows, *came)
    second_in.ready()
    came = begin(
        hop_together(second_out.ring, second_in.ring),
        conv_in.hop(),
        attn_out.hop(),
        beside=[lows],
    )
    flow.value, here, there, sums, half_low = middle_call(
        attention_in_backward_kernel,
        "attention_in_backward",
        3,
        [flow.value, after_first.value, attn_normed, lows.value, vectors, sums],
        [stream, low_stream],
        [VMEM((tokens, width), f32)],
        12,
    )
    attn_in = Share(here, there)
    half_low = Cell(half_low)
    bind(half_low, *came)
    conv_total = jnp.concatenate([conv_in.total(), conv_out.total()], axis=1)
    if pairs:
        conv_chips = ChipSum(wires, blocks=conv_total, cuts=[(0, 1), (1, 3)])
    else:
        conv_part = ring_of(0, conv_total)
    far_low = []
    came = begin(
        second_in.hop(),
        attn_in.hop(),
        [(half_low.value, "chip", far_low.append)],
        beside=[half_low],
    )
    both_low = Cell(all_four(half_low.value, far_low[0].value))
    if pairs:
        came += begin(conv_chips.send(), beside=[both_low])
    low, sums, *matrices = ffn_backward_out(
        both_low.value, first, [], kept_first, 12, sums, False
    )
    first_out = ring_of(0, matrices[0])
    low = Cell(low)
    bind(low, *came)
    attn_part = ring_of(1, jnp.concatenate([attn_in.total(), attn_out.total()], axis=1))
    conv_sends = conv_chips.send() if pairs else []
    came = begin(hop_together(second_in.ring, attn_part, first_out), conv_sends, beside=[low])
    mine, away, *matrices = ffn_backward_in(low.value, first, [], kept_first, False)
    first_in = ring_of(0, matrices[0])
    mine, away = Cell(mine), Cell(away)
    bind(mine, away, *came)
    if pairs:
        conv_part = ring_of(1, conv_chips.total().astype(bf16))
    came = begin(
        hop_together(second_in.ring, attn_part, first_out, first_in, conv_part),
        beside=[mine, away],
    )
    own, far = sum_four(mine.value, away.value)
    own, far_came = Cell(own), []
    came += begin([(far, "chip", far_came.append)], beside=[own])
    bind(*came)
    came = begin(hop_together(attn_part, first_out, first_in, conv_part), second_out.finish())
    frames_grad, sums = pull_call(
        0, flow.value, start.value, own.value, far_came[0].value, vectors, sums, bf16
    )
    frames_grad, sums = Cell(frames_grad), Cell(sums)
    vector_sum = AllSum(wires, sums.value)
    bind(vector_sum.value, frames_grad, *came)
    came = begin(hop_together(attn_part, first_out, first_in, conv_part))
    bind(*came)
    attn_chips = ChipSum(wires, blocks=attn_part.total())
    came = begin(hop_together(first_out, first_in, conv_part), attn_chips.send())
    bind(*came)
    conv_total = conv_part.total()
    if not pairs:
        conv_total = ChipSum(wires, blocks=conv_total).total()

    def spread(mine):
        if not pairs:
            big = jnp.zeros((outer, 2, 2, 2) + mine.shape[2:], f32)
            at = (lax.broadcasted_iota(jnp.int32, (1, 1, 2, 2, 1, 1, 1), 2) == core) & (
                lax.broadcasted_iota(jnp.int32, (1, 1, 2, 2, 1, 1, 1), 3) == parity
            )
            big = jnp.where(at, mine[:, :, None, None], big).astype(bf16)
            big = big.reshape((outer * 2,) + big.shape[2:])
            return lax.psum_scatter(big, ("o", "c"), scatter_dimension=0, tiled=True)[0].astype(f32)
        low = trade_blocks(mine.astype(bf16), "o", outer)
        low = trade_blocks(low.transpose(1, 0, 2, 3, 4), "c", 2)
        return low.astype(f32)

    first_sum = spread(jnp.concatenate([first_in.total(), first_out.total()], axis=2))
    first_sum = [first_sum[:, :, kind].reshape(4, depth, quarter) for kind in range(2)]
    early = [trade_cores(second_in.total()), trade_cores(second_out.total()), conv_total]
    early = [Cell(part) for part in early]
    late = [Cell(first_sum[0]), Cell(attn_chips.total()), Cell(first_sum[1])]
    bind(*early, *late)
    panel_grads = jnp.concatenate(
        [
            late[0].value,
            late[2].value,
            late[1].value,
            early[2].value,
            early[0].value,
            early[1].value,
        ],
        axis=0,
    )
    panel_grads = Cell(panel_grads)
    bind(panel_grads, vector_sum.value, frames_grad)
    panel_grads = panel_grads.value

    slot_count = panel_first.shape[1]
    panel_count = owners.shape[0]
    panel_index = jnp.arange(panel_count, dtype=jnp.int32)
    same_owner = owners[:, None] == owners[None, :]
    earlier = panel_index[None, :] < panel_index[:, None]
    slot_of = jnp.sum((same_owner & earlier).astype(jnp.int32), axis=1)
    target = owners * slot_count + slot_of
    slot_hit = target[:, None] == jnp.arange(owners_count * slot_count, dtype=jnp.int32)[None, :]
    source = jnp.sum(slot_hit.astype(jnp.int32) * panel_index[:, None], axis=0)
    filled = jnp.any(slot_hit, axis=0)
    mine = lax.dynamic_slice_in_dim(filled, lax.axis_index("f") * slot_count, slot_count)

    outgoing = pick(panel_grads.astype(bf16), source)
    outgoing = outgoing.reshape(owners_count, slot_count, depth, quarter)
    incoming = lax.all_to_all(outgoing, "f", split_axis=0, concat_axis=0, tiled=True)
    block = lax.axis_index("o") * 2 + core
    left_rows = lax.dynamic_slice_in_dim(left.value, block * quarter, quarter, 1)
    incoming = Cell(incoming)
    last = None
    while vector_sum.todo:
        last = begin(vector_sum.hop())
        if len(vector_sum.todo) == 2:
            bind(incoming, *last)
    vector_grads = vector_sum.total()
    vector_first_new = beta_one * vector_first + (1.0 - beta_one) * vector_grads
    vector_second_new = beta_two * vector_second + (1.0 - beta_two) * vector_grads * vector_grads
    vectors_new = vectors - vector_rate * adam_step(vector_first_new, vector_second_new)
    updated = [Cell(vector_first_new), Cell(vector_second_new), Cell(vectors_new)]

    traded = []
    for s in range(slot_count):
        turned = dot_tn(left.value[s], incoming.value[:, s].reshape(width, quarter)).astype(bf16)
        turned = turned.reshape(outer, 2 * quarter, quarter)
        traded.append(Cell(trade_blocks(turned, "o", outer)))
    backs, firsts, seconds = [], [], []
    for s in range(slot_count):
        if s:
            bind(traded[s], backs[-1])
        turned = traded[s].value.reshape(outer, 2, quarter, quarter).transpose(1, 0, 2, 3)
        turned = trade_blocks(turned, "c", 2)
        turned = turned.transpose(2, 1, 0, 3).reshape(quarter, width)
        rotated = dot(turned, right.value[s])
        first_new = beta_one * panel_first[:, s] + (1.0 - beta_one) * rotated
        second_new = beta_two * panel_second[:, s] + (1.0 - beta_two) * rotated * rotated
        step_values = adam_step(first_new, second_new).astype(bf16)
        back_turn = Cell(dot_nt(step_values, right.value[s]).astype(bf16))
        firsts.append(jnp.where(mine[s], first_new, 0.0))
        seconds.append(jnp.where(mine[s], second_new, 0.0))
        backs.append(back_turn)
    masters = []
    for s in range(slot_count):
        back_turn = gather_blocks(backs[s].value, "o", outer)
        back_turn = gather_blocks(back_turn, "c", 2)
        back_turn = back_turn.transpose(1, 0, 2, 3).reshape(width, width)
        update = dot(left_rows[s], back_turn)
        masters.append(jnp.where(mine[s], panel_master[:, s] - learn_rate * update, 0.0))
    results = list(zip(firsts, seconds, masters))
    first_new, second_new, master_new = [jnp.stack(part, axis=1) for part in zip(*results)]
    return (
        layer_out.reshape(frames.shape),
        frames_grad.value.reshape(frames.shape),
        panel_grads,
        vector_grads,
        *values(updated),
        first_new,
        second_new,
        master_new,
    )


def solution(mesh):
    outer = mesh.shape["dp"] // 2
    owners_count = mesh.shape["fsdp"]
    split = Mesh(mesh.devices.reshape(outer, 2, owners_count), ("o", "c", "f"))
    every = P(("o", "c", "f"), None, None)
    state = P(("o", "c"), "f", None)
    return jax.shard_map(
        functools.partial(on_device, outer, owners_count),
        mesh=split,
        in_specs=(
            every,
            P(("o", "c", "f")),
            every,
            P(None, "f", None),
            P(),
            P(),
            P(),
            P(),
            P("f", None, None),
            P("f", None, None),
            state,
            state,
            state,
        ),
        out_specs=(
            every,
            every,
            P(None, "f", ("o", "c")),
            P(),
            P(),
            P(),
            P(),
            state,
            state,
            state,
        ),
        check_vma=False,
    )
```

```python
import functools

import jax
import jax.numpy as jnp
from jax import lax
from jax.experimental import pallas as pl
from jax.experimental.pallas import tpu as pltpu
from jax.sharding import Mesh
from jax.sharding import PartitionSpec as P

HEADS = 8
KERNEL = 5
STEPS = 4


norm_eps = 1e-05
adam_eps = 1e-08
beta_one = 0.5
beta_two = 0.5
learn_rate = 0.02
vector_rate = 0.25

bf16 = jnp.bfloat16
f32 = jnp.float32
ANY = pl.ANY
VMEM = pltpu.VMEM
SMEM = pltpu.SMEM
SWAP = [(0, 1), (1, 0)]
TILE = 1024
tie = lax.optimization_barrier
VMEM_LIMIT = 56 * 1024 * 1024


def layer_norm(values, gain_row, shift_row):
    centred = values - jnp.mean(values, axis=-1, keepdims=True)
    inverse = lax.rsqrt(jnp.mean(centred * centred, axis=-1, keepdims=True) + norm_eps)
    return centred * inverse * gain_row + shift_row


def norm_backward(residual, gain_row, shift_row, normed_grad):
    ignored, pull_back = jax.vjp(layer_norm, residual, gain_row, shift_row)
    return pull_back(normed_grad)


def adam_step(first_new, second_new):
    return (
        first_new
        / (1.0 - beta_one**STEPS)
        / (jnp.sqrt(second_new / (1.0 - beta_two**STEPS)) + adam_eps)
    )


def token_sum(values):
    return jnp.sum(values, axis=0, dtype=f32)


def dot(left, right):
    return lax.dot_general(left, right, (((1,), (0,)), ((), ())), preferred_element_type=f32)


def dot_nt(left, right):
    return lax.dot_general(left, right, (((1,), (1,)), ((), ())), preferred_element_type=f32)


def dot_tn(left, right):
    return lax.dot_general(left, right, (((0,), (0,)), ((), ())), preferred_element_type=f32)


class Cell:
    def __init__(self, value):
        self.value = value


def bind(*cells):
    for cell, value in zip(cells, tie(tuple(cell.value for cell in cells))):
        cell.value = value


class Wires:
    def __init__(self, outer, owners_count):
        self.outer, self.count = outer, owners_count
        walk = list(range(0, owners_count, 2)) + list(range(owners_count - 1, 0, -2))
        onward = [(walk[i], walk[(i + 1) % owners_count]) for i in range(owners_count)]
        self.routes = {
            "onward": ("f", onward),
            "back": ("f", [(b, a) for a, b in onward]),
            "chip": ("o", [(i, i ^ 1) for i in range(outer)]),
            "core": ("c", SWAP),
        }
        for name, count in (("o", outer), ("f", owners_count)):
            step = 1
            while step < count:
                self.routes[f"{name}{step}"] = (name, [(i, i ^ step) for i in range(count)])
                step *= 2
        index = lax.axis_index("f")
        self.place = jnp.where(index % 2 == 0, index // 2, owners_count - 1 - index // 2)
        self.past = []

    def start(self, *groups, after=(), beside=()):
        sends = [send for group in groups for send in group]
        if sends and not after:
            cells = [Cell(value) for value, route, take in sends]
            bind(*cells, *beside)
            sends = [(cell.value, *send[1:]) for cell, send in zip(cells, sends)]
        came = []
        for value, route, take in sends:
            if after:
                value = tie((value, *[cell.value for cell in after]))[0]
            axis, pairs = self.routes[route]
            came.append(Cell(lax.ppermute(value, axis, pairs)))
            take(came[-1])
        return came

    def slot(self, *groups):
        came = self.start(*groups, after=self.past[-2] if len(self.past) >= 2 else ())
        if came:
            self.past.append(came)
        return came

    def index_at(self, steps):
        spot = (self.place + steps + self.count) % self.count
        return jnp.where(spot < self.count // 2, 2 * spot, 2 * (self.count - 1 - spot) + 1)

    def reach(self, turn):
        half = self.count // 2
        return (half, half - 1) if turn == 0 else (half - 1, half)


class Gather:
    def __init__(self, wires, unit, turn):
        self.wires = wires
        self.left = list(wires.reach(turn))
        self.pieces = [Cell(unit)]
        self.origin = [wires.index_at(0)]
        self.moving = [self.pieces[0], self.pieces[0]]
        self.hops = 0

    def hop(self):
        self.hops += 1
        sends = []
        for way, (route, sign) in enumerate((("onward", -1), ("back", 1))):
            if self.left[way]:
                self.left[way] -= 1
                self.origin.append(self.wires.index_at(sign * self.hops))

                def take(cell, way=way):
                    self.moving[way] = cell
                    self.pieces.append(cell)

                sends.append((self.moving[way].value, route, take))
        return sends

    def spots(self):
        return jnp.stack(self.origin).astype(jnp.int32)


class Reduce:
    def __init__(self, wires, matrices, depth, turn):
        self.wires, self.depth = wires, depth
        self.lead = matrices.shape[:-2]
        self.flat = matrices.reshape((-1,) + matrices.shape[-2:])
        self.left = list(wires.reach(turn))
        self.moving = [None, None]

    def hop(self):
        return hop_together(self)

    def arrived(self, way):
        cell, first = self.moving[way]
        return cell.value[first : first + self.flat.shape[0]]

    def total(self):
        while any(self.left):
            self.wires.slot(self.hop())
        start = self.wires.index_at(0) * self.depth
        own = lax.dynamic_slice_in_dim(self.flat, start, self.depth, 1).astype(f32)
        total = own + self.arrived(0).astype(f32) + self.arrived(1).astype(f32)
        return total.reshape(self.lead + total.shape[1:])


def hop_kernel(plan, counts, starts, *refs):
    n_in = counts[0]
    outs = refs[n_in : n_in + counts[1]]
    came, sems = refs[n_in + counts[1] : -1], refs[-1]
    depth = outs[0].shape[1]
    copies = []
    for i, (way, place, panels, matrix, had, spot) in enumerate(plan):
        row = pl.multiple_of(starts[i] * depth, depth)
        out = outs[way].at[pl.ds(place, panels)]
        copies.append(
            pltpu.make_async_copy(refs[matrix].at[:, pl.ds(row, depth)], out, sems.at[2 * i])
        )
        if had is not None:
            copies.append(
                pltpu.make_async_copy(
                    refs[had].at[pl.ds(spot, panels)],
                    came[way].at[pl.ds(place, panels)],
                    sems.at[2 * i + 1],
                )
            )
    start_all(copies)
    wait_all(copies)
    for way, place, panels, matrix, had, spot in plan:
        if had is not None:
            for p in range(place, place + panels):
                total = outs[way][p].astype(f32) + came[way][p].astype(f32)
                outs[way][p] = total.astype(bf16)


def hop_together(*sums):
    wires, depth = sums[0].wires, sums[0].depth
    columns = sums[0].flat.shape[-1]
    arrays = [part.flat for part in sums]
    cells, plan, starts, sends, sizes = [], [], [], [], []
    for way, (route, sign) in enumerate((("onward", 1), ("back", -1))):
        going = [i for i, part in enumerate(sums) if part.left[way]]
        if not going:
            continue
        place = 0
        places = []
        for i in going:
            part = sums[i]
            had, spot = None, 0
            if part.moving[way] is not None:
                cell, spot = part.moving[way]
                if all(cell is not c for c in cells):
                    cells.append(cell)
                had = len(arrays) + [cell is c for c in cells].index(True)
            panels = part.flat.shape[0]
            plan.append((len(sends), place, panels, i, had, spot))
            starts.append(wires.index_at(sign * part.left[way]))
            part.left[way] -= 1
            places.append((part, place))
            place += panels

        def take(cell, way=way, places=places):
            for part, first in places:
                part.moving[way] = (cell, first)

        sends.append((route, take))
        sizes.append(place)
    if not sends:
        return []
    inputs = arrays + [cell.value for cell in cells]
    messages = pl.pallas_call(
        functools.partial(hop_kernel, tuple(plan), (len(inputs), len(sizes))),
        out_shape=[jax.ShapeDtypeStruct((n, depth, columns), bf16) for n in sizes],
        in_specs=[pl.BlockSpec(memory_space=SMEM)] + [pl.BlockSpec(memory_space=ANY)] * len(inputs),
        out_specs=[pl.BlockSpec(memory_space=VMEM)] * len(sizes),
        scratch_shapes=[VMEM((n, depth, columns), bf16) for n in sizes]
        + [pltpu.SemaphoreType.DMA((2 * len(plan),))],
        compiler_params=pltpu.CompilerParams(vmem_limit_bytes=VMEM_LIMIT),
        cost_estimate=pl.CostEstimate(
            flops=sum(sizes) * depth * columns,
            bytes_accessed=6 * sum(sizes) * depth * columns,
            transcendentals=0,
        ),
        name="hop",
    )(jnp.stack(starts).astype(jnp.int32), *inputs)
    return [(message, *send) for message, send in zip(messages, sends)]


class AllSum:
    def __init__(self, wires, value):
        self.wires, self.value = wires, Cell(value)
        self.todo = ["core"] + [name for name in wires.routes if name[1:].isdigit()]
        self.came = None

    def hop(self):
        if not self.todo:
            return []
        self.settle()
        return [(self.value.value, self.todo.pop(0), self.take)]

    def take(self, cell):
        self.came = cell

    def settle(self):
        if self.came is not None:
            self.value = Cell(self.value.value + self.came.value)
            self.came = None

    def total(self):
        while self.todo:
            self.wires.slot(self.hop())
        self.settle()
        return self.value.value


class ChipSum:
    def __init__(self, wires, blocks=None, here=None, there=None, cuts=None):
        self.wires, self.blocks, self.cuts = wires, blocks, cuts
        if blocks is not None and wires.outer == 2:
            index = lax.axis_index("o")
            here = lax.dynamic_index_in_dim(blocks, index, 0, keepdims=False)
            there = lax.dynamic_index_in_dim(blocks, 1 - index, 0, keepdims=False)
            there = [there] if cuts is None else [there[a:b] for a, b in cuts]
        self.here, self.there, self.came = here, list(there or []), []

    def send(self):
        if not self.there:
            return []
        return [(self.there.pop(0).astype(bf16), "chip", self.came.append)]

    def total(self):
        if self.here is None:
            low = self.blocks.astype(bf16)
            low = lax.psum_scatter(low, "o", scatter_dimension=0, tiled=True)
            return low[0].astype(f32)
        while self.there:
            self.wires.slot(self.send())
        came = [cell.value for cell in self.came]
        if len(came) > 1:
            came = jnp.stack(came) if self.cuts is None else jnp.concatenate(came)
        else:
            came = came[0]
        return self.here.astype(f32) + came.astype(f32)


def swap_cores(values):
    return lax.ppermute(values, "c", SWAP)


def gather_blocks(values, name, count):
    if count == 2:
        index = lax.axis_index(name)
        other = lax.ppermute(values, name, SWAP)
        first = jnp.where(index == 0, values, other)
        second = jnp.where(index == 0, other, values)
        return jnp.stack([first, second])
    return lax.all_gather(values, name)


def trade_blocks(values, name, count):
    if count == 2:
        index = lax.axis_index(name)
        there = lax.dynamic_index_in_dim(values, 1 - index, 0, keepdims=False)
        here = lax.dynamic_index_in_dim(values, index, 0, keepdims=False)
        came = lax.ppermute(there, name, SWAP)
        return jnp.stack([jnp.where(index == 0, here, came), jnp.where(index == 0, came, here)])
    return lax.all_to_all(values, name, split_axis=0, concat_axis=0, tiled=True)


def pick_kernel(slots, source, grads, out, sems):
    copies = [
        pltpu.make_async_copy(grads.at[source[i]], out.at[i], sems.at[i]) for i in range(slots)
    ]
    for copy in copies:
        copy.start()
    for copy in copies:
        copy.wait()


def pick(grads, source):
    slots = source.shape[0]
    return pl.pallas_call(
        functools.partial(pick_kernel, slots),
        out_shape=jax.ShapeDtypeStruct((slots,) + grads.shape[1:], grads.dtype),
        in_specs=[pl.BlockSpec(memory_space=SMEM), pl.BlockSpec(memory_space=ANY)],
        out_specs=pl.BlockSpec(memory_space=VMEM),
        scratch_shapes=[pltpu.SemaphoreType.DMA((slots,))],
        name="pick",
    )(source, grads)


def load_share(sides, spots, first, weights, sems):
    depth = sides[0][0].shape[1]
    copies = []
    for side, pieces in enumerate(sides):
        for i, piece in enumerate(pieces):
            row = pl.multiple_of(spots[i] * depth, depth)
            copies.append(
                pltpu.make_async_copy(
                    piece.at[first],
                    weights.at[len(sides) * first + side, pl.ds(row, depth)],
                    sems.at[first, side, i],
                )
            )
    return copies


def cut_sides(refs, count, halves):
    return [refs[i * count : (i + 1) * count] for i in range(halves)], refs[halves * count :]


def ffn_forward_kernel(count, halves, meta, normed, bias, *refs):
    sides, refs = cut_sides(refs, count, halves)
    hidden, active, branch, away, weights, sems = refs
    tokens, width = branch.shape
    ins = load_share(sides, meta, 0, weights, sems)
    outs = load_share(sides, meta, 1, weights, sems)
    start_all(ins + outs)
    wait_all(ins)
    for p in range(halves):

        @column_loop(width)
        def columns(cols):
            value = dot(normed[...], weights[p, :, cols]) + bias[p, :, cols]
            hidden[p, :, cols] = value
            active[p, :, cols] = (value * jax.nn.sigmoid(value)).astype(bf16)

    wait_all(outs)

    @column_loop(width)
    def out_columns(cols):
        total = dot(active[0], weights[halves, :, cols])
        for p in range(1, halves):
            total = total + dot(active[p], weights[halves + p, :, cols])
        branch[:, cols] = total[:tokens]
        away[:, cols] = total[tokens:].astype(bf16)


def ffn_forward_call(normed, bias, sides, meta):
    tokens, width = normed.shape
    count, halves = len(sides[0]), len(sides)
    return pl.pallas_call(
        functools.partial(ffn_forward_kernel, count, halves),
        out_shape=[
            jax.ShapeDtypeStruct((halves, tokens, width), f32),
            jax.ShapeDtypeStruct((halves, tokens, width), bf16),
            jax.ShapeDtypeStruct((tokens // 2, width), f32),
            jax.ShapeDtypeStruct((tokens // 2, width), bf16),
        ],
        in_specs=[
            pl.BlockSpec(memory_space=SMEM),
            pl.BlockSpec(memory_space=VMEM),
            pl.BlockSpec(memory_space=VMEM),
        ]
        + [pl.BlockSpec(memory_space=ANY)] * (halves * count),
        out_specs=[pl.BlockSpec(memory_space=VMEM)] * 4,
        scratch_shapes=[
            VMEM((2 * halves, width, width), bf16),
            pltpu.SemaphoreType.DMA((2, halves, count)),
        ],
        compiler_params=pltpu.CompilerParams(vmem_limit_bytes=VMEM_LIMIT),
        cost_estimate=pl.CostEstimate(
            flops=4 * halves * tokens * width * width,
            bytes_accessed=8 * width * width + tokens * width * 18,
            transcendentals=halves * tokens * width,
        ),
        name="ffn_forward",
    )(meta, normed, bias, *[piece for pieces in sides for piece in pieces])


def ffn_out_backward_kernel(count, halves, bias, blocks, meta, hidden, active, grad, had, *refs):
    sides, refs = cut_sides(refs, count, halves)
    low, sums, *matrices, weights, sems = refs
    outer, ways = blocks
    width = low.shape[-1]
    parity, core = meta[count], meta[count + 1]
    store = share_store(ways, meta[count + 2], matrices)
    sums[...] = had[...]
    copies = load_share(sides, meta, 1, weights, sems)
    start_all(copies)
    for p in range(halves):
        put_blocks(store, p ^ parity if halves == 2 else p, active.at[p], grad, outer)
    wait_all(copies)
    for p in range(halves):
        row = bias + 2 * core + (p ^ parity)

        @column_loop(width)
        def rows(cols):
            value = hidden[p, :, cols]
            share = jax.nn.sigmoid(value)
            slope = share * (1.0 + value * (1.0 - share))
            part = (dot_nt(grad[...], weights[halves + p, cols, :]) * slope).astype(bf16)
            low[p, :, cols] = part
            sums[pl.ds(row, 1), cols] = jnp.sum(part.astype(f32), axis=0, keepdims=True)


def ffn_in_backward_kernel(count, halves, bias, blocks, meta, normed, low, *refs):
    sides, refs = cut_sides(refs, count, halves)
    normed_grad, away, *matrices, weights, sems = refs
    tokens, width = away.shape
    outer, ways = blocks
    parity = meta[count]
    store = share_store(ways, meta[count + 2], matrices)
    copies = load_share(sides, meta, 0, weights, sems)
    start_all(copies)
    for p in range(halves):
        put_blocks(store, p ^ parity if halves == 2 else p, normed, low.at[p], outer)
    wait_all(copies)

    @column_loop(width)
    def back(cols):
        total = dot_nt(low[0], weights[0, cols, :])
        for p in range(1, halves):
            total = total + dot_nt(low[p], weights[p, cols, :])
        normed_grad[:, cols] = total[:tokens]
        away[:, cols] = total[tokens:].astype(bf16)


def share_store(ways, chip, matrices):
    if ways:
        return store_by_chip(chip, matrices[0], matrices[1:])
    return store_all(matrices[0])


def ffn_backward_call(kernel, name, bias, outer, ways, meta, arrays, sides, outs):
    width = sides[0][0].shape[-1]
    tokens = arrays[0].shape[-2]
    count, halves = len(sides[0]), len(sides)
    quarter = width // (2 * outer)
    if ways:
        part = jax.ShapeDtypeStruct((2, width, quarter), bf16)
        blocks = [jax.ShapeDtypeStruct((2, 2, width, quarter), bf16), part, part]
    else:
        blocks = [jax.ShapeDtypeStruct((outer, 2, halves, width, quarter), bf16)]
    return pl.pallas_call(
        functools.partial(kernel, count, halves, bias, (outer, ways)),
        out_shape=[*outs, *blocks],
        in_specs=[pl.BlockSpec(memory_space=SMEM)]
        + [pl.BlockSpec(memory_space=VMEM)] * len(arrays)
        + [pl.BlockSpec(memory_space=ANY)] * (halves * count),
        out_specs=[pl.BlockSpec(memory_space=VMEM)] * (len(outs) + len(blocks)),
        scratch_shapes=[
            VMEM((2 * halves, width, width), bf16),
            pltpu.SemaphoreType.DMA((2, halves, count)),
        ],
        compiler_params=pltpu.CompilerParams(vmem_limit_bytes=VMEM_LIMIT),
        cost_estimate=pl.CostEstimate(
            flops=4 * halves * tokens * width * width,
            bytes_accessed=8 * width * width + tokens * width * 16,
            transcendentals=tokens * width,
        ),
        name=name,
    )(meta, *arrays, *[piece for pieces in sides for piece in pieces])


def norm_parts(values):
    centred = values - jnp.mean(values, axis=-1, keepdims=True)
    inverse = lax.rsqrt(jnp.mean(centred * centred, axis=-1, keepdims=True) + norm_eps)
    return centred * inverse, inverse


def norm_pull(normed, inverse, gain_row, grad):
    scaled = grad * gain_row
    along = jnp.mean(scaled * normed, axis=-1, keepdims=True)
    return inverse * (scaled - jnp.mean(scaled, axis=-1, keepdims=True) - normed * along)


def column_sum(values):
    return jnp.sum(values, axis=0, keepdims=True)


def halves_to_panels(first, last, own, other, spots, core, weights, sems):
    depth, half = own[0].shape[1:]
    copies = []
    for i in range(len(own)):
        row = pl.multiple_of(spots[i] * depth, depth)
        for side, pieces in ((core, own), (1 - core, other)):
            col = pl.multiple_of(side * half, half)
            copies.append(
                pltpu.make_async_copy(
                    pieces[i].at[pl.ds(first, last - first)],
                    weights.at[pl.ds(0, last - first), pl.ds(row, depth), pl.ds(col, half)],
                    sems.at[len(copies)],
                )
            )
    return copies


def start_all(copies):
    for copy in copies:
        copy.start()


def wait_all(copies):
    for copy in copies:
        copy.wait()


def column_loop(width):
    def run(body):
        for start in range(0, width, TILE):
            body(slice(start, start + TILE))

    return run


def put_blocks(store, panel, left, right, outer):
    quarter = right.shape[-1] // (2 * outer)

    @column_loop(left.shape[1])
    def rows(part):
        value = dot_tn(left[:, part], right[...]).astype(bf16)
        for o in range(outer):
            for c in range(2):
                at = (2 * o + c) * quarter
                store(o, c, panel, part, value[:, at : at + quarter])


def store_all(blocks):
    def store(o, c, panel, part, value):
        blocks[o, c, panel, part, :] = value

    return store


def store_by_core(core, here, there):
    def store(o, c, panel, part, value):
        @pl.when(c == core)
        def kept():
            here[o, panel, part, :] = value

        @pl.when(c != core)
        def sent():
            there[o, panel, part, :] = value

    return store


def store_by_chip(chip, here, there):
    def store(o, c, panel, part, value):
        @pl.when(o == chip)
        def kept():
            here[c, panel, part, :] = value

        @pl.when(o != chip)
        def sent():
            there[c][panel, part, :] = value

    return store


def attend(queries, keys, head, size, length, score_scale):
    cols = slice(head * size, (head + 1) * size)
    scores = dot_nt(queries[:, cols], keys[:, cols]) * score_scale
    spot = lax.broadcasted_iota(jnp.int32, scores.shape, 1)
    scores = jnp.where(spot < length, scores, -1000000000.0)
    peak = jnp.max(scores, axis=-1, keepdims=True)
    raised = jnp.exp(scores - peak)
    return raised * (1.0 / jnp.sum(raised, axis=-1, keepdims=True)), cols


def attention_forward_kernel(count, meta, stream, rows, *refs):
    own, other = refs[:count], refs[count : 2 * count]
    out, normed, queries, keys, values, mixed, weights, sems = refs[2 * count :]
    core, length = meta[count], meta[count + 1]
    width = stream.shape[1]
    size = width // HEADS
    copies = halves_to_panels(0, 4, own, other, meta, core, weights, sems)
    start_all(copies)
    inside, ignored = norm_parts(stream[...])
    normed[...] = (inside * rows[2:3] + rows[3:4]).astype(bf16)
    wait_all(copies)

    @column_loop(width)
    def project(cols):
        low = normed[...]
        queries[:, cols] = (dot(low, weights[0, :, cols]) + rows[22:23, cols]).astype(bf16)
        keys[:, cols] = dot(low, weights[1, :, cols]).astype(bf16)
        values[:, cols] = (dot(low, weights[2, :, cols]) + rows[23:24, cols]).astype(bf16)

    for head in range(HEADS):
        soft, cols = attend(queries, keys, head, size, length, size ** (-0.5))
        mixed[:, cols] = dot(soft.astype(bf16), values[:, cols]).astype(bf16)

    @column_loop(width)
    def branch(cols):
        out[:, cols] = (
            stream[:, cols] + dot(mixed[...], weights[3, :, cols]) + rows[24:25, cols]
        )


def attention_heads_backward_kernel(
    count, meta, grad, queries, keys, values, mixed, had, *refs
):
    own, other = refs[:count], refs[count : 2 * count]
    lows, here, there, sums, weights, branch_grad, low_mixed, sems = refs[2 * count :]
    store = store_by_core(meta[count], here, there)
    sums[...] = had[...]
    core, length = meta[count], meta[count + 1]
    width = grad.shape[1]
    size = width // HEADS
    score_scale = size ** (-0.5)
    copies = halves_to_panels(3, 4, own, other, meta, core, weights, sems)
    start_all(copies)
    branch_grad[...] = grad[...].astype(bf16)
    sums[24:25] = column_sum(branch_grad[...].astype(f32))
    put_blocks(store, 0, mixed, branch_grad, here.shape[0])
    wait_all(copies)

    @column_loop(width)
    def through(cols):
        low_mixed[:, cols] = dot_nt(branch_grad[...], weights[0, cols, :]).astype(bf16)

    for head in range(HEADS):
        soft, cols = attend(queries, keys, head, size, length, score_scale)
        low = low_mixed[:, cols]
        soft_grad = dot_nt(low, values[:, cols])
        lows[2, :, cols] = dot_tn(soft.astype(bf16), low).astype(bf16)
        along = jnp.sum(soft_grad * soft, axis=-1, keepdims=True)
        score_grad = (soft * (soft_grad - along)).astype(bf16)
        lows[0, :, cols] = (dot(score_grad, keys[:, cols]) * score_scale).astype(bf16)
        lows[1, :, cols] = (dot_tn(score_grad, queries[:, cols]) * score_scale).astype(bf16)

    sums[22:23] = column_sum(lows[0].astype(f32))
    sums[23:24] = column_sum(lows[2].astype(f32))


def attention_in_backward_kernel(count, meta, grad, stream, normed, lows, rows, had, *refs):
    own, other = refs[:count], refs[count : 2 * count]
    out, here, there, sums, half_low, weights, normed_grad, sems = refs[2 * count :]
    core = meta[count]
    store = store_by_core(core, here, there)
    sums[...] = had[...]
    width = stream.shape[1]
    copies = halves_to_panels(0, 3, own, other, meta, core, weights, sems)
    start_all(copies)
    for i in range(3):
        put_blocks(store, i, normed, lows.at[i], here.shape[0])
    wait_all(copies)

    @column_loop(width)
    def back(cols):
        total = dot_nt(lows[0], weights[0, cols, :])
        total = total + dot_nt(lows[1], weights[1, cols, :])
        normed_grad[:, cols] = total + dot_nt(lows[2], weights[2, cols, :])

    inside, inverse = norm_parts(stream[...])
    pulled = normed_grad[...]
    sums[2:3] = column_sum(pulled * inside)
    sums[3:4] = column_sum(pulled)
    flow = grad[...] + norm_pull(inside, inverse, rows[2:3], pulled)
    out[...] = flow
    half_low[...] = (0.5 * flow).astype(bf16)
    sums[16:17] = column_sum(half_low[...].astype(f32))


def moved(values, steps):
    if steps == 0:
        return values
    tall = values.shape[0]
    spot = lax.broadcasted_iota(jnp.int32, values.shape, 0) + steps
    return jnp.where((spot >= 0) & (spot < tall), pltpu.roll(values, (-steps) % tall, 0), 0.0)


def gated_depth(wide, rows, length):
    value, gate = wide[0], wide[1]
    open_gate = jax.nn.sigmoid(gate)
    inside = lax.broadcasted_iota(jnp.int32, value.shape, 0) < length
    gated = jnp.where(inside, value * open_gate, 0.0)
    depth = rows[27:28] + rows[28:29] * moved(gated, -(KERNEL // 2))
    for tap in range(1, KERNEL):
        depth = depth + rows[28 + tap : 29 + tap] * moved(gated, tap - KERNEL // 2)
    return value, open_gate, inside, gated, depth


def conv_forward_kernel(count, meta, stream, rows, *refs):
    own, other = refs[:count], refs[count : 2 * count]
    out, normed, wide, active, next_low, weights, sems = refs[2 * count :]
    core, length = meta[count], meta[count + 1]
    width = stream.shape[1]
    copies = halves_to_panels(4, 7, own, other, meta, core, weights, sems)
    start_all(copies)
    inside, ignored = norm_parts(stream[...])
    normed[...] = (inside * rows[4:5] + rows[5:6]).astype(bf16)
    wait_all(copies)

    @column_loop(width)
    def project(cols):
        for i in range(2):
            wide[i, :, cols] = dot(normed[...], weights[i, :, cols]) + rows[25 + i : 26 + i, cols]

    depth = gated_depth(wide, rows, length)[-1]
    inside, ignored = norm_parts(depth)
    shifted = inside * rows[6:7] + rows[7:8]
    active[...] = (shifted * jax.nn.sigmoid(shifted)).astype(bf16)

    @column_loop(width)
    def branch(cols):
        out[:, cols] = (
            stream[:, cols] + dot(active[...], weights[2, :, cols]) + rows[33:34, cols]
        )

    inside, ignored = norm_parts(out[...])
    next_low[...] = (inside * rows[8:9] + rows[9:10]).astype(bf16)


def conv_out_backward_kernel(count, meta, grad, wide, active, rows, had, *refs):
    own, other = refs[:count], refs[count : 2 * count]
    lows, here, there, sums, weights, full, sems = refs[2 * count :]
    core, length = meta[count], meta[count + 1]
    store = store_by_core(core, here, there)
    sums[...] = had[...]
    width = grad.shape[1]
    copies = halves_to_panels(6, 7, own, other, meta, core, weights, sems)
    start_all(copies)
    branch_grad = grad[...].astype(bf16)
    lows[0] = branch_grad
    sums[33:34] = column_sum(branch_grad.astype(f32))
    put_blocks(store, 0, active, lows.at[0], here.shape[0])
    wait_all(copies)

    @column_loop(width)
    def through(cols):
        full[:, cols] = dot_nt(lows[0], weights[0, cols, :])

    value, open_gate, valid, gated, depth = gated_depth(wide, rows, length)
    inside, inverse = norm_parts(depth)
    shifted = inside * rows[6:7] + rows[7:8]
    share = jax.nn.sigmoid(shifted)
    outer_grad = full[...] * share * (1.0 + shifted * (1.0 - share))
    sums[6:7] = column_sum(outer_grad * inside)
    sums[7:8] = column_sum(outer_grad)
    depth_grad = norm_pull(inside, inverse, rows[6:7], outer_grad)
    sums[27:28] = column_sum(depth_grad)
    gated_grad = jnp.zeros_like(depth_grad)
    for tap in range(KERNEL):
        off = tap - KERNEL // 2
        sums[28 + tap : 29 + tap] = column_sum(depth_grad * moved(gated, off))
        gated_grad = gated_grad + rows[28 + tap : 29 + tap] * moved(depth_grad, -off)
    gated_grad = jnp.where(valid, gated_grad, 0.0)
    lows[0] = (gated_grad * open_gate).astype(bf16)
    lows[1] = (gated_grad * value * open_gate * (1.0 - open_gate)).astype(bf16)
    for i in range(2):
        sums[25 + i : 26 + i] = column_sum(lows[i].astype(f32))


def conv_in_backward_kernel(count, meta, grad, stream, normed, lows, rows, had, *refs):
    own, other = refs[:count], refs[count : 2 * count]
    out, here, there, sums, weights, full, sems = refs[2 * count :]
    core = meta[count]
    store = store_by_core(core, here, there)
    sums[...] = had[...]
    width = stream.shape[1]
    copies = halves_to_panels(4, 6, own, other, meta, core, weights, sems)
    start_all(copies)
    for i in range(2):
        put_blocks(store, i, normed, lows.at[i], here.shape[0])
    wait_all(copies)

    @column_loop(width)
    def back(cols):
        full[:, cols] = dot_nt(lows[0], weights[0, cols, :]) + dot_nt(lows[1], weights[1, cols, :])

    inside, inverse = norm_parts(stream[...])
    pulled = full[...]
    sums[4:5] = column_sum(pulled * inside)
    sums[5:6] = column_sum(pulled)
    out[...] = grad[...] + norm_pull(inside, inverse, rows[4:5], pulled)


def pull_kernel(gain, grad, stream, mine, came, rows, had, out, sums):
    sums[...] = had[...]
    inside, inverse = norm_parts(stream[...])
    pulled = mine[...] + came[...].astype(f32)
    sums[gain : gain + 1] = column_sum(pulled * inside)
    sums[gain + 1 : gain + 2] = column_sum(pulled)
    flow = grad[...] + norm_pull(inside, inverse, rows[gain : gain + 1], pulled)
    out[...] = flow.astype(out.dtype)


def pull_call(gain, grad, stream, mine, came, rows, had, dtype):
    return pl.pallas_call(
        functools.partial(pull_kernel, gain),
        out_shape=[
            jax.ShapeDtypeStruct(grad.shape, dtype),
            jax.ShapeDtypeStruct(had.shape, f32),
        ],
        cost_estimate=pl.CostEstimate(
            flops=20 * grad.size, bytes_accessed=16 * grad.size, transcendentals=0
        ),
        compiler_params=pltpu.CompilerParams(vmem_limit_bytes=VMEM_LIMIT),
        name="norm_pull",
    )(grad, stream, mine, came, rows, had)


def turn_kernel(meta, stream, mine, came, cotangent, rows, layer_out, out, half_low, sums):
    last = stream[...] + 0.5 * (mine[...] + came[...].astype(f32) + rows[21:22])
    inside, inverse = norm_parts(last)
    layer_out[...] = (inside * rows[10:11] + rows[11:12]).astype(bf16)
    spot = lax.broadcasted_iota(jnp.int32, last.shape, 0)
    grad = jnp.where(spot < meta[0], cotangent[...].astype(f32), 0.0)
    sums[...] = jnp.zeros_like(sums)
    sums[10:11] = column_sum(grad * inside)
    sums[11:12] = column_sum(grad)
    flow = norm_pull(inside, inverse, rows[10:11], grad)
    out[...] = flow
    half_low[...] = (0.5 * flow).astype(bf16)
    sums[21:22] = column_sum(half_low[...].astype(f32))


def turn_call(length, stream, mine, came, cotangent, rows):
    return pl.pallas_call(
        turn_kernel,
        in_specs=[pl.BlockSpec(memory_space=SMEM)] + [pl.BlockSpec(memory_space=VMEM)] * 5,
        out_shape=[
            jax.ShapeDtypeStruct(stream.shape, bf16),
            jax.ShapeDtypeStruct(stream.shape, f32),
            jax.ShapeDtypeStruct(stream.shape, bf16),
            jax.ShapeDtypeStruct(rows.shape, f32),
        ],
        cost_estimate=pl.CostEstimate(
            flops=30 * stream.size, bytes_accessed=20 * stream.size, transcendentals=0
        ),
        compiler_params=pltpu.CompilerParams(vmem_limit_bytes=VMEM_LIMIT),
        name="turn",
    )(length, stream, mine, came, cotangent, rows)


def panel_call(kernel, name, panels, meta, blocks, own, other, outs, scratch, flops):
    count = len(own)
    width = blocks[0].shape[1]
    return pl.pallas_call(
        functools.partial(kernel, count),
        out_shape=outs,
        in_specs=[pl.BlockSpec(memory_space=SMEM)]
        + [pl.BlockSpec(memory_space=VMEM)] * len(blocks)
        + [pl.BlockSpec(memory_space=ANY)] * (2 * count),
        out_specs=[pl.BlockSpec(memory_space=VMEM)] * len(outs),
        scratch_shapes=[VMEM((panels, width, width), bf16)]
        + scratch
        + [pltpu.SemaphoreType.DMA((2 * count,))],
        compiler_params=pltpu.CompilerParams(vmem_limit_bytes=VMEM_LIMIT),
        cost_estimate=pl.CostEstimate(
            flops=flops,
            bytes_accessed=panels * width * width * 2 + 8 * blocks[0].size * 4,
            transcendentals=2 * blocks[0].size,
        ),
        name=name,
    )(meta, *blocks, *own, *other)


def both_cores(values):
    return jnp.concatenate([values, swap_cores(values)], axis=0)


def on_device(
    outer,
    owners_count,
    frames,
    lengths,
    cotangent,
    panels,
    vectors,
    vector_first,
    vector_second,
    owners,
    basis_left,
    basis_right,
    panel_first,
    panel_second,
    panel_master,
):
    seq_count, seq_len, width = frames.shape
    tokens = seq_count * seq_len
    depth = panels.shape[1]
    half = width // 2
    quarter = width // (2 * outer)
    core = lax.axis_index("c")
    parity = lax.axis_index("o") % 2
    wires = Wires(outer, owners_count)
    shape = jax.ShapeDtypeStruct

    def chip_share(first, side):
        panel = first + 2 * core + side
        ins = lax.dynamic_slice_in_dim(panels, panel, 1, 0)
        outs = lax.dynamic_slice_in_dim(panels, panel + 4, 1, 0)
        return jnp.concatenate([ins, outs], axis=0)

    first = Gather(wires, chip_share(0, parity), 0)
    middle = Gather(wires, lax.dynamic_slice(panels, (8, 0, core * half), (7, depth, half)), 1)
    second = Gather(wires, chip_share(15, parity), 0)
    second_other = [Cell(chip_share(15, 1 - parity))]
    middle_other = []

    class Passing:
        def __init__(self, gather, route, store, start):
            self.gather, self.route, self.store, self.next = gather, route, store, start

        def more(self, most=1):
            sends = []
            while most and self.next < len(self.gather.pieces):
                sends.append((self.gather.pieces[self.next].value, self.route, self.store.append))
                self.next += 1
                most -= 1
            return sends

    to_chip = Passing(second, "chip", second_other, 1)
    to_core = Passing(middle, "core", middle_other, 0)
    slot = wires.slot

    def values(cells):
        return [cell.value for cell in cells]

    def core_rows(first):
        rows = lax.dynamic_slice_in_dim(vectors, first + 2 * core, 2, 0)
        rows = jnp.where(parity == 0, rows, rows[::-1])
        return rows[:, None, :]

    def meta_of(gather, *more):
        return jnp.concatenate([gather.spots(), jnp.stack(more).astype(jnp.int32)])

    low_stream = shape((tokens, width), bf16)
    stream = shape((tokens, width), f32)

    left = Cell(basis_left.astype(bf16))
    right = Cell(basis_right.astype(bf16))
    def exchange(values):
        return lax.ppermute(values, "o", wires.routes["chip"][1])

    def all_four(own, came):
        mine = jnp.concatenate([own, came])
        return jnp.concatenate([mine, swap_cores(mine)])

    def sum_four(mine, away):
        total = mine + swap_cores(away).astype(f32)
        return total[:tokens], total[tokens:].astype(bf16)

    start = Cell(frames.reshape(tokens, width).astype(f32))
    own_first = layer_norm(start.value, vectors[0], vectors[1]).astype(bf16)
    bias_first, bias_second = Cell(core_rows(12)[:1]), Cell(core_rows(17))
    ready = [start, bias_first, bias_second, *second_other]
    far_first = []
    came = slot(first.hop(), [(own_first, "chip", far_first.append)])
    bind(*ready, *came)
    slot(middle.hop(), to_core.more())
    normed = Cell(all_four(own_first, far_first[0].value))
    slot(first.hop())
    bind(normed, left, right, *wires.past[-2])
    slot(second.hop(), to_core.more(2))
    slot(first.hop(), to_chip.more())
    slot(middle.hop(), to_chip.more())
    came = slot(first.hop())
    while any(first.left):
        came = slot(first.hop())
    slot(second.hop(), to_core.more(2))
    bind(normed, *came)
    slot(middle.hop(), to_chip.more())
    hidden, active, mine, away = ffn_forward_call(
        normed.value, bias_first.value, [values(first.pieces)], meta_of(first, parity)
    )
    own, far = sum_four(mine, away)
    own, far = Cell(own), Cell(far)
    kept_first = (normed.value, hidden, active)
    bind(own, far, *wires.past[-1], *wires.past[-2])
    far_came = []
    slot(second.hop(), to_chip.more(), [(far.value, "chip", far_came.append)])
    slot(middle.hop(), to_chip.more(), to_core.more(2))
    slot(second.hop(), to_chip.more())
    while any(middle.left) or any(second.left):
        slot(middle.hop(), second.hop(), to_chip.more(2), to_core.more(2))
    after_first = Cell(
        start.value + 0.5 * (own.value + far_came[0].value.astype(f32) + vectors[16])
    )
    came = wires.start(to_core.more(2), to_chip.more(), after=wires.past[-1])
    while to_core.next < len(middle.pieces):
        came += slot(to_core.more(2))
    middle_meta = meta_of(middle, core, lengths[0])

    def sides_of(gather, other):
        return [values(gather.pieces)] + ([values(other)] if other else [])

    bind(after_first, *wires.past[-1])
    after_attn, attn_normed, queries, keys, values_, mixed = panel_call(
        attention_forward_kernel,
        "attention_forward",
        4,
        middle_meta,
        [after_first.value, vectors],
        values(middle.pieces),
        values(middle_other),
        [stream] + [low_stream] * 5,
        [],
        8 * tokens * width * width,
    )
    after_attn = Cell(after_attn)
    bind(after_attn, *came, *[cell for past in wires.past[-4:-1] for cell in past])
    came = []
    while to_chip.next < len(second.pieces):
        came += wires.start(to_chip.more(2), after=[after_attn])
    after_conv, conv_normed, wide, conv_active, second_low = panel_call(
        conv_forward_kernel,
        "conv_forward",
        3,
        middle_meta,
        [after_attn.value, vectors],
        values(middle.pieces),
        values(middle_other),
        [stream, low_stream, shape((2, tokens, width), f32), low_stream, low_stream],
        [],
        6 * tokens * width * width,
    )
    normed = both_cores(second_low)
    hidden, active, mine, away = ffn_forward_call(
        normed, bias_second.value, sides_of(second, second_other), meta_of(second, parity)
    )
    kept_second = (normed, hidden, active)
    layer_out, grad_flow, half_low, sums = turn_call(
        lengths, after_conv, mine, swap_cores(away), cotangent.reshape(tokens, width), vectors
    )

    def ring_of(turn, matrices):
        return Reduce(wires, matrices, depth, turn)

    class Share:
        def __init__(self, here, there):
            self.here, self.there = here, there

        def hop(self):
            return [(self.there, "core", self.take)]

        def take(self, cell):
            self.came = cell

        def total(self):
            return (self.here.astype(f32) + self.came.value.astype(f32)).astype(bf16)

    def trade_cores(block):
        there = lax.dynamic_index_in_dim(block, 1 - core, 0, keepdims=False)
        here = lax.dynamic_index_in_dim(block, core, 0, keepdims=False)
        came = swap_cores(there.astype(bf16)).astype(f32)
        return jnp.where(
            core == 0, jnp.concatenate([here, came]), jnp.concatenate([came, here])
        )

    chip = lax.axis_index("o")
    pairs = outer == 2

    def ffn_backward_out(both_low, gather, other, kept, bias, sums, ways):
        normed, hidden, active = kept
        return ffn_backward_call(
            ffn_out_backward_kernel,
            "ffn_out_backward",
            bias,
            outer,
            ways,
            meta_of(gather, parity, core, chip),
            [hidden, active, both_low, sums],
            sides_of(gather, other),
            [shape(active.shape, bf16), shape(vectors.shape, f32)],
        )

    def ffn_backward_in(low, gather, other, kept, ways):
        return ffn_backward_call(
            ffn_in_backward_kernel,
            "ffn_in_backward",
            0,
            outer,
            ways,
            meta_of(gather, parity, core, chip),
            [kept[0], low],
            sides_of(gather, other),
            [
                shape((kept[0].shape[0] // 2, width), f32),
                shape((kept[0].shape[0] // 2, width), bf16),
            ],
        )

    def middle_call(kernel, name, used, arrays, outs, scratch, flops):
        block_shape = shape((outer, used, width, quarter), bf16)
        return panel_call(
            kernel,
            name,
            used,
            middle_meta,
            arrays,
            values(middle.pieces),
            values(middle_other),
            [outs[0], block_shape, block_shape, shape(vectors.shape, f32), *outs[1:]],
            scratch,
            flops * tokens * width * width,
        )

    class Part:
        def __init__(self, matrices, turn):
            self.turn = turn
            self.ring = None
            if len(matrices) == 3:
                self.chips = ChipSum(wires, here=matrices[0], there=matrices[1:])
            else:
                self.chips = None
                self.ring = ring_of(turn, matrices[0])

        def send(self):
            return self.chips.send() if self.chips is not None and not hasattr(self, "late") else []

        def ready(self):
            if self.ring is None:
                self.ring = ring_of(self.turn, self.chips.total().astype(bf16))

        def hop(self):
            self.ready()
            return self.ring.hop()

        def finish(self):
            if self.chips is not None:
                return []
            self.chips = ChipSum(wires, blocks=self.ring.total())
            self.late = True
            return self.chips.send()

        def total(self):
            if self.chips is None:
                slot(self.finish())
            return self.chips.total() if hasattr(self, "late") else self.ring.total()

    begin = wires.start
    low, sums, *matrices = ffn_backward_out(
        both_cores(half_low), second, second_other, kept_second, 17, sums, False
    )
    second_out = Part(matrices, 0)
    low = Cell(low)
    came = begin(second_out.hop(), beside=[low])
    mine, away, *matrices = ffn_backward_in(low.value, second, second_other, kept_second, pairs)
    mine, away = Cell(mine), Cell(away)
    bind(mine, away, *came)
    second_in = Part(matrices, 1)
    came = begin(second_out.hop(), second_in.send(), beside=[mine, away])
    grad_flow, sums = pull_call(
        8, grad_flow, after_conv, mine.value, swap_cores(away.value), vectors, sums, f32
    )
    lows, here, there, sums = middle_call(
        conv_out_backward_kernel,
        "conv_out_backward",
        1,
        [grad_flow, wide, conv_active, vectors, sums],
        [shape((2, tokens, width), bf16)],
        [VMEM((tokens, width), f32)],
        4,
    )
    lows = Cell(lows)
    conv_out = Share(here, there)
    bind(lows, *came)
    came = begin(second_out.hop(), second_in.send(), conv_out.hop(), beside=[lows])
    flow, here, there, sums = middle_call(
        conv_in_backward_kernel,
        "conv_in_backward",
        2,
        [grad_flow, after_attn.value, conv_normed, lows.value, vectors, sums],
        [stream],
        [VMEM((tokens, width), f32)],
        8,
    )
    flow = Cell(flow)
    conv_in = Share(here, there)
    lows, here, there, sums = middle_call(
        attention_heads_backward_kernel,
        "attention_heads_backward",
        1,
        [flow.value, queries, keys, values_, mixed, sums],
        [shape((3, tokens, width), bf16)],
        [VMEM((tokens, width), bf16), VMEM((tokens, width), bf16)],
        6,
    )
    lows = Cell(lows)
    attn_out = Share(here, there)
    bind(lows, *came)
    second_in.ready()
    came = begin(
        hop_together(second_out.ring, second_in.ring),
        conv_in.hop(),
        attn_out.hop(),
        beside=[lows],
    )
    flow.value, here, there, sums, half_low = middle_call(
        attention_in_backward_kernel,
        "attention_in_backward",
        3,
        [flow.value, after_first.value, attn_normed, lows.value, vectors, sums],
        [stream, low_stream],
        [VMEM((tokens, width), f32)],
        12,
    )
    attn_in = Share(here, there)
    half_low = Cell(half_low)
    bind(half_low, *came)
    conv_total = jnp.concatenate([conv_in.total(), conv_out.total()], axis=1)
    if pairs:
        conv_chips = ChipSum(wires, blocks=conv_total, cuts=[(0, 1), (1, 3)])
    else:
        conv_part = ring_of(0, conv_total)
    far_low = []
    came = begin(
        second_in.hop(),
        attn_in.hop(),
        [(half_low.value, "chip", far_low.append)],
        beside=[half_low],
    )
    both_low = Cell(all_four(half_low.value, far_low[0].value))
    if pairs:
        came += begin(conv_chips.send(), beside=[both_low])
    low, sums, *matrices = ffn_backward_out(
        both_low.value, first, [], kept_first, 12, sums, False
    )
    first_out = ring_of(0, matrices[0])
    low = Cell(low)
    bind(low, *came)
    attn_part = ring_of(1, jnp.concatenate([attn_in.total(), attn_out.total()], axis=1))
    conv_sends = conv_chips.send() if pairs else []
    came = begin(hop_together(second_in.ring, attn_part, first_out), conv_sends, beside=[low])
    mine, away, *matrices = ffn_backward_in(low.value, first, [], kept_first, False)
    first_in = ring_of(0, matrices[0])
    mine, away = Cell(mine), Cell(away)
    bind(mine, away, *came)
    if pairs:
        conv_part = ring_of(1, conv_chips.total().astype(bf16))
    came = begin(
        hop_together(second_in.ring, attn_part, first_out, first_in, conv_part),
        beside=[mine, away],
    )
    own, far = sum_four(mine.value, away.value)
    own, far_came = Cell(own), []
    came += begin([(far, "chip", far_came.append)], beside=[own])
    bind(*came)
    came = begin(hop_together(attn_part, first_out, first_in, conv_part), second_out.finish())
    frames_grad, sums = pull_call(
        0, flow.value, start.value, own.value, far_came[0].value, vectors, sums, bf16
    )
    frames_grad, sums = Cell(frames_grad), Cell(sums)
    vector_sum = AllSum(wires, sums.value)
    bind(vector_sum.value, frames_grad, *came)
    came = begin(hop_together(attn_part, first_out, first_in, conv_part))
    bind(*came)
    attn_chips = ChipSum(wires, blocks=attn_part.total())
    came = begin(hop_together(first_out, first_in, conv_part), attn_chips.send())
    bind(*came)
    conv_total = conv_part.total()
    if not pairs:
        conv_total = ChipSum(wires, blocks=conv_total).total()

    def spread(mine):
        if not pairs:
            big = jnp.zeros((outer, 2, 2, 2) + mine.shape[2:], f32)
            at = (lax.broadcasted_iota(jnp.int32, (1, 1, 2, 2, 1, 1, 1), 2) == core) & (
                lax.broadcasted_iota(jnp.int32, (1, 1, 2, 2, 1, 1, 1), 3) == parity
            )
            big = jnp.where(at, mine[:, :, None, None], big).astype(bf16)
            big = big.reshape((outer * 2,) + big.shape[2:])
            return lax.psum_scatter(big, ("o", "c"), scatter_dimension=0, tiled=True)[0].astype(f32)
        low = trade_blocks(mine.astype(bf16), "o", outer)
        low = trade_blocks(low.transpose(1, 0, 2, 3, 4), "c", 2)
        return low.astype(f32)

    first_sum = spread(jnp.concatenate([first_in.total(), first_out.total()], axis=2))
    first_sum = [first_sum[:, :, kind].reshape(4, depth, quarter) for kind in range(2)]
    early = [trade_cores(second_in.total()), trade_cores(second_out.total()), conv_total]
    early = [Cell(part) for part in early]
    late = [Cell(first_sum[0]), Cell(attn_chips.total()), Cell(first_sum[1])]
    bind(*early, *late)
    panel_grads = jnp.concatenate(
        [
            late[0].value,
            late[2].value,
            late[1].value,
            early[2].value,
            early[0].value,
            early[1].value,
        ],
        axis=0,
    )
    panel_grads = Cell(panel_grads)
    bind(panel_grads, vector_sum.value, frames_grad)
    panel_grads = panel_grads.value

    slot_count = panel_first.shape[1]
    panel_count = owners.shape[0]
    panel_index = jnp.arange(panel_count, dtype=jnp.int32)
    same_owner = owners[:, None] == owners[None, :]
    earlier = panel_index[None, :] < panel_index[:, None]
    slot_of = jnp.sum((same_owner & earlier).astype(jnp.int32), axis=1)
    target = owners * slot_count + slot_of
    slot_hit = target[:, None] == jnp.arange(owners_count * slot_count, dtype=jnp.int32)[None, :]
    source = jnp.sum(slot_hit.astype(jnp.int32) * panel_index[:, None], axis=0)
    filled = jnp.any(slot_hit, axis=0)
    mine = lax.dynamic_slice_in_dim(filled, lax.axis_index("f") * slot_count, slot_count)

    outgoing = pick(panel_grads.astype(bf16), source)
    outgoing = outgoing.reshape(owners_count, slot_count, depth, quarter)
    incoming = lax.all_to_all(outgoing, "f", split_axis=0, concat_axis=0, tiled=True)
    block = lax.axis_index("o") * 2 + core
    left_rows = lax.dynamic_slice_in_dim(left.value, block * quarter, quarter, 1)
    incoming = Cell(incoming)
    last = None
    while vector_sum.todo:
        last = begin(vector_sum.hop())
        if len(vector_sum.todo) == 2:
            bind(incoming, *last)
    vector_grads = vector_sum.total()
    vector_first_new = beta_one * vector_first + (1.0 - beta_one) * vector_grads
    vector_second_new = beta_two * vector_second + (1.0 - beta_two) * vector_grads * vector_grads
    vectors_new = vectors - vector_rate * adam_step(vector_first_new, vector_second_new)
    updated = [Cell(vector_first_new), Cell(vector_second_new), Cell(vectors_new)]

    traded = []
    for s in range(slot_count):
        turned = dot_tn(left.value[s], incoming.value[:, s].reshape(width, quarter)).astype(bf16)
        turned = turned.reshape(outer, 2 * quarter, quarter)
        traded.append(Cell(trade_blocks(turned, "o", outer)))
    backs, firsts, seconds = [], [], []
    for s in range(slot_count):
        if s:
            bind(traded[s], backs[-1])
        turned = traded[s].value.reshape(outer, 2, quarter, quarter).transpose(1, 0, 2, 3)
        turned = trade_blocks(turned, "c", 2)
        turned = turned.transpose(2, 1, 0, 3).reshape(quarter, width)
        rotated = dot(turned, right.value[s])
        first_new = beta_one * panel_first[:, s] + (1.0 - beta_one) * rotated
        second_new = beta_two * panel_second[:, s] + (1.0 - beta_two) * rotated * rotated
        step_values = adam_step(first_new, second_new).astype(bf16)
        back_turn = Cell(dot_nt(step_values, right.value[s]).astype(bf16))
        firsts.append(jnp.where(mine[s], first_new, 0.0))
        seconds.append(jnp.where(mine[s], second_new, 0.0))
        backs.append(back_turn)
    masters = []
    for s in range(slot_count):
        back_turn = gather_blocks(backs[s].value, "o", outer)
        back_turn = gather_blocks(back_turn, "c", 2)
        back_turn = back_turn.transpose(1, 0, 2, 3).reshape(width, width)
        update = dot(left_rows[s], back_turn)
        masters.append(jnp.where(mine[s], panel_master[:, s] - learn_rate * update, 0.0))
    results = list(zip(firsts, seconds, masters))
    first_new, second_new, master_new = [jnp.stack(part, axis=1) for part in zip(*results)]
    return (
        layer_out.reshape(frames.shape),
        frames_grad.value.reshape(frames.shape),
        panel_grads,
        vector_grads,
        *values(updated),
        first_new,
        second_new,
        master_new,
    )


def solution(mesh):
    outer = mesh.shape["dp"] // 2
    owners_count = mesh.shape["fsdp"]
    split = Mesh(mesh.devices.reshape(outer, 2, owners_count), ("o", "c", "f"))
    every = P(("o", "c", "f"), None, None)
    state = P(("o", "c"), "f", None)
    return jax.shard_map(
        functools.partial(on_device, outer, owners_count),
        mesh=split,
        in_specs=(
            every,
            P(("o", "c", "f")),
            every,
            P(None, "f", None),
            P(),
            P(),
            P(),
            P(),
            P("f", None, None),
            P("f", None, None),
            state,
            state,
            state,
        ),
        out_specs=(
            every,
            every,
            P(None, "f", ("o", "c")),
            P(),
            P(),
            P(),
            P(),
            state,
            state,
            state,
        ),
        check_vma=False,
    )
```

```python
import functools

import jax
import jax.numpy as jnp
from jax import lax
from jax.experimental import pallas as pl
from jax.experimental.pallas import tpu as pltpu
from jax.sharding import Mesh
from jax.sharding import PartitionSpec as P

HEADS = 8
KERNEL = 5
STEPS = 4


norm_eps = 1e-05
adam_eps = 1e-08
beta_one = 0.5
beta_two = 0.5
learn_rate = 0.02
vector_rate = 0.25

bf16 = jnp.bfloat16
f32 = jnp.float32
ANY = pl.ANY
VMEM = pltpu.VMEM
SMEM = pltpu.SMEM
SWAP = [(0, 1), (1, 0)]
TILE = 1024
tie = lax.optimization_barrier
VMEM_LIMIT = 56 * 1024 * 1024


def layer_norm(values, gain_row, shift_row):
    centred = values - jnp.mean(values, axis=-1, keepdims=True)
    inverse = lax.rsqrt(jnp.mean(centred * centred, axis=-1, keepdims=True) + norm_eps)
    return centred * inverse * gain_row + shift_row


def norm_backward(residual, gain_row, shift_row, normed_grad):
    ignored, pull_back = jax.vjp(layer_norm, residual, gain_row, shift_row)
    return pull_back(normed_grad)


def adam_step(first_new, second_new):
    return (
        first_new
        / (1.0 - beta_one**STEPS)
        / (jnp.sqrt(second_new / (1.0 - beta_two**STEPS)) + adam_eps)
    )


def token_sum(values):
    return jnp.sum(values, axis=0, dtype=f32)


def dot(left, right):
    return lax.dot_general(left, right, (((1,), (0,)), ((), ())), preferred_element_type=f32)


def dot_nt(left, right):
    return lax.dot_general(left, right, (((1,), (1,)), ((), ())), preferred_element_type=f32)


def dot_tn(left, right):
    return lax.dot_general(left, right, (((0,), (0,)), ((), ())), preferred_element_type=f32)


class Cell:
    def __init__(self, value):
        self.value = value


def bind(*cells):
    for cell, value in zip(cells, tie(tuple(cell.value for cell in cells))):
        cell.value = value


class Wires:
    def __init__(self, outer, owners_count):
        self.outer, self.count = outer, owners_count
        walk = list(range(0, owners_count, 2)) + list(range(owners_count - 1, 0, -2))
        onward = [(walk[i], walk[(i + 1) % owners_count]) for i in range(owners_count)]
        self.routes = {
            "onward": ("f", onward),
            "back": ("f", [(b, a) for a, b in onward]),
            "chip": ("o", [(i, i ^ 1) for i in range(outer)]),
            "core": ("c", SWAP),
        }
        for name, count in (("o", outer), ("f", owners_count)):
            step = 1
            while step < count:
                self.routes[f"{name}{step}"] = (name, [(i, i ^ step) for i in range(count)])
                step *= 2
        index = lax.axis_index("f")
        self.place = jnp.where(index % 2 == 0, index // 2, owners_count - 1 - index // 2)
        self.past = []

    def start(self, *groups, after=(), beside=()):
        sends = [send for group in groups for send in group]
        if sends and not after:
            cells = [Cell(value) for value, route, take in sends]
            bind(*cells, *beside)
            sends = [(cell.value, *send[1:]) for cell, send in zip(cells, sends)]
        came = []
        for value, route, take in sends:
            if after:
                value = tie((value, *[cell.value for cell in after]))[0]
            axis, pairs = self.routes[route]
            came.append(Cell(lax.ppermute(value, axis, pairs)))
            take(came[-1])
        return came

    def slot(self, *groups):
        came = self.start(*groups, after=self.past[-2] if len(self.past) >= 2 else ())
        if came:
            self.past.append(came)
        return came

    def index_at(self, steps):
        spot = (self.place + steps + self.count) % self.count
        return jnp.where(spot < self.count // 2, 2 * spot, 2 * (self.count - 1 - spot) + 1)

    def reach(self, turn):
        half = self.count // 2
        return (half, half - 1) if turn == 0 else (half - 1, half)


class Gather:
    def __init__(self, wires, unit, turn):
        self.wires = wires
        self.left = list(wires.reach(turn))
        self.pieces = [Cell(unit)]
        self.origin = [wires.index_at(0)]
        self.moving = [self.pieces[0], self.pieces[0]]
        self.hops = 0

    def hop(self):
        self.hops += 1
        sends = []
        for way, (route, sign) in enumerate((("onward", -1), ("back", 1))):
            if self.left[way]:
                self.left[way] -= 1
                self.origin.append(self.wires.index_at(sign * self.hops))

                def take(cell, way=way):
                    self.moving[way] = cell
                    self.pieces.append(cell)

                sends.append((self.moving[way].value, route, take))
        return sends

    def spots(self):
        return jnp.stack(self.origin).astype(jnp.int32)


class Reduce:
    def __init__(self, wires, matrices, depth, turn):
        self.wires, self.depth = wires, depth
        self.lead = matrices.shape[:-2]
        self.flat = matrices.reshape((-1,) + matrices.shape[-2:])
        self.left = list(wires.reach(turn))
        self.moving = [None, None]

    def hop(self):
        return hop_together(self)

    def arrived(self, way):
        cell, first = self.moving[way]
        return cell.value[first : first + self.flat.shape[0]]

    def total(self):
        while any(self.left):
            self.wires.slot(self.hop())
        start = self.wires.index_at(0) * self.depth
        own = lax.dynamic_slice_in_dim(self.flat, start, self.depth, 1).astype(f32)
        total = own + self.arrived(0).astype(f32) + self.arrived(1).astype(f32)
        return total.reshape(self.lead + total.shape[1:])


def hop_kernel(plan, counts, starts, *refs):
    n_in = counts[0]
    outs = refs[n_in : n_in + counts[1]]
    came, sems = refs[n_in + counts[1] : -1], refs[-1]
    depth = outs[0].shape[1]
    copies = []
    for i, (way, place, panels, matrix, had, spot) in enumerate(plan):
        row = pl.multiple_of(starts[i] * depth, depth)
        out = outs[way].at[pl.ds(place, panels)]
        copies.append(
            pltpu.make_async_copy(refs[matrix].at[:, pl.ds(row, depth)], out, sems.at[2 * i])
        )
        if had is not None:
            copies.append(
                pltpu.make_async_copy(
                    refs[had].at[pl.ds(spot, panels)],
                    came[way].at[pl.ds(place, panels)],
                    sems.at[2 * i + 1],
                )
            )
    start_all(copies)
    wait_all(copies)
    for way, place, panels, matrix, had, spot in plan:
        if had is not None:
            for p in range(place, place + panels):
                total = outs[way][p].astype(f32) + came[way][p].astype(f32)
                outs[way][p] = total.astype(bf16)


def hop_together(*sums):
    wires, depth = sums[0].wires, sums[0].depth
    columns = sums[0].flat.shape[-1]
    arrays = [part.flat for part in sums]
    cells, plan, starts, sends, sizes = [], [], [], [], []
    for way, (route, sign) in enumerate((("onward", 1), ("back", -1))):
        going = [i for i, part in enumerate(sums) if part.left[way]]
        if not going:
            continue
        place = 0
        places = []
        for i in going:
            part = sums[i]
            had, spot = None, 0
            if part.moving[way] is not None:
                cell, spot = part.moving[way]
                if all(cell is not c for c in cells):
                    cells.append(cell)
                had = len(arrays) + [cell is c for c in cells].index(True)
            panels = part.flat.shape[0]
            plan.append((len(sends), place, panels, i, had, spot))
            starts.append(wires.index_at(sign * part.left[way]))
            part.left[way] -= 1
            places.append((part, place))
            place += panels

        def take(cell, way=way, places=places):
            for part, first in places:
                part.moving[way] = (cell, first)

        sends.append((route, take))
        sizes.append(place)
    if not sends:
        return []
    inputs = arrays + [cell.value for cell in cells]
    messages = pl.pallas_call(
        functools.partial(hop_kernel, tuple(plan), (len(inputs), len(sizes))),
        out_shape=[jax.ShapeDtypeStruct((n, depth, columns), bf16) for n in sizes],
        in_specs=[pl.BlockSpec(memory_space=SMEM)] + [pl.BlockSpec(memory_space=ANY)] * len(inputs),
        out_specs=[pl.BlockSpec(memory_space=VMEM)] * len(sizes),
        scratch_shapes=[VMEM((n, depth, columns), bf16) for n in sizes]
        + [pltpu.SemaphoreType.DMA((2 * len(plan),))],
        compiler_params=pltpu.CompilerParams(vmem_limit_bytes=VMEM_LIMIT),
        cost_estimate=pl.CostEstimate(
            flops=sum(sizes) * depth * columns,
            bytes_accessed=6 * sum(sizes) * depth * columns,
            transcendentals=0,
        ),
        name="hop",
    )(jnp.stack(starts).astype(jnp.int32), *inputs)
    return [(message, *send) for message, send in zip(messages, sends)]


class AllSum:
    def __init__(self, wires, value):
        self.wires, self.value = wires, Cell(value)
        self.todo = ["core"] + [name for name in wires.routes if name[1:].isdigit()]
        self.came = None

    def hop(self):
        if not self.todo:
            return []
        self.settle()
        return [(self.value.value, self.todo.pop(0), self.take)]

    def take(self, cell):
        self.came = cell

    def settle(self):
        if self.came is not None:
            self.value = Cell(self.value.value + self.came.value)
            self.came = None

    def total(self):
        while self.todo:
            self.wires.slot(self.hop())
        self.settle()
        return self.value.value


class ChipSum:
    def __init__(self, wires, blocks=None, here=None, there=None, cuts=None):
        self.wires, self.blocks, self.cuts = wires, blocks, cuts
        if blocks is not None and wires.outer == 2:
            index = lax.axis_index("o")
            here = lax.dynamic_index_in_dim(blocks, index, 0, keepdims=False)
            there = lax.dynamic_index_in_dim(blocks, 1 - index, 0, keepdims=False)
            there = [there] if cuts is None else [there[a:b] for a, b in cuts]
        self.here, self.there, self.came = here, list(there or []), []

    def send(self):
        if not self.there:
            return []
        return [(self.there.pop(0).astype(bf16), "chip", self.came.append)]

    def total(self):
        if self.here is None:
            low = self.blocks.astype(bf16)
            low = lax.psum_scatter(low, "o", scatter_dimension=0, tiled=True)
            return low[0].astype(f32)
        while self.there:
            self.wires.slot(self.send())
        came = [cell.value for cell in self.came]
        if len(came) > 1:
            came = jnp.stack(came) if self.cuts is None else jnp.concatenate(came)
        else:
            came = came[0]
        return self.here.astype(f32) + came.astype(f32)


def swap_cores(values):
    return lax.ppermute(values, "c", SWAP)


def gather_blocks(values, name, count):
    if count == 2:
        index = lax.axis_index(name)
        other = lax.ppermute(values, name, SWAP)
        first = jnp.where(index == 0, values, other)
        second = jnp.where(index == 0, other, values)
        return jnp.stack([first, second])
    return lax.all_gather(values, name)


def trade_blocks(values, name, count):
    if count == 2:
        index = lax.axis_index(name)
        there = lax.dynamic_index_in_dim(values, 1 - index, 0, keepdims=False)
        here = lax.dynamic_index_in_dim(values, index, 0, keepdims=False)
        came = lax.ppermute(there, name, SWAP)
        return jnp.stack([jnp.where(index == 0, here, came), jnp.where(index == 0, came, here)])
    return lax.all_to_all(values, name, split_axis=0, concat_axis=0, tiled=True)


def pick_kernel(slots, source, grads, out, sems):
    copies = [
        pltpu.make_async_copy(grads.at[source[i]], out.at[i], sems.at[i]) for i in range(slots)
    ]
    for copy in copies:
        copy.start()
    for copy in copies:
        copy.wait()


def pick(grads, source):
    slots = source.shape[0]
    return pl.pallas_call(
        functools.partial(pick_kernel, slots),
        out_shape=jax.ShapeDtypeStruct((slots,) + grads.shape[1:], grads.dtype),
        in_specs=[pl.BlockSpec(memory_space=SMEM), pl.BlockSpec(memory_space=ANY)],
        out_specs=pl.BlockSpec(memory_space=VMEM),
        scratch_shapes=[pltpu.SemaphoreType.DMA((slots,))],
        name="pick",
    )(source, grads)


def load_share(sides, spots, first, weights, sems):
    depth = sides[0][0].shape[1]
    copies = []
    for side, pieces in enumerate(sides):
        for i, piece in enumerate(pieces):
            row = pl.multiple_of(spots[i] * depth, depth)
            copies.append(
                pltpu.make_async_copy(
                    piece.at[first],
                    weights.at[len(sides) * first + side, pl.ds(row, depth)],
                    sems.at[first, side, i],
                )
            )
    return copies


def cut_sides(refs, count, halves):
    return [refs[i * count : (i + 1) * count] for i in range(halves)], refs[halves * count :]


def ffn_forward_kernel(count, halves, meta, normed, bias, *refs):
    sides, refs = cut_sides(refs, count, halves)
    hidden, active, branch, away, weights, sems = refs
    tokens, width = branch.shape
    ins = load_share(sides, meta, 0, weights, sems)
    outs = load_share(sides, meta, 1, weights, sems)
    start_all(ins + outs)
    wait_all(ins)
    for p in range(halves):

        @column_loop(width)
        def columns(cols):
            value = dot(normed[...], weights[p, :, cols]) + bias[p, :, cols]
            hidden[p, :, cols] = value
            active[p, :, cols] = (value * jax.nn.sigmoid(value)).astype(bf16)

    wait_all(outs)

    @column_loop(width)
    def out_columns(cols):
        total = dot(active[0], weights[halves, :, cols])
        for p in range(1, halves):
            total = total + dot(active[p], weights[halves + p, :, cols])
        branch[:, cols] = total[:tokens]
        away[:, cols] = total[tokens:].astype(bf16)


def ffn_forward_call(normed, bias, sides, meta):
    tokens, width = normed.shape
    count, halves = len(sides[0]), len(sides)
    return pl.pallas_call(
        functools.partial(ffn_forward_kernel, count, halves),
        out_shape=[
            jax.ShapeDtypeStruct((halves, tokens, width), f32),
            jax.ShapeDtypeStruct((halves, tokens, width), bf16),
            jax.ShapeDtypeStruct((tokens // 2, width), f32),
            jax.ShapeDtypeStruct((tokens // 2, width), bf16),
        ],
        in_specs=[
            pl.BlockSpec(memory_space=SMEM),
            pl.BlockSpec(memory_space=VMEM),
            pl.BlockSpec(memory_space=VMEM),
        ]
        + [pl.BlockSpec(memory_space=ANY)] * (halves * count),
        out_specs=[pl.BlockSpec(memory_space=VMEM)] * 4,
        scratch_shapes=[
            VMEM((2 * halves, width, width), bf16),
            pltpu.SemaphoreType.DMA((2, halves, count)),
        ],
        compiler_params=pltpu.CompilerParams(vmem_limit_bytes=VMEM_LIMIT),
        cost_estimate=pl.CostEstimate(
            flops=4 * halves * tokens * width * width,
            bytes_accessed=8 * width * width + tokens * width * 18,
            transcendentals=halves * tokens * width,
        ),
        name="ffn_forward",
    )(meta, normed, bias, *[piece for pieces in sides for piece in pieces])


def ffn_out_backward_kernel(count, halves, bias, blocks, meta, hidden, active, grad, had, *refs):
    sides, refs = cut_sides(refs, count, halves)
    low, sums, *matrices, weights, sems = refs
    outer, ways = blocks
    width = low.shape[-1]
    parity, core = meta[count], meta[count + 1]
    store = share_store(ways, meta[count + 2], matrices)
    sums[...] = had[...]
    copies = load_share(sides, meta, 1, weights, sems)
    start_all(copies)
    for p in range(halves):
        put_blocks(store, p ^ parity if halves == 2 else p, active.at[p], grad, outer)
    wait_all(copies)
    for p in range(halves):
        row = bias + 2 * core + (p ^ parity)

        @column_loop(width)
        def rows(cols):
            value = hidden[p, :, cols]
            share = jax.nn.sigmoid(value)
            slope = share * (1.0 + value * (1.0 - share))
            part = (dot_nt(grad[...], weights[halves + p, cols, :]) * slope).astype(bf16)
            low[p, :, cols] = part
            sums[pl.ds(row, 1), cols] = jnp.sum(part.astype(f32), axis=0, keepdims=True)


def ffn_in_backward_kernel(count, halves, bias, blocks, meta, normed, low, *refs):
    sides, refs = cut_sides(refs, count, halves)
    normed_grad, away, *matrices, weights, sems = refs
    tokens, width = away.shape
    outer, ways = blocks
    parity = meta[count]
    store = share_store(ways, meta[count + 2], matrices)
    copies = load_share(sides, meta, 0, weights, sems)
    start_all(copies)
    for p in range(halves):
        put_blocks(store, p ^ parity if halves == 2 else p, normed, low.at[p], outer)
    wait_all(copies)

    @column_loop(width)
    def back(cols):
        total = dot_nt(low[0], weights[0, cols, :])
        for p in range(1, halves):
            total = total + dot_nt(low[p], weights[p, cols, :])
        normed_grad[:, cols] = total[:tokens]
        away[:, cols] = total[tokens:].astype(bf16)


def share_store(ways, chip, matrices):
    if ways:
        return store_by_chip(chip, matrices[0], matrices[1:])
    return store_all(matrices[0])


def ffn_backward_call(kernel, name, bias, outer, ways, meta, arrays, sides, outs):
    width = sides[0][0].shape[-1]
    tokens = arrays[0].shape[-2]
    count, halves = len(sides[0]), len(sides)
    quarter = width // (2 * outer)
    if ways:
        part = jax.ShapeDtypeStruct((2, width, quarter), bf16)
        blocks = [jax.ShapeDtypeStruct((2, 2, width, quarter), bf16), part, part]
    else:
        blocks = [jax.ShapeDtypeStruct((outer, 2, halves, width, quarter), bf16)]
    return pl.pallas_call(
        functools.partial(kernel, count, halves, bias, (outer, ways)),
        out_shape=[*outs, *blocks],
        in_specs=[pl.BlockSpec(memory_space=SMEM)]
        + [pl.BlockSpec(memory_space=VMEM)] * len(arrays)
        + [pl.BlockSpec(memory_space=ANY)] * (halves * count),
        out_specs=[pl.BlockSpec(memory_space=VMEM)] * (len(outs) + len(blocks)),
        scratch_shapes=[
            VMEM((2 * halves, width, width), bf16),
            pltpu.SemaphoreType.DMA((2, halves, count)),
        ],
        compiler_params=pltpu.CompilerParams(vmem_limit_bytes=VMEM_LIMIT),
        cost_estimate=pl.CostEstimate(
            flops=4 * halves * tokens * width * width,
            bytes_accessed=8 * width * width + tokens * width * 16,
            transcendentals=tokens * width,
        ),
        name=name,
    )(meta, *arrays, *[piece for pieces in sides for piece in pieces])


def norm_parts(values):
    centred = values - jnp.mean(values, axis=-1, keepdims=True)
    inverse = lax.rsqrt(jnp.mean(centred * centred, axis=-1, keepdims=True) + norm_eps)
    return centred * inverse, inverse


def norm_pull(normed, inverse, gain_row, grad):
    scaled = grad * gain_row
    along = jnp.mean(scaled * normed, axis=-1, keepdims=True)
    return inverse * (scaled - jnp.mean(scaled, axis=-1, keepdims=True) - normed * along)


def column_sum(values):
    return jnp.sum(values, axis=0, keepdims=True)


def halves_to_panels(first, last, own, other, spots, core, weights, sems):
    depth, half = own[0].shape[1:]
    copies = []
    for i in range(len(own)):
        row = pl.multiple_of(spots[i] * depth, depth)
        for side, pieces in ((core, own), (1 - core, other)):
            col = pl.multiple_of(side * half, half)
            copies.append(
                pltpu.make_async_copy(
                    pieces[i].at[pl.ds(first, last - first)],
                    weights.at[pl.ds(0, last - first), pl.ds(row, depth), pl.ds(col, half)],
                    sems.at[len(copies)],
                )
            )
    return copies


def start_all(copies):
    for copy in copies:
        copy.start()


def wait_all(copies):
    for copy in copies:
        copy.wait()


def column_loop(width):
    def run(body):
        for start in range(0, width, TILE):
            body(slice(start, start + TILE))

    return run


def put_blocks(store, panel, left, right, outer):
    quarter = right.shape[-1] // (2 * outer)

    @column_loop(left.shape[1])
    def rows(part):
        value = dot_tn(left[:, part], right[...]).astype(bf16)
        for o in range(outer):
            for c in range(2):
                at = (2 * o + c) * quarter
                store(o, c, panel, part, value[:, at : at + quarter])


def store_all(blocks):
    def store(o, c, panel, part, value):
        blocks[o, c, panel, part, :] = value

    return store


def store_by_core(core, here, there):
    def store(o, c, panel, part, value):
        @pl.when(c == core)
        def kept():
            here[o, panel, part, :] = value

        @pl.when(c != core)
        def sent():
            there[o, panel, part, :] = value

    return store


def store_by_chip(chip, here, there):
    def store(o, c, panel, part, value):
        @pl.when(o == chip)
        def kept():
            here[c, panel, part, :] = value

        @pl.when(o != chip)
        def sent():
            there[c][panel, part, :] = value

    return store


def attend(queries, keys, head, size, length, score_scale):
    cols = slice(head * size, (head + 1) * size)
    scores = dot_nt(queries[:, cols], keys[:, cols]) * score_scale
    spot = lax.broadcasted_iota(jnp.int32, scores.shape, 1)
    scores = jnp.where(spot < length, scores, -1000000000.0)
    peak = jnp.max(scores, axis=-1, keepdims=True)
    raised = jnp.exp(scores - peak)
    return raised * (1.0 / jnp.sum(raised, axis=-1, keepdims=True)), cols


def attention_forward_kernel(count, meta, stream, rows, *refs):
    own, other = refs[:count], refs[count : 2 * count]
    out, normed, queries, keys, values, mixed, weights, sems = refs[2 * count :]
    core, length = meta[count], meta[count + 1]
    width = stream.shape[1]
    size = width // HEADS
    copies = halves_to_panels(0, 4, own, other, meta, core, weights, sems)
    start_all(copies)
    inside, ignored = norm_parts(stream[...])
    normed[...] = (inside * rows[2:3] + rows[3:4]).astype(bf16)
    wait_all(copies)

    @column_loop(width)
    def project(cols):
        low = normed[...]
        queries[:, cols] = (dot(low, weights[0, :, cols]) + rows[22:23, cols]).astype(bf16)
        keys[:, cols] = dot(low, weights[1, :, cols]).astype(bf16)
        values[:, cols] = (dot(low, weights[2, :, cols]) + rows[23:24, cols]).astype(bf16)

    for head in range(HEADS):
        soft, cols = attend(queries, keys, head, size, length, size ** (-0.5))
        mixed[:, cols] = dot(soft.astype(bf16), values[:, cols]).astype(bf16)

    @column_loop(width)
    def branch(cols):
        out[:, cols] = (
            stream[:, cols] + dot(mixed[...], weights[3, :, cols]) + rows[24:25, cols]
        )


def attention_heads_backward_kernel(
    count, meta, grad, queries, keys, values, mixed, had, *refs
):
    own, other = refs[:count], refs[count : 2 * count]
    lows, here, there, sums, weights, branch_grad, low_mixed, sems = refs[2 * count :]
    store = store_by_core(meta[count], here, there)
    sums[...] = had[...]
    core, length = meta[count], meta[count + 1]
    width = grad.shape[1]
    size = width // HEADS
    score_scale = size ** (-0.5)
    copies = halves_to_panels(3, 4, own, other, meta, core, weights, sems)
    start_all(copies)
    branch_grad[...] = grad[...].astype(bf16)
    sums[24:25] = column_sum(branch_grad[...].astype(f32))
    put_blocks(store, 0, mixed, branch_grad, here.shape[0])
    wait_all(copies)

    @column_loop(width)
    def through(cols):
        low_mixed[:, cols] = dot_nt(branch_grad[...], weights[0, cols, :]).astype(bf16)

    for head in range(HEADS):
        soft, cols = attend(queries, keys, head, size, length, score_scale)
        low = low_mixed[:, cols]
        soft_grad = dot_nt(low, values[:, cols])
        lows[2, :, cols] = dot_tn(soft.astype(bf16), low).astype(bf16)
        along = jnp.sum(soft_grad * soft, axis=-1, keepdims=True)
        score_grad = (soft * (soft_grad - along)).astype(bf16)
        lows[0, :, cols] = (dot(score_grad, keys[:, cols]) * score_scale).astype(bf16)
        lows[1, :, cols] = (dot_tn(score_grad, queries[:, cols]) * score_scale).astype(bf16)

    sums[22:23] = column_sum(lows[0].astype(f32))
    sums[23:24] = column_sum(lows[2].astype(f32))


def attention_in_backward_kernel(count, meta, grad, stream, normed, lows, rows, had, *refs):
    own, other = refs[:count], refs[count : 2 * count]
    out, here, there, sums, half_low, weights, normed_grad, sems = refs[2 * count :]
    core = meta[count]
    store = store_by_core(core, here, there)
    sums[...] = had[...]
    width = stream.shape[1]
    copies = halves_to_panels(0, 3, own, other, meta, core, weights, sems)
    start_all(copies)
    for i in range(3):
        put_blocks(store, i, normed, lows.at[i], here.shape[0])
    wait_all(copies)

    @column_loop(width)
    def back(cols):
        total = dot_nt(lows[0], weights[0, cols, :])
        total = total + dot_nt(lows[1], weights[1, cols, :])
        normed_grad[:, cols] = total + dot_nt(lows[2], weights[2, cols, :])

    inside, inverse = norm_parts(stream[...])
    pulled = normed_grad[...]
    sums[2:3] = column_sum(pulled * inside)
    sums[3:4] = column_sum(pulled)
    flow = grad[...] + norm_pull(inside, inverse, rows[2:3], pulled)
    out[...] = flow
    half_low[...] = (0.5 * flow).astype(bf16)
    sums[16:17] = column_sum(half_low[...].astype(f32))


def moved(values, steps):
    if steps == 0:
        return values
    tall = values.shape[0]
    spot = lax.broadcasted_iota(jnp.int32, values.shape, 0) + steps
    return jnp.where((spot >= 0) & (spot < tall), pltpu.roll(values, (-steps) % tall, 0), 0.0)


def gated_depth(wide, rows, length):
    value, gate = wide[0], wide[1]
    open_gate = jax.nn.sigmoid(gate)
    inside = lax.broadcasted_iota(jnp.int32, value.shape, 0) < length
    gated = jnp.where(inside, value * open_gate, 0.0)
    depth = rows[27:28] + rows[28:29] * moved(gated, -(KERNEL // 2))
    for tap in range(1, KERNEL):
        depth = depth + rows[28 + tap : 29 + tap] * moved(gated, tap - KERNEL // 2)
    return value, open_gate, inside, gated, depth


def conv_forward_kernel(count, meta, stream, rows, *refs):
    own, other = refs[:count], refs[count : 2 * count]
    out, normed, wide, active, next_low, weights, sems = refs[2 * count :]
    core, length = meta[count], meta[count + 1]
    width = stream.shape[1]
    copies = halves_to_panels(4, 7, own, other, meta, core, weights, sems)
    start_all(copies)
    inside, ignored = norm_parts(stream[...])
    normed[...] = (inside * rows[4:5] + rows[5:6]).astype(bf16)
    wait_all(copies)

    @column_loop(width)
    def project(cols):
        for i in range(2):
            wide[i, :, cols] = dot(normed[...], weights[i, :, cols]) + rows[25 + i : 26 + i, cols]

    depth = gated_depth(wide, rows, length)[-1]
    inside, ignored = norm_parts(depth)
    shifted = inside * rows[6:7] + rows[7:8]
    active[...] = (shifted * jax.nn.sigmoid(shifted)).astype(bf16)

    @column_loop(width)
    def branch(cols):
        out[:, cols] = (
            stream[:, cols] + dot(active[...], weights[2, :, cols]) + rows[33:34, cols]
        )

    inside, ignored = norm_parts(out[...])
    next_low[...] = (inside * rows[8:9] + rows[9:10]).astype(bf16)


def conv_out_backward_kernel(count, meta, grad, wide, active, rows, had, *refs):
    own, other = refs[:count], refs[count : 2 * count]
    lows, here, there, sums, weights, full, sems = refs[2 * count :]
    core, length = meta[count], meta[count + 1]
    store = store_by_core(core, here, there)
    sums[...] = had[...]
    width = grad.shape[1]
    copies = halves_to_panels(6, 7, own, other, meta, core, weights, sems)
    start_all(copies)
    branch_grad = grad[...].astype(bf16)
    lows[0] = branch_grad
    sums[33:34] = column_sum(branch_grad.astype(f32))
    put_blocks(store, 0, active, lows.at[0], here.shape[0])
    wait_all(copies)

    @column_loop(width)
    def through(cols):
        full[:, cols] = dot_nt(lows[0], weights[0, cols, :])

    value, open_gate, valid, gated, depth = gated_depth(wide, rows, length)
    inside, inverse = norm_parts(depth)
    shifted = inside * rows[6:7] + rows[7:8]
    share = jax.nn.sigmoid(shifted)
    outer_grad = full[...] * share * (1.0 + shifted * (1.0 - share))
    sums[6:7] = column_sum(outer_grad * inside)
    sums[7:8] = column_sum(outer_grad)
    depth_grad = norm_pull(inside, inverse, rows[6:7], outer_grad)
    sums[27:28] = column_sum(depth_grad)
    gated_grad = jnp.zeros_like(depth_grad)
    for tap in range(KERNEL):
        off = tap - KERNEL // 2
        sums[28 + tap : 29 + tap] = column_sum(depth_grad * moved(gated, off))
        gated_grad = gated_grad + rows[28 + tap : 29 + tap] * moved(depth_grad, -off)
    gated_grad = jnp.where(valid, gated_grad, 0.0)
    lows[0] = (gated_grad * open_gate).astype(bf16)
    lows[1] = (gated_grad * value * open_gate * (1.0 - open_gate)).astype(bf16)
    for i in range(2):
        sums[25 + i : 26 + i] = column_sum(lows[i].astype(f32))


def conv_in_backward_kernel(count, meta, grad, stream, normed, lows, rows, had, *refs):
    own, other = refs[:count], refs[count : 2 * count]
    out, here, there, sums, weights, full, sems = refs[2 * count :]
    core = meta[count]
    store = store_by_core(core, here, there)
    sums[...] = had[...]
    width = stream.shape[1]
    copies = halves_to_panels(4, 6, own, other, meta, core, weights, sems)
    start_all(copies)
    for i in range(2):
        put_blocks(store, i, normed, lows.at[i], here.shape[0])
    wait_all(copies)

    @column_loop(width)
    def back(cols):
        full[:, cols] = dot_nt(lows[0], weights[0, cols, :]) + dot_nt(lows[1], weights[1, cols, :])

    inside, inverse = norm_parts(stream[...])
    pulled = full[...]
    sums[4:5] = column_sum(pulled * inside)
    sums[5:6] = column_sum(pulled)
    out[...] = grad[...] + norm_pull(inside, inverse, rows[4:5], pulled)


def pull_kernel(gain, grad, stream, mine, came, rows, had, out, sums):
    sums[...] = had[...]
    inside, inverse = norm_parts(stream[...])
    pulled = mine[...] + came[...].astype(f32)
    sums[gain : gain + 1] = column_sum(pulled * inside)
    sums[gain + 1 : gain + 2] = column_sum(pulled)
    flow = grad[...] + norm_pull(inside, inverse, rows[gain : gain + 1], pulled)
    out[...] = flow.astype(out.dtype)


def pull_call(gain, grad, stream, mine, came, rows, had, dtype):
    return pl.pallas_call(
        functools.partial(pull_kernel, gain),
        out_shape=[
            jax.ShapeDtypeStruct(grad.shape, dtype),
            jax.ShapeDtypeStruct(had.shape, f32),
        ],
        cost_estimate=pl.CostEstimate(
            flops=20 * grad.size, bytes_accessed=16 * grad.size, transcendentals=0
        ),
        compiler_params=pltpu.CompilerParams(vmem_limit_bytes=VMEM_LIMIT),
        name="norm_pull",
    )(grad, stream, mine, came, rows, had)


def turn_kernel(meta, stream, mine, came, cotangent, rows, layer_out, out, half_low, sums):
    last = stream[...] + 0.5 * (mine[...] + came[...].astype(f32) + rows[21:22])
    inside, inverse = norm_parts(last)
    layer_out[...] = (inside * rows[10:11] + rows[11:12]).astype(bf16)
    spot = lax.broadcasted_iota(jnp.int32, last.shape, 0)
    grad = jnp.where(spot < meta[0], cotangent[...].astype(f32), 0.0)
    sums[...] = jnp.zeros_like(sums)
    sums[10:11] = column_sum(grad * inside)
    sums[11:12] = column_sum(grad)
    flow = norm_pull(inside, inverse, rows[10:11], grad)
    out[...] = flow
    half_low[...] = (0.5 * flow).astype(bf16)
    sums[21:22] = column_sum(half_low[...].astype(f32))


def turn_call(length, stream, mine, came, cotangent, rows):
    return pl.pallas_call(
        turn_kernel,
        in_specs=[pl.BlockSpec(memory_space=SMEM)] + [pl.BlockSpec(memory_space=VMEM)] * 5,
        out_shape=[
            jax.ShapeDtypeStruct(stream.shape, bf16),
            jax.ShapeDtypeStruct(stream.shape, f32),
            jax.ShapeDtypeStruct(stream.shape, bf16),
            jax.ShapeDtypeStruct(rows.shape, f32),
        ],
        cost_estimate=pl.CostEstimate(
            flops=30 * stream.size, bytes_accessed=20 * stream.size, transcendentals=0
        ),
        compiler_params=pltpu.CompilerParams(vmem_limit_bytes=VMEM_LIMIT),
        name="turn",
    )(length, stream, mine, came, cotangent, rows)


def panel_call(kernel, name, panels, meta, blocks, own, other, outs, scratch, flops):
    count = len(own)
    width = blocks[0].shape[1]
    return pl.pallas_call(
        functools.partial(kernel, count),
        out_shape=outs,
        in_specs=[pl.BlockSpec(memory_space=SMEM)]
        + [pl.BlockSpec(memory_space=VMEM)] * len(blocks)
        + [pl.BlockSpec(memory_space=ANY)] * (2 * count),
        out_specs=[pl.BlockSpec(memory_space=VMEM)] * len(outs),
        scratch_shapes=[VMEM((panels, width, width), bf16)]
        + scratch
        + [pltpu.SemaphoreType.DMA((2 * count,))],
        compiler_params=pltpu.CompilerParams(vmem_limit_bytes=VMEM_LIMIT),
        cost_estimate=pl.CostEstimate(
            flops=flops,
            bytes_accessed=panels * width * width * 2 + 8 * blocks[0].size * 4,
            transcendentals=2 * blocks[0].size,
        ),
        name=name,
    )(meta, *blocks, *own, *other)


def both_cores(values):
    return jnp.concatenate([values, swap_cores(values)], axis=0)


def on_device(
    outer,
    owners_count,
    frames,
    lengths,
    cotangent,
    panels,
    vectors,
    vector_first,
    vector_second,
    owners,
    basis_left,
    basis_right,
    panel_first,
    panel_second,
    panel_master,
):
    seq_count, seq_len, width = frames.shape
    tokens = seq_count * seq_len
    depth = panels.shape[1]
    half = width // 2
    quarter = width // (2 * outer)
    core = lax.axis_index("c")
    parity = lax.axis_index("o") % 2
    wires = Wires(outer, owners_count)
    shape = jax.ShapeDtypeStruct

    def chip_share(first, side):
        panel = first + 2 * core + side
        ins = lax.dynamic_slice_in_dim(panels, panel, 1, 0)
        outs = lax.dynamic_slice_in_dim(panels, panel + 4, 1, 0)
        return jnp.concatenate([ins, outs], axis=0)

    first = Gather(wires, chip_share(0, parity), 0)
    middle = Gather(wires, lax.dynamic_slice(panels, (8, 0, core * half), (7, depth, half)), 1)
    second = Gather(wires, chip_share(15, parity), 0)
    second_other = [Cell(chip_share(15, 1 - parity))]
    middle_other = []

    class Passing:
        def __init__(self, gather, route, store, start):
            self.gather, self.route, self.store, self.next = gather, route, store, start

        def more(self, most=1):
            sends = []
            while most and self.next < len(self.gather.pieces):
                sends.append((self.gather.pieces[self.next].value, self.route, self.store.append))
                self.next += 1
                most -= 1
            return sends

    to_chip = Passing(second, "chip", second_other, 1)
    to_core = Passing(middle, "core", middle_other, 0)
    slot = wires.slot

    def values(cells):
        return [cell.value for cell in cells]

    def core_rows(first):
        rows = lax.dynamic_slice_in_dim(vectors, first + 2 * core, 2, 0)
        rows = jnp.where(parity == 0, rows, rows[::-1])
        return rows[:, None, :]

    def meta_of(gather, *more):
        return jnp.concatenate([gather.spots(), jnp.stack(more).astype(jnp.int32)])

    low_stream = shape((tokens, width), bf16)
    stream = shape((tokens, width), f32)

    left = Cell(basis_left.astype(bf16))
    right = Cell(basis_right.astype(bf16))
    def exchange(values):
        return lax.ppermute(values, "o", wires.routes["chip"][1])

    def all_four(own, came):
        mine = jnp.concatenate([own, came])
        return jnp.concatenate([mine, swap_cores(mine)])

    def sum_four(mine, away):
        total = mine + swap_cores(away).astype(f32)
        return total[:tokens], total[tokens:].astype(bf16)

    start = Cell(frames.reshape(tokens, width).astype(f32))
    own_first = layer_norm(start.value, vectors[0], vectors[1]).astype(bf16)
    bias_first, bias_second = Cell(core_rows(12)[:1]), Cell(core_rows(17))
    ready = [start, bias_first, bias_second, *second_other]
    far_first = []
    came = slot(first.hop(), [(own_first, "chip", far_first.append)])
    bind(*ready, *came)
    slot(middle.hop(), to_core.more())
    normed = Cell(all_four(own_first, far_first[0].value))
    slot(first.hop())
    bind(normed, left, right, *wires.past[-2])
    slot(second.hop(), to_core.more(2))
    slot(first.hop(), to_chip.more())
    slot(middle.hop(), to_chip.more())
    came = slot(first.hop())
    while any(first.left):
        came = slot(first.hop())
    slot(second.hop(), to_core.more(2))
    bind(normed, *came)
    slot(middle.hop(), to_chip.more())
    hidden, active, mine, away = ffn_forward_call(
        normed.value, bias_first.value, [values(first.pieces)], meta_of(first, parity)
    )
    own, far = sum_four(mine, away)
    own, far = Cell(own), Cell(far)
    kept_first = (normed.value, hidden, active)
    bind(own, far, *wires.past[-1], *wires.past[-2])
    far_came = []
    slot(second.hop(), to_chip.more(), [(far.value, "chip", far_came.append)])
    slot(middle.hop(), to_chip.more(), to_core.more(2))
    slot(second.hop(), to_chip.more())
    while any(middle.left) or any(second.left):
        slot(middle.hop(), second.hop(), to_chip.more(2), to_core.more(2))
    after_first = Cell(
        start.value + 0.5 * (own.value + far_came[0].value.astype(f32) + vectors[16])
    )
    came = wires.start(to_core.more(2), to_chip.more(), after=wires.past[-1])
    while to_core.next < len(middle.pieces):
        came += slot(to_core.more(2))
    middle_meta = meta_of(middle, core, lengths[0])

    def sides_of(gather, other):
        return [values(gather.pieces)] + ([values(other)] if other else [])

    bind(after_first, *wires.past[-1])
    after_attn, attn_normed, queries, keys, values_, mixed = panel_call(
        attention_forward_kernel,
        "attention_forward",
        4,
        middle_meta,
        [after_first.value, vectors],
        values(middle.pieces),
        values(middle_other),
        [stream] + [low_stream] * 5,
        [],
        8 * tokens * width * width,
    )
    after_attn = Cell(after_attn)
    bind(after_attn, *came, *[cell for past in wires.past[-4:-1] for cell in past])
    came = []
    while to_chip.next < len(second.pieces):
        came += wires.start(to_chip.more(2), after=[after_attn])
    after_conv, conv_normed, wide, conv_active, second_low = panel_call(
        conv_forward_kernel,
        "conv_forward",
        3,
        middle_meta,
        [after_attn.value, vectors],
        values(middle.pieces),
        values(middle_other),
        [stream, low_stream, shape((2, tokens, width), f32), low_stream, low_stream],
        [],
        6 * tokens * width * width,
    )
    normed = both_cores(second_low)
    hidden, active, mine, away = ffn_forward_call(
        normed, bias_second.value, sides_of(second, second_other), meta_of(second, parity)
    )
    kept_second = (normed, hidden, active)
    layer_out, grad_flow, half_low, sums = turn_call(
        lengths, after_conv, mine, swap_cores(away), cotangent.reshape(tokens, width), vectors
    )

    def ring_of(turn, matrices):
        return Reduce(wires, matrices, depth, turn)

    class Share:
        def __init__(self, here, there):
            self.here, self.there = here, there

        def hop(self):
            return [(self.there, "core", self.take)]

        def take(self, cell):
            self.came = cell

        def total(self):
            return (self.here.astype(f32) + self.came.value.astype(f32)).astype(bf16)

    def trade_cores(block):
        there = lax.dynamic_index_in_dim(block, 1 - core, 0, keepdims=False)
        here = lax.dynamic_index_in_dim(block, core, 0, keepdims=False)
        came = swap_cores(there.astype(bf16)).astype(f32)
        return jnp.where(
            core == 0, jnp.concatenate([here, came]), jnp.concatenate([came, here])
        )

    chip = lax.axis_index("o")
    pairs = outer == 2

    def ffn_backward_out(both_low, gather, other, kept, bias, sums, ways):
        normed, hidden, active = kept
        return ffn_backward_call(
            ffn_out_backward_kernel,
            "ffn_out_backward",
            bias,
            outer,
            ways,
            meta_of(gather, parity, core, chip),
            [hidden, active, both_low, sums],
            sides_of(gather, other),
            [shape(active.shape, bf16), shape(vectors.shape, f32)],
        )

    def ffn_backward_in(low, gather, other, kept, ways):
        return ffn_backward_call(
            ffn_in_backward_kernel,
            "ffn_in_backward",
            0,
            outer,
            ways,
            meta_of(gather, parity, core, chip),
            [kept[0], low],
            sides_of(gather, other),
            [
                shape((kept[0].shape[0] // 2, width), f32),
                shape((kept[0].shape[0] // 2, width), bf16),
            ],
        )

    def middle_call(kernel, name, used, arrays, outs, scratch, flops):
        block_shape = shape((outer, used, width, quarter), bf16)
        return panel_call(
            kernel,
            name,
            used,
            middle_meta,
            arrays,
            values(middle.pieces),
            values(middle_other),
            [outs[0], block_shape, block_shape, shape(vectors.shape, f32), *outs[1:]],
            scratch,
            flops * tokens * width * width,
        )

    class Part:
        def __init__(self, matrices, turn):
            self.turn = turn
            self.ring = None
            if len(matrices) == 3:
                self.chips = ChipSum(wires, here=matrices[0], there=matrices[1:])
            else:
                self.chips = None
                self.ring = ring_of(turn, matrices[0])

        def send(self):
            return self.chips.send() if self.chips is not None and not hasattr(self, "late") else []

        def ready(self):
            if self.ring is None:
                self.ring = ring_of(self.turn, self.chips.total().astype(bf16))

        def hop(self):
            self.ready()
            return self.ring.hop()

        def finish(self):
            if self.chips is not None:
                return []
            self.chips = ChipSum(wires, blocks=self.ring.total())
            self.late = True
            return self.chips.send()

        def total(self):
            if self.chips is None:
                slot(self.finish())
            return self.chips.total() if hasattr(self, "late") else self.ring.total()

    begin = wires.start
    low, sums, *matrices = ffn_backward_out(
        both_cores(half_low), second, second_other, kept_second, 17, sums, False
    )
    second_out = Part(matrices, 0)
    low = Cell(low)
    came = begin(second_out.hop(), beside=[low])
    mine, away, *matrices = ffn_backward_in(low.value, second, second_other, kept_second, pairs)
    mine, away = Cell(mine), Cell(away)
    bind(mine, away, *came)
    second_in = Part(matrices, 1)
    came = begin(second_out.hop(), second_in.send(), beside=[mine, away])
    grad_flow, sums = pull_call(
        8, grad_flow, after_conv, mine.value, swap_cores(away.value), vectors, sums, f32
    )
    lows, here, there, sums = middle_call(
        conv_out_backward_kernel,
        "conv_out_backward",
        1,
        [grad_flow, wide, conv_active, vectors, sums],
        [shape((2, tokens, width), bf16)],
        [VMEM((tokens, width), f32)],
        4,
    )
    lows = Cell(lows)
    conv_out = Share(here, there)
    bind(lows, *came)
    came = begin(second_out.hop(), second_in.send(), conv_out.hop(), beside=[lows])
    flow, here, there, sums = middle_call(
        conv_in_backward_kernel,
        "conv_in_backward",
        2,
        [grad_flow, after_attn.value, conv_normed, lows.value, vectors, sums],
        [stream],
        [VMEM((tokens, width), f32)],
        8,
    )
    flow = Cell(flow)
    conv_in = Share(here, there)
    lows, here, there, sums = middle_call(
        attention_heads_backward_kernel,
        "attention_heads_backward",
        1,
        [flow.value, queries, keys, values_, mixed, sums],
        [shape((3, tokens, width), bf16)],
        [VMEM((tokens, width), bf16), VMEM((tokens, width), bf16)],
        6,
    )
    lows = Cell(lows)
    attn_out = Share(here, there)
    bind(lows, *came)
    second_in.ready()
    came = begin(
        hop_together(second_out.ring, second_in.ring),
        conv_in.hop(),
        attn_out.hop(),
        beside=[lows],
    )
    flow.value, here, there, sums, half_low = middle_call(
        attention_in_backward_kernel,
        "attention_in_backward",
        3,
        [flow.value, after_first.value, attn_normed, lows.value, vectors, sums],
        [stream, low_stream],
        [VMEM((tokens, width), f32)],
        12,
    )
    attn_in = Share(here, there)
    half_low = Cell(half_low)
    bind(half_low, *came)
    conv_total = jnp.concatenate([conv_in.total(), conv_out.total()], axis=1)
    if pairs:
        conv_chips = ChipSum(wires, blocks=conv_total, cuts=[(0, 1), (1, 3)])
    else:
        conv_part = ring_of(0, conv_total)
    far_low = []
    came = begin(
        second_in.hop(),
        attn_in.hop(),
        [(half_low.value, "chip", far_low.append)],
        beside=[half_low],
    )
    both_low = Cell(all_four(half_low.value, far_low[0].value))
    attn_total = Cell(jnp.concatenate([attn_in.total(), attn_out.total()], axis=1))
    bind(both_low, attn_total)
    if pairs:
        came += begin(conv_chips.send(), beside=[both_low])
    low, sums, *matrices = ffn_backward_out(
        both_low.value, first, [], kept_first, 12, sums, False
    )
    first_out = ring_of(0, matrices[0])
    low = Cell(low)
    bind(low, *came)
    attn_part = ring_of(1, attn_total.value)
    conv_sends = conv_chips.send() if pairs else []
    came = begin(hop_together(second_in.ring, attn_part, first_out), conv_sends, beside=[low])
    mine, away, *matrices = ffn_backward_in(low.value, first, [], kept_first, False)
    first_in = ring_of(0, matrices[0])
    mine, away = Cell(mine), Cell(away)
    bind(mine, away, *came)
    if pairs:
        conv_part = ring_of(1, conv_chips.total().astype(bf16))
    came = begin(
        hop_together(second_in.ring, attn_part, first_out, first_in, conv_part),
        beside=[mine, away],
    )
    own, far = sum_four(mine.value, away.value)
    own, far_came = Cell(own), []
    came += begin([(far, "chip", far_came.append)], beside=[own])
    bind(*came)
    came = begin(hop_together(attn_part, first_out, first_in, conv_part), second_out.finish())
    frames_grad, sums = pull_call(
        0, flow.value, start.value, own.value, far_came[0].value, vectors, sums, bf16
    )
    frames_grad, sums = Cell(frames_grad), Cell(sums)
    vector_sum = AllSum(wires, sums.value)
    bind(vector_sum.value, frames_grad, *came)
    came = begin(hop_together(attn_part, first_out, first_in, conv_part))
    bind(*came)
    attn_chips = ChipSum(wires, blocks=attn_part.total())
    came = begin(hop_together(first_out, first_in, conv_part), attn_chips.send())
    bind(*came)
    conv_total = conv_part.total()
    if not pairs:
        conv_total = ChipSum(wires, blocks=conv_total).total()

    def spread(mine):
        if not pairs:
            big = jnp.zeros((outer, 2, 2, 2) + mine.shape[2:], f32)
            at = (lax.broadcasted_iota(jnp.int32, (1, 1, 2, 2, 1, 1, 1), 2) == core) & (
                lax.broadcasted_iota(jnp.int32, (1, 1, 2, 2, 1, 1, 1), 3) == parity
            )
            big = jnp.where(at, mine[:, :, None, None], big).astype(bf16)
            big = big.reshape((outer * 2,) + big.shape[2:])
            return lax.psum_scatter(big, ("o", "c"), scatter_dimension=0, tiled=True)[0].astype(f32)
        low = trade_blocks(mine.astype(bf16), "o", outer)
        low = trade_blocks(low.transpose(1, 0, 2, 3, 4), "c", 2)
        return low.astype(f32)

    first_sum = spread(jnp.concatenate([first_in.total(), first_out.total()], axis=2))
    first_sum = [first_sum[:, :, kind].reshape(4, depth, quarter) for kind in range(2)]
    early = [trade_cores(second_in.total()), trade_cores(second_out.total()), conv_total]
    early = [Cell(part) for part in early]
    late = [Cell(first_sum[0]), Cell(attn_chips.total()), Cell(first_sum[1])]
    bind(*early, *late)
    panel_grads = jnp.concatenate(
        [
            late[0].value,
            late[2].value,
            late[1].value,
            early[2].value,
            early[0].value,
            early[1].value,
        ],
        axis=0,
    )
    panel_grads = Cell(panel_grads)
    bind(panel_grads, vector_sum.value, frames_grad)
    panel_grads = panel_grads.value

    slot_count = panel_first.shape[1]
    panel_count = owners.shape[0]
    panel_index = jnp.arange(panel_count, dtype=jnp.int32)
    same_owner = owners[:, None] == owners[None, :]
    earlier = panel_index[None, :] < panel_index[:, None]
    slot_of = jnp.sum((same_owner & earlier).astype(jnp.int32), axis=1)
    target = owners * slot_count + slot_of
    slot_hit = target[:, None] == jnp.arange(owners_count * slot_count, dtype=jnp.int32)[None, :]
    source = jnp.sum(slot_hit.astype(jnp.int32) * panel_index[:, None], axis=0)
    filled = jnp.any(slot_hit, axis=0)
    mine = lax.dynamic_slice_in_dim(filled, lax.axis_index("f") * slot_count, slot_count)

    outgoing = pick(panel_grads.astype(bf16), source)
    outgoing = outgoing.reshape(owners_count, slot_count, depth, quarter)
    incoming = lax.all_to_all(outgoing, "f", split_axis=0, concat_axis=0, tiled=True)
    block = lax.axis_index("o") * 2 + core
    left_rows = lax.dynamic_slice_in_dim(left.value, block * quarter, quarter, 1)
    incoming = Cell(incoming)
    last = None
    while vector_sum.todo:
        last = begin(vector_sum.hop())
        if len(vector_sum.todo) == 2:
            bind(incoming, *last)
    vector_grads = vector_sum.total()
    vector_first_new = beta_one * vector_first + (1.0 - beta_one) * vector_grads
    vector_second_new = beta_two * vector_second + (1.0 - beta_two) * vector_grads * vector_grads
    vectors_new = vectors - vector_rate * adam_step(vector_first_new, vector_second_new)
    updated = [Cell(vector_first_new), Cell(vector_second_new), Cell(vectors_new)]

    traded = []
    for s in range(slot_count):
        turned = dot_tn(left.value[s], incoming.value[:, s].reshape(width, quarter)).astype(bf16)
        turned = turned.reshape(outer, 2 * quarter, quarter)
        traded.append(Cell(trade_blocks(turned, "o", outer)))
    backs, firsts, seconds = [], [], []
    for s in range(slot_count):
        if s:
            bind(traded[s], backs[-1])
        turned = traded[s].value.reshape(outer, 2, quarter, quarter).transpose(1, 0, 2, 3)
        turned = trade_blocks(turned, "c", 2)
        turned = turned.transpose(2, 1, 0, 3).reshape(quarter, width)
        rotated = dot(turned, right.value[s])
        first_new = beta_one * panel_first[:, s] + (1.0 - beta_one) * rotated
        second_new = beta_two * panel_second[:, s] + (1.0 - beta_two) * rotated * rotated
        step_values = adam_step(first_new, second_new).astype(bf16)
        back_turn = Cell(dot_nt(step_values, right.value[s]).astype(bf16))
        firsts.append(jnp.where(mine[s], first_new, 0.0))
        seconds.append(jnp.where(mine[s], second_new, 0.0))
        backs.append(back_turn)
    masters = []
    for s in range(slot_count):
        back_turn = gather_blocks(backs[s].value, "o", outer)
        back_turn = gather_blocks(back_turn, "c", 2)
        back_turn = back_turn.transpose(1, 0, 2, 3).reshape(width, width)
        update = dot(left_rows[s], back_turn)
        masters.append(jnp.where(mine[s], panel_master[:, s] - learn_rate * update, 0.0))
    results = list(zip(firsts, seconds, masters))
    first_new, second_new, master_new = [jnp.stack(part, axis=1) for part in zip(*results)]
    return (
        layer_out.reshape(frames.shape),
        frames_grad.value.reshape(frames.shape),
        panel_grads,
        vector_grads,
        *values(updated),
        first_new,
        second_new,
        master_new,
    )


def solution(mesh):
    outer = mesh.shape["dp"] // 2
    owners_count = mesh.shape["fsdp"]
    split = Mesh(mesh.devices.reshape(outer, 2, owners_count), ("o", "c", "f"))
    every = P(("o", "c", "f"), None, None)
    state = P(("o", "c"), "f", None)
    return jax.shard_map(
        functools.partial(on_device, outer, owners_count),
        mesh=split,
        in_specs=(
            every,
            P(("o", "c", "f")),
            every,
            P(None, "f", None),
            P(),
            P(),
            P(),
            P(),
            P("f", None, None),
            P("f", None, None),
            state,
            state,
            state,
        ),
        out_specs=(
            every,
            every,
            P(None, "f", ("o", "c")),
            P(),
            P(),
            P(),
            P(),
            state,
            state,
            state,
        ),
        check_vma=False,
    )
```
